128 devices in a mesh: dp: 4 (over x_hi, core), section: 4 (over z), tensor: 8 (over x_lo, y).
Axes of the slice: x: 4 (x_hi: 2, x_lo: 2; x = x_hi * 2 + x_lo), y: 4, z: 4, core: 2. Of those that a mesh axis runs over, the one named last changes fastest.
Arguments:
- embeds: bfloat16 [8, 128, 4096], P('dp', None, 'tensor'), may hold values from -6 to 6
- source: int32 [8], replicated, may hold values from 0 to 7, each once
- lengths: int32 [8], replicated, may hold values from 32 to 128, as said below
- bounds: int32 [8, 4], replicated, may hold values from 0 to 127, as said below
- targets: int32 [8, 4], replicated, may hold values from 0 to 127
- w_query: bfloat16 [4, 4096, 4096], P('section', None, 'tensor'), may hold values from -0.09375 to 0.09375
- w_key: bfloat16 [4, 4096, 1024], P('section', None, 'tensor'), may hold values from -0.09375 to 0.09375
- w_value: bfloat16 [4, 4096, 1024], P('section', None, 'tensor'), may hold values from -0.09375 to 0.09375
- w_out: bfloat16 [4, 4096, 4096], P('section', 'tensor'), may hold values from -0.09375 to 0.09375
- w_class: bfloat16 [4096, 128], P('tensor'), may hold values from -0.09375 to 0.09375
Outputs:
- grad_query: float32 [4, 4096, 4096], P('section', 'dp', 'tensor')
- grad_key: float32 [4, 4096, 1024], P('section', 'dp', 'tensor')
- grad_value: float32 [4, 4096, 1024], P('section', 'dp', 'tensor')
- grad_out: float32 [4, 4096, 4096], P('section', 'tensor', 'dp')
The draws below stay inside these ranges and needn't reach their ends.
Inputs may be any that keep to these rules, and one draw needn't show every extreme that they name: `lengths`: a trace's length is at least 32; some trace has exactly 128 tokens. `bounds`: within a trace the step ends rise strictly and the last is its length minus one. `source`: each trace fills exactly one slot.
All inputs are finite; a program needn't handle non-finite values.
Results may differ from the reference program's by a relative error of at most 0.04.
Values may be sent and summed in bfloat16 or wider, within the bound.
No kernel may reach another device: no remote copies, remote signals or barrier semaphores. Data moves between devices by JAX's collectives and lax.ppermute only.
A program may use at most 320 MiB of HBM per device.

```python
import jax
import jax.numpy as jnp
from jax import lax

D = 4096
HEADS = 32
KV_HEADS = 8
HEAD_DIM = 128
CLASSES = 128
SEQ = 128
STEPS = 4
TRACES_REP = 2
TRACES = 8
LAYERS = 4
N_DP = 4
N_TENSOR = 8


def trace_lengths(key):
    base = jax.random.fold_in(key, 11)
    lens = jax.random.randint(base, (TRACES,), SEQ // 4, SEQ + 1)
    where_full = jax.random.randint(jax.random.fold_in(base, 1), (), 0, TRACES)
    return jnp.where(jnp.arange(TRACES) == where_full, SEQ, lens).astype(jnp.int32)


def draw_lengths(key, part):
    anchor = key
    return trace_lengths(anchor)


def draw_bounds(key, part):
    anchor = key
    key = jax.random.fold_in(key, 5)
    lens = trace_lengths(anchor)
    raw = jax.random.randint(key, (TRACES, STEPS), 0, 1 << 20)
    jitter = raw % (lens // (2 * STEPS) + 1)[:, None]
    order = jnp.arange(STEPS, dtype=jnp.int32)[None, :]
    ends = (order + 1) * lens[:, None] // STEPS - 1 - jitter
    ends = jnp.where(order == STEPS - 1, lens[:, None] - 1, ends)
    return ends.astype(jnp.int32)


def set_ends(entries, own_key, least, largest):
    longest = entries.shape.index(max(entries.shape))
    spots = []
    for shift in (0, 1):
        where = [jax.random.randint(jax.random.fold_in(own_key, axis), (), 0, length) for axis, length in enumerate(entries.shape)]
        where[longest] = (where[longest] + shift) % entries.shape[longest]
        spots.append(tuple(where))
    return entries.at[spots[0]].set(least).at[spots[1]].set(largest)


def levels(stream_key, dims, cuts, low, high):
    level, own = 1.0, jax.random.fold_in(stream_key, 6)
    for position, shards_of in cuts:
        heights = jnp.exp(jax.random.uniform(jax.random.fold_in(own, position), (shards_of,), jnp.float32, low / len(cuts), high / len(cuts)))
        level = level * jnp.repeat(heights, dims[position] // shards_of).reshape([-1 if axis == position else 1 for axis in range(len(dims))])
    return level


def scatter_about(own_key, extent, deviation, bound, shards=(), kind=jnp.bfloat16):
    array = deviation * jax.random.normal(own_key, extent, jnp.float32)
    if shards:
        array = array * levels(own_key, extent, shards, -0.22, 0.18)
    return jnp.clip(array, -bound, bound).astype(kind)


def setup_inputs(seed: int = 0) -> dict:
    streams_of = jax.random.split(jax.random.key(seed), 11)
    return {
        "embeds": scatter_about(streams_of[0], (TRACES, SEQ, D), 1.0, 6.0, ((0, 4), (2, 8))),
        "source": jax.random.permutation(streams_of[1], TRACES).astype(jnp.int32),
        "lengths": draw_lengths(jax.random.fold_in(streams_of[10], 71), 0),
        "bounds": draw_bounds(jax.random.fold_in(streams_of[10], 71), 0),
        "targets": set_ends(jax.random.randint(streams_of[4], (TRACES, STEPS), 0, CLASSES), jax.random.fold_in(streams_of[4], 1), 0, CLASSES - 1).astype(jnp.int32),
        "w_query": scatter_about(streams_of[5], (LAYERS, D, HEADS * HEAD_DIM), D ** -0.5, 0.09375, ((0, 4), (2, 8))),
        "w_key": scatter_about(streams_of[6], (LAYERS, D, KV_HEADS * HEAD_DIM), D ** -0.5, 0.09375, ((0, 4), (2, 8))),
        "w_value": scatter_about(streams_of[7], (LAYERS, D, KV_HEADS * HEAD_DIM), D ** -0.5, 0.09375, ((0, 4), (2, 8))),
        "w_out": scatter_about(streams_of[8], (LAYERS, HEADS * HEAD_DIM, D), (HEADS * HEAD_DIM) ** -0.5, 0.09375, ((0, 4), (1, 8))),
        "w_class": scatter_about(streams_of[9], (D, CLASSES), D ** -0.5, 0.09375, ((0, 8),)),
    }


EPS = 1e-06
LOSS_SCALE = 16384.0

def visible(lens, width):
    posq = jnp.arange(width, dtype=jnp.int32)[:, None]
    posk = jnp.arange(width, dtype=jnp.int32)[None, :]
    allowed = (posk <= posq)[None] & (posk[None] < lens[:, None, None])
    return allowed.astype(jnp.float32)

def local_layer(full, wq, wk, wv, wo, keep):
    xf = full.astype(jnp.float32)
    scale = lax.rsqrt(lax.optimization_barrier(jnp.mean(xf * xf, axis=-1, keepdims=True)) + EPS)
    normed = (xf * scale).astype(jnp.bfloat16)
    query = jnp.dot(normed, wq, preferred_element_type=jnp.float32).astype(jnp.bfloat16)
    key_rows = jnp.dot(normed, wk, preferred_element_type=jnp.float32).astype(jnp.bfloat16)
    value_rows = jnp.dot(normed, wv, preferred_element_type=jnp.float32).astype(jnp.bfloat16)
    ntr = keep.shape[0]
    width = keep.shape[1]
    kvh = wk.shape[1] // HEAD_DIM
    qh = wq.shape[1] // HEAD_DIM
    q5 = query.reshape(ntr, width, kvh, qh // kvh, HEAD_DIM).astype(jnp.float32)
    k4 = key_rows.reshape(ntr, width, kvh, HEAD_DIM).astype(jnp.float32)
    v4 = value_rows.reshape(ntr, width, kvh, HEAD_DIM).astype(jnp.float32)
    scores = jnp.einsum('tqgrd,tkgd->tgrqk', q5, k4) / jnp.sqrt(jnp.float32(HEAD_DIM))
    expo = jnp.exp(scores) * keep[:, None, None]
    weights = (expo / lax.optimization_barrier(jnp.sum(expo, axis=-1, keepdims=True))).astype(jnp.bfloat16)
    attended = jnp.einsum('tgrqk,tkgd->tqgrd', weights.astype(jnp.float32), v4)
    attended = attended.astype(jnp.bfloat16).reshape(ntr * width, qh * HEAD_DIM)
    return jnp.dot(attended, wo, preferred_element_type=jnp.float32)

def head_grad(rows, w_class, tgt, tokens_total):
    zeta = jnp.dot(rows, w_class, preferred_element_type=jnp.float32)
    rf = rows.astype(jnp.float32)
    sumsq = lax.optimization_barrier(jnp.sum(rf * rf, axis=1))
    rstd = lax.rsqrt(sumsq / rows.shape[1] + EPS)
    logits = zeta * rstd[:, None]
    expo = jnp.exp(logits)
    prob = expo / lax.optimization_barrier(jnp.sum(expo, axis=1, keepdims=True))
    onehot = (tgt[:, None] == jnp.arange(logits.shape[1], dtype=jnp.int32)[None, :]).astype(jnp.float32)
    dlog = LOSS_SCALE / tokens_total * (prob - onehot)
    dzeta = dlog * rstd[:, None]
    drstd = lax.optimization_barrier(jnp.sum(dlog * zeta, axis=1))
    dmean = drstd * -0.5 * rstd * rstd * rstd
    return (dzeta, dmean)

def reference(embeds, source, lengths, bounds, targets, w_query, w_key, w_value, w_out, w_class):
    ntp = N_TENSOR
    qcol = HEADS // ntp * HEAD_DIM
    kcol = KV_HEADS // ntp * HEAD_DIM
    rows_rep = TRACES_REP * SEQ
    acc_q = jnp.zeros(w_query.shape, jnp.float32)
    acc_k = jnp.zeros(w_key.shape, jnp.float32)
    acc_v = jnp.zeros(w_value.shape, jnp.float32)
    acc_o = jnp.zeros(w_out.shape, jnp.float32)
    for rep in range(N_DP):
        picks = source[rep * TRACES_REP:(rep + 1) * TRACES_REP]
        state = embeds[picks].reshape(rows_rep, D)
        lens = lengths[picks]
        bnd = bounds[picks]
        tgt = targets[picks].reshape(-1)
        keep = visible(lens, SEQ)
        pieces = []
        inputs = []
        for layer in range(LAYERS):
            ws = (w_query[layer].reshape(D, ntp, qcol).transpose(1, 0, 2), w_key[layer].reshape(D, ntp, kcol).transpose(1, 0, 2), w_value[layer].reshape(D, ntp, kcol).transpose(1, 0, 2), w_out[layer].reshape(ntp, qcol, D))
            pieces.append(ws)
            inputs.append(state)
            parts = lax.map(lambda w: local_layer(state, w[0], w[1], w[2], w[3], keep), ws)
            rounded = lax.optimization_barrier(parts.astype(jnp.bfloat16))
            state = (state.astype(jnp.float32) + lax.optimization_barrier(jnp.sum(rounded.astype(jnp.float32), axis=0))).astype(jnp.bfloat16)
        index = (jnp.arange(TRACES_REP, dtype=jnp.int32)[:, None] * SEQ + bnd).reshape(-1)
        rows = state[index]
        tokens_total = jnp.sum(lens).astype(jnp.float32)
        dzeta, dmean = head_grad(rows, w_class, tgt, tokens_total)
        drows = jnp.dot(dzeta, w_class.astype(jnp.float32).T, precision=lax.Precision.HIGHEST)
        drows = drows + dmean[:, None] * 2.0 * rows.astype(jnp.float32) / D
        grad = jnp.zeros((rows_rep, D), jnp.float32).at[index].set(drows).astype(jnp.bfloat16)
        for layer in reversed(range(LAYERS)):
            saved = inputs[layer]
            cot = grad.astype(jnp.float32)

            def pull_one(w):
                _, pull = jax.vjp(lambda xx, a, b, c, d: local_layer(xx, a, b, c, d, keep), saved, w[0], w[1], w[2], w[3])
                return pull(cot)
            dx, dq, dk, dv, do = lax.map(pull_one, pieces[layer])
            grad = (grad.astype(jnp.float32) + lax.optimization_barrier(jnp.sum(dx.astype(jnp.float32), axis=0))).astype(jnp.bfloat16)
            acc_q = acc_q.at[layer].add(dq.astype(jnp.float32).transpose(1, 0, 2).reshape(D, ntp * qcol))
            acc_k = acc_k.at[layer].add(dk.astype(jnp.float32).transpose(1, 0, 2).reshape(D, ntp * kcol))
            acc_v = acc_v.at[layer].add(dv.astype(jnp.float32).transpose(1, 0, 2).reshape(D, ntp * kcol))
            acc_o = acc_o.at[layer].add(do.astype(jnp.float32).reshape(ntp * qcol, D))
    return (acc_q, acc_k, acc_v, acc_o)
```

```python
import jax
import jax.numpy as jnp
from jax import lax
from jax.sharding import PartitionSpec as P

HEAD_DIM = 128
EPS = 1e-06
LOSS_SCALE = 16384.0
F32 = jnp.float32
BF16 = jnp.bfloat16


def dot(a, b):
    return jnp.dot(a, b, preferred_element_type=F32)


def dot_nt(a, b):
    return lax.dot_general(a, b, (((1,), (1,)), ((), ())), preferred_element_type=F32)


def dot_tn(a, b):
    return lax.dot_general(a, b, (((0,), (0,)), ((), ())), preferred_element_type=F32)


def passed_along(x, axis, by):
    peers = lax.axis_size(axis)
    pairs = [(i, i + by) for i in range(peers) if 0 <= i + by < peers]
    return lax.ppermute(x, axis, pairs)


def swapped(x, axis, mask):
    return lax.ppermute(x, axis, [(i, i ^ mask) for i in range(lax.axis_size(axis))])


def exchange(blocks):
    return lax.all_to_all(blocks, "tensor", split_axis=0, concat_axis=0, tiled=True)


def gathered(cur):
    peers = lax.axis_size("tensor")
    got = exchange(jnp.broadcast_to(cur[None], (peers,) + cur.shape))
    return joined(got)


def joined(blocks):
    return blocks.transpose(1, 0, 2).reshape(blocks.shape[1], -1)


def cut(whole):
    peers = lax.axis_size("tensor")
    return whole.reshape(whole.shape[0], peers, -1).transpose(1, 0, 2)


def heads_down(x):
    rows = x.shape[0]
    return x.reshape(rows, -1, HEAD_DIM).transpose(1, 0, 2).reshape(-1, HEAD_DIM)


def heads_across(x, rows):
    return x.reshape(-1, rows, HEAD_DIM).transpose(1, 0, 2).reshape(rows, -1)


def visible(length, width):
    posq = jnp.arange(width, dtype=jnp.int32)[:, None]
    posk = jnp.arange(width, dtype=jnp.int32)[None, :]
    return ((posk <= posq) & (posk < length)).astype(F32)


def forward(full, wq, wk, wv, keep):
    xf = full.astype(F32)
    scale = lax.rsqrt(jnp.mean(xf * xf, axis=-1, keepdims=True) + EPS)
    h = (xf * scale).astype(BF16)
    rows = full.shape[0]
    q = heads_down(dot(h, wq).astype(BF16))
    k = dot(h, wk).astype(BF16)
    v = dot(h, wv).astype(BF16)
    scores = dot_nt(q, k) / jnp.sqrt(F32(HEAD_DIM))
    expo = (jnp.exp(scores).reshape(-1, rows, rows) * keep[None]).reshape(scores.shape)
    weights = (expo / jnp.sum(expo, axis=-1, keepdims=True)).astype(BF16)
    o = heads_across(dot(weights, v).astype(BF16), rows)
    return dict(x=full, scale=scale, h=h, q=q, k=k, v=v, w=weights, o=o)


def backward_heads(g, kept, wo):
    rows = g.shape[0]
    do = heads_down(dot_nt(g, wo).astype(BF16))
    wf = kept["w"].astype(F32)
    dw = dot_nt(do, kept["v"])
    ds = wf * (dw - jnp.sum(dw * wf, axis=-1, keepdims=True)) / jnp.sqrt(F32(HEAD_DIM))
    ds = ds.astype(BF16)
    dq = heads_across(dot(ds, kept["k"]).astype(BF16), rows)
    dk = dot_tn(ds, kept["q"]).astype(BF16)
    dv = dot_tn(kept["w"], do).astype(BF16)
    return dq, dk, dv


def backward_input(dq, dk, dv, kept, wq, wk, wv):
    dh = dot_nt(dq, wq) + dot_nt(dk, wk) + dot_nt(dv, wv)
    hf = kept["x"].astype(F32) * kept["scale"]
    return (kept["scale"] * (dh - hf * jnp.mean(dh * hf, axis=-1, keepdims=True))).astype(BF16)


def step_end_grad(rows, w_class, tgt, tokens_total):
    width = rows.shape[1]
    zeta = dot(rows, w_class)
    rf = rows.astype(F32)
    rstd = lax.rsqrt(jnp.sum(rf * rf, axis=1) / width + EPS)
    logits = zeta * rstd[:, None]
    expo = jnp.exp(logits)
    prob = expo / jnp.sum(expo, axis=1, keepdims=True)
    onehot = (tgt[:, None] == jnp.arange(logits.shape[1], dtype=jnp.int32)[None, :]).astype(F32)
    dlog = LOSS_SCALE / tokens_total * (prob - onehot)
    dzeta = dlog * rstd[:, None]
    dmean = jnp.sum(dlog * zeta, axis=1) * -0.5 * rstd * rstd * rstd
    drows = jnp.dot(dzeta, w_class.astype(F32).T, precision=lax.Precision.HIGHEST)
    drows = drows + dmean[:, None] * 2.0 * rf / width
    return drows.astype(BF16)


def among_replicas(x):
    return [x] + [swapped(x, "dp", k) for k in (1, 2, 3)]


def quarters_among_replicas(x, mine_rep):
    ndp = lax.axis_size("dp")
    size = x.shape[1] // ndp
    take = lambda who: lax.dynamic_slice_in_dim(x, who * size, size, axis=1)
    return [take(mine_rep)] + [swapped(take(mine_rep ^ k), "dp", k) for k in (1, 2, 3)]


def by_section(section_at, choices):
    out = choices[-1]
    for s in reversed(range(len(choices) - 1)):
        out = jnp.where(section_at == s, choices[s], out)
    return out


def on_device(embeds, source, lengths, bounds, targets, w_query, w_key, w_value, w_out, w_class):
    nst = lax.axis_size("section")
    peers = lax.axis_size("tensor")
    rep = lax.axis_index("dp")
    section_at = lax.axis_index("section")
    tensor_at = lax.axis_index("tensor")
    ntr, width, dsh = embeds.shape
    wq, wk, wv, wo = w_query[0], w_key[0], w_value[0], w_out[0]
    w_class = lax.all_gather(w_class, "tensor", axis=0, tiled=True)

    hi, core = rep // 2, rep % 2
    slots = source.reshape(2, 2, ntr) - rep * ntr

    def mine_for(col):
        owner = lax.dynamic_slice_in_dim(slots, col, 1, axis=1)[:, 0]
        out = jnp.zeros((2, ntr, width, dsh), BF16)
        for n in range(ntr):
            out = jnp.where((owner == n)[:, :, None, None], embeds[n][None, None], out)
        return out

    both = mine_for(core) + swapped(mine_for(1 - core), "dp", 1)
    own = lax.dynamic_slice_in_dim(both, hi, 1, axis=0)[0]
    away = lax.dynamic_slice_in_dim(both, 1 - hi, 1, axis=0)[0]
    first = [own[j] + swapped(away[j], "dp", 2) for j in range(ntr)]

    wanted = lax.dynamic_slice_in_dim(source, rep * ntr, ntr)
    lens = lengths[wanted]
    bnd = bounds[wanted]
    tgt = targets[wanted]
    tokens_total = jnp.sum(lens).astype(F32)
    keeps = [visible(lens[j], width) for j in range(ntr)]
    picks = [
        (bnd[j][:, None] == jnp.arange(width, dtype=jnp.int32)[None, :]).astype(BF16)
        for j in range(ntr)
    ]
    nstep = bnd.shape[1]

    def ends_to_all(part_rows):
        flat = part_rows.reshape(1, nstep * peers, dsh)
        return jnp.broadcast_to(flat, (peers, nstep * peers, dsh))

    def ends_sum(got):
        return jnp.sum(got.astype(F32), axis=0).reshape(nstep, peers * dsh)

    kept = []
    arriving = None
    for turn in range(nst):
        cur = first[turn] if turn < ntr else jnp.zeros((width, dsh), BF16)
        if arriving is not None:
            cur = jnp.where(section_at == 0, cur, arriving)
        keep = jnp.where(section_at == turn, keeps[0], keeps[1])
        now = forward(gathered(cur), wq, wk, wv, keep)
        kept.append(now)
        part = dot(now["o"], wo).astype(BF16)
        blocks = cut(part)
        if turn == nst - 1:
            ends = dot(picks[0], part).astype(BF16)
            blocks = jnp.concatenate([blocks, ends_to_all(ends)], axis=1)
        got = exchange(blocks)
        share = jnp.sum(got[:, :width].astype(F32), axis=0)
        arriving = passed_along((cur.astype(F32) + share).astype(BF16), "section", 1)

    def end_cotangent(which, parts, full):
        rows = dot(picks[which], full) + parts
        grad = step_end_grad(rows.astype(BF16), w_class, tgt[which], tokens_total)
        return dot_tn(picks[which], grad).astype(BF16)

    taken = {}
    g_top = end_cotangent(0, ends_sum(got[:, width:]), kept[-1]["x"])
    dq, dk, dv = backward_heads(g_top, kept[nst - 1], wo)
    dx = backward_input(dq, dk, dv, kept[nst - 1], wq, wk, wv)
    taken[nst] = (dq, dk, dv, g_top)
    own_cols = lambda whole: lax.dynamic_slice_in_dim(whole, tensor_at * dsh, dsh, axis=1)
    grad = own_cols(g_top)
    now = forward(gathered(arriving), wq, wk, wv, keeps[1])
    kept.append(now)
    ends = dot(dot(picks[1], now["o"]).astype(BF16), wo).astype(BF16)
    got = exchange(jnp.concatenate([cut(dx), ends_to_all(ends)], axis=1))
    g_top = end_cotangent(1, ends_sum(got[:, width:]), now["x"])

    for turn in range(nst + 1, 2 * nst + 1):
        share = jnp.sum(got[:, :width].astype(F32), axis=0)
        grad = passed_along((grad.astype(F32) + share).astype(BF16), "section", -1)
        g_full = gathered(grad)
        if turn == nst + 1:
            g_full = jnp.where(section_at == nst - 1, g_top, g_full)
            grad = jnp.where(section_at == nst - 1, own_cols(g_top), grad)
        late = 2 * nst + 1 - turn
        early = late - 2
        if early < 0:
            old = kept[late]
        else:
            old = {
                name: jnp.where(section_at == early, kept[early][name], kept[late][name])
                for name in kept[late]
            }
        dq, dk, dv = backward_heads(g_full, old, wo)
        taken[turn] = (dq, dk, dv, g_full)
        if turn < 2 * nst:
            dx = backward_input(dq, dk, dv, old, wq, wk, wv)
            got = exchange(cut(dx))

    h_rows, o_rows, g_rows, d_rows = [], [], [], []
    for which in range(ntr):
        h = by_section(section_at, [kept[s + which]["h"] for s in range(nst)])
        o = by_section(section_at, [kept[s + which]["o"] for s in range(nst)])
        back = [taken[2 * nst - 1 - s + which] for s in range(nst)]
        cots = by_section(section_at, [jnp.concatenate(b[:3], axis=1) for b in back])
        g = by_section(section_at, [b[3] for b in back])
        h_rows += quarters_among_replicas(h, rep)
        o_rows += among_replicas(o)
        d_rows += among_replicas(cots)
        g_rows += quarters_among_replicas(g, rep)
    h_rows, o_rows, g_rows, d_rows = (
        jnp.concatenate(part, axis=0) for part in (h_rows, o_rows, g_rows, d_rows)
    )
    qcol, kcol = wq.shape[1], wk.shape[1]
    grad_q = dot_tn(h_rows, d_rows[:, :qcol])
    grad_k = dot_tn(h_rows, d_rows[:, qcol : qcol + kcol])
    grad_v = dot_tn(h_rows, d_rows[:, qcol + kcol :])
    grad_o = dot_tn(o_rows, g_rows)
    return (grad_q[None], grad_k[None], grad_v[None], grad_o[None])


def solution(mesh):
    placed = (
        P("dp", None, "tensor"),
        P(),
        P(),
        P(),
        P(),
        P("section", None, "tensor"),
        P("section", None, "tensor"),
        P("section", None, "tensor"),
        P("section", "tensor", None),
        P("tensor", None),
    )
    return jax.shard_map(
        on_device,
        mesh=mesh,
        in_specs=placed,
        out_specs=(
            P("section", "dp", "tensor"),
            P("section", "dp", "tensor"),
            P("section", "dp", "tensor"),
            P("section", "tensor", "dp"),
        ),
        check_vma=False,
    )
```

```python
import functools

import jax
import jax.numpy as jnp
from jax import lax
from jax.experimental import pallas as pl
from jax.experimental.pallas import tpu as pltpu
from jax.sharding import PartitionSpec as P

HEAD_DIM = 128
EPS = 1e-06
LOSS_SCALE = 16384.0
SCORE_SCALE = 1.0 / HEAD_DIM**0.5
F32 = jnp.float32
BF16 = jnp.bfloat16
VMEM_LIMIT = 48 * 1024 * 1024


def dot(a, b):
    return jnp.dot(a, b, preferred_element_type=F32)


def dot_nt(a, b):
    return lax.dot_general(a, b, (((1,), (1,)), ((), ())), preferred_element_type=F32)


def dot_tn(a, b):
    return lax.dot_general(a, b, (((0,), (0,)), ((), ())), preferred_element_type=F32)


def in_vmem():
    return pl.BlockSpec(memory_space=pltpu.VMEM)


def in_smem():
    return pl.BlockSpec(memory_space=pltpu.SMEM)


def anywhere():
    return pl.BlockSpec(memory_space=pl.ANY)


def kernel_params():
    return pltpu.CompilerParams(vmem_limit_bytes=VMEM_LIMIT)


def forward_kernel(len_ref, x_ref, wq_ref, wk_ref, wv_ref, wo_ref, part_ref, h_ref, scale_ref, pack_ref, o_ref):
    nblk, rows, dsh = x_ref.shape
    qh = wq_ref.shape[1] // HEAD_DIM
    sq = jnp.zeros((rows, 1), F32)
    for j in range(nblk):
        xf = x_ref[j].astype(F32)
        sq = sq + jnp.sum(xf * xf, axis=1, keepdims=True)
    scale = lax.rsqrt(sq / (nblk * dsh) + EPS)
    scale_ref[...] = jnp.broadcast_to(scale, scale_ref.shape)
    q = jnp.zeros((rows, wq_ref.shape[1]), F32)
    k = jnp.zeros((rows, HEAD_DIM), F32)
    v = jnp.zeros((rows, HEAD_DIM), F32)
    for j in range(nblk):
        h = (x_ref[j].astype(F32) * scale).astype(BF16)
        h_ref[j] = h
        at = pl.ds(j * dsh, dsh)
        q = q + dot(h, wq_ref[at, :])
        k = k + dot(h, wk_ref[at, :])
        v = v + dot(h, wv_ref[at, :])
    q = q.astype(BF16)
    k = k.astype(BF16)
    v = v.astype(BF16)
    top = qh * rows
    pack_ref[pl.ds(2 * top, rows), :] = k
    pack_ref[pl.ds(2 * top + rows, rows), :] = v
    posq = lax.broadcasted_iota(jnp.int32, (rows, rows), 0)
    posk = lax.broadcasted_iota(jnp.int32, (rows, rows), 1)
    keep = ((posk <= posq) & (posk < len_ref[0])).astype(F32)
    for n in range(qh):
        qn = q[:, n * HEAD_DIM : (n + 1) * HEAD_DIM]
        pack_ref[pl.ds(n * rows, rows), :] = qn
        expo = jnp.exp(dot_nt(qn, k) * SCORE_SCALE) * keep
        weights = (expo / jnp.sum(expo, axis=1, keepdims=True)).astype(BF16)
        pack_ref[pl.ds(top + n * rows, rows), :] = weights
        o_ref[:, pl.ds(n * HEAD_DIM, HEAD_DIM)] = dot(weights, v).astype(BF16)
    o = o_ref[...]
    for j in range(nblk):
        part_ref[j] = dot(o, wo_ref[:, pl.ds(j * dsh, dsh)]).astype(BF16)


def forward(length, x, wq, wk, wv, wo):
    nblk, rows, dsh = x.shape
    qcol = wq.shape[1]
    packed = 2 * qcol // HEAD_DIM * rows + 2 * rows
    out = pl.pallas_call(
        forward_kernel,
        out_shape=(
            jax.ShapeDtypeStruct(x.shape, BF16),
            jax.ShapeDtypeStruct(x.shape, BF16),
            jax.ShapeDtypeStruct((rows, HEAD_DIM), F32),
            jax.ShapeDtypeStruct((packed, HEAD_DIM), BF16),
            jax.ShapeDtypeStruct((rows, qcol), BF16),
        ),
        in_specs=[in_smem()] + [in_vmem()] * 5,
        out_specs=tuple([in_vmem()] * 5),
        compiler_params=kernel_params(),
        cost_estimate=pl.CostEstimate(
            flops=2 * rows * nblk * dsh * (2 * qcol + 2 * HEAD_DIM),
            bytes_accessed=4 * nblk * dsh * (qcol + HEAD_DIM),
            transcendentals=rows * rows * qcol // HEAD_DIM,
        ),
        name="forward_layer",
    )(length.reshape(1), x, wq, wk, wv, wo)
    return dict(zip(("part", "h", "scale", "pack", "o"), out))


def backward_kernel(
    with_input, flag_ref, g_ref, pack0_ref, pack1_ref, h0_ref, h1_ref, scale0_ref, scale1_ref,
    wq_ref, wk_ref, wv_ref, wo_ref, *rest
):
    if with_input:
        d_ref, dx_ref, pack_ref, h_ref, scale_ref, dh_ref, sems = rest
    else:
        d_ref, pack_ref, sems = rest
    nblk, rows, dsh = g_ref.shape
    qcol = wq_ref.shape[1]
    qh = qcol // HEAD_DIM
    top = qh * rows
    pairs = [(pack0_ref, pack1_ref, pack_ref)]
    if with_input:
        pairs += [(h0_ref, h1_ref, h_ref), (scale0_ref, scale1_ref, scale_ref)]
    for at, (one, two, to) in enumerate(pairs):

        @pl.when(flag_ref[0] == 0)
        def _(one=one, to=to, at=at):
            pltpu.make_async_copy(one, to, sems.at[at]).start()

        @pl.when(flag_ref[0] != 0)
        def _(two=two, to=to, at=at):
            pltpu.make_async_copy(two, to, sems.at[at]).start()

    do = jnp.zeros((rows, qcol), F32)
    for j in range(nblk):
        do = do + dot_nt(g_ref[j], wo_ref[:, pl.ds(j * dsh, dsh)])
    do = do.astype(BF16)
    pltpu.make_async_copy(pack0_ref, pack_ref, sems.at[0]).wait()
    k = pack_ref[pl.ds(2 * top, rows), :]
    v = pack_ref[pl.ds(2 * top + rows, rows), :]
    dk = jnp.zeros((rows, HEAD_DIM), F32)
    dv = jnp.zeros((rows, HEAD_DIM), F32)
    for n in range(qh):
        cols = slice(n * HEAD_DIM, (n + 1) * HEAD_DIM)
        qn = pack_ref[pl.ds(n * rows, rows), :]
        weights = pack_ref[pl.ds(top + n * rows, rows), :]
        don = do[:, cols]
        wf = weights.astype(F32)
        dw = dot_nt(don, v)
        ds = wf * (dw - jnp.sum(dw * wf, axis=1, keepdims=True)) * SCORE_SCALE
        ds = ds.astype(BF16)
        d_ref[:, cols] = dot(ds, k).astype(BF16)
        dk = dk + dot_tn(ds, qn)
        dv = dv + dot_tn(weights, don)
    d_ref[:, qcol : qcol + HEAD_DIM] = dk.astype(BF16)
    d_ref[:, qcol + HEAD_DIM :] = dv.astype(BF16)
    if not with_input:
        return
    pltpu.make_async_copy(h0_ref, h_ref, sems.at[1]).wait()
    pltpu.make_async_copy(scale0_ref, scale_ref, sems.at[2]).wait()
    dq = d_ref[:, :qcol]
    dk = dk.astype(BF16)
    dv = dv.astype(BF16)
    inner = jnp.zeros((rows, 1), F32)
    for j in range(nblk):
        at = pl.ds(j * dsh, dsh)
        dh = dot_nt(dq, wq_ref[at, :]) + dot_nt(dk, wk_ref[at, :]) + dot_nt(dv, wv_ref[at, :])
        dh_ref[j] = dh
        inner = inner + jnp.sum(dh * h_ref[j].astype(F32), axis=1, keepdims=True)
    inner = inner / (nblk * dsh)
    scale = scale_ref[:, :1]
    for j in range(nblk):
        dx_ref[j] = (scale * (dh_ref[j] - h_ref[j].astype(F32) * inner)).astype(BF16)


def backward(flag, g, one, two, weights, with_input):
    nblk, rows, dsh = g.shape
    wq, wk, wv, wo = weights
    qcol = wq.shape[1]
    out_shape = [jax.ShapeDtypeStruct((rows, qcol + 2 * HEAD_DIM), BF16)]
    scratch = [pltpu.VMEM(one["pack"].shape, BF16)]
    if with_input:
        out_shape.append(jax.ShapeDtypeStruct(g.shape, BF16))
        scratch += [
            pltpu.VMEM(g.shape, BF16),
            pltpu.VMEM(one["scale"].shape, F32),
            pltpu.VMEM(g.shape, F32),
        ]
    scratch.append(pltpu.SemaphoreType.DMA((3,)))
    return pl.pallas_call(
        functools.partial(backward_kernel, with_input),
        out_shape=tuple(out_shape),
        in_specs=[in_smem(), in_vmem()] + [anywhere()] * 6 + [in_vmem()] * 4,
        out_specs=tuple([in_vmem()] * len(out_shape)),
        scratch_shapes=scratch,
        compiler_params=kernel_params(),
        cost_estimate=pl.CostEstimate(
            flops=2 * rows * nblk * dsh * (2 * qcol + 2 * HEAD_DIM),
            bytes_accessed=4 * nblk * dsh * (qcol + HEAD_DIM),
            transcendentals=0,
        ),
        name="backward_layer" if with_input else "backward_heads",
    )(
        flag.astype(jnp.int32).reshape(1), g, one["pack"], two["pack"], one["h"], two["h"],
        one["scale"], two["scale"], wq, wk, wv, wo,
    )


def qkv_grad_kernel(n, *refs):
    h_refs, d_refs = refs[:n], refs[n : 2 * n]
    gq_ref, gk_ref, gv_ref, h_all, d_all = refs[2 * n :]
    rows = d_refs[0].shape[0]
    nblk, _, dsh = h_refs[0].shape
    qcol = gq_ref.shape[1]
    for i in range(n):
        at = pl.ds(i * rows, rows)
        d_all[at, :] = d_refs[i][...]
        for b in range(nblk):
            h_all[at, pl.ds(b * dsh, dsh)] = h_refs[i][b]
    for c in range(nblk * dsh // 256):
        cols = pl.ds(c * 256, 256)
        got = dot_tn(h_all[:, cols], d_all[...])
        gq_ref[cols, :] = got[:, :qcol]
        gk_ref[cols, :] = got[:, qcol : qcol + HEAD_DIM]
        gv_ref[cols, :] = got[:, qcol + HEAD_DIM :]


def qkv_grad(h, d):
    n = len(h)
    rows, dcol = d[0].shape
    nblk, _, dsh = h[0].shape
    width = nblk * dsh
    return pl.pallas_call(
        functools.partial(qkv_grad_kernel, n),
        out_shape=(
            jax.ShapeDtypeStruct((width, dcol - 2 * HEAD_DIM), F32),
            jax.ShapeDtypeStruct((width, HEAD_DIM), F32),
            jax.ShapeDtypeStruct((width, HEAD_DIM), F32),
        ),
        in_specs=[in_vmem()] * (2 * n),
        out_specs=tuple([in_vmem()] * 3),
        scratch_shapes=[pltpu.VMEM((n * rows, width), BF16), pltpu.VMEM((n * rows, dcol), BF16)],
        compiler_params=kernel_params(),
        name="qkv_grad",
    )(*h, *d)


def out_grad_kernel(n, *refs):
    o_refs, g_refs = refs[:n], refs[n : 2 * n]
    go_ref, o_all, g_all = refs[2 * n :]
    rows, qcol = o_refs[0].shape
    nblk, _, dsh = g_refs[0].shape
    for i in range(n):
        at = pl.ds(i * rows, rows)
        o_all[at, :] = o_refs[i][...]
        for b in range(nblk):
            g_all[at, pl.ds(b * dsh, dsh)] = g_refs[i][b]
    for c in range(qcol // 256):
        cols = pl.ds(c * 256, 256)
        go_ref[cols, :] = dot_tn(o_all[:, cols], g_all[...])


def out_grad(o, g):
    n = len(o)
    rows, qcol = o[0].shape
    nblk, _, dsh = g[0].shape
    width = nblk * dsh
    return pl.pallas_call(
        functools.partial(out_grad_kernel, n),
        out_shape=jax.ShapeDtypeStruct((qcol, width), F32),
        in_specs=[in_vmem()] * (2 * n),
        out_specs=in_vmem(),
        scratch_shapes=[pltpu.VMEM((n * rows, qcol), BF16), pltpu.VMEM((n * rows, width), BF16)],
        compiler_params=kernel_params(),
        name="out_grad",
    )(*o, *g)


def passed_along(x, axis, by):
    peers = lax.axis_size(axis)
    pairs = [(i, i + by) for i in range(peers) if 0 <= i + by < peers]
    return lax.ppermute(x, axis, pairs)


def swapped(x, axis, mask):
    return lax.ppermute(x, axis, [(i, i ^ mask) for i in range(lax.axis_size(axis))])


def exchange(blocks):
    return lax.all_to_all(blocks, "tensor", split_axis=0, concat_axis=0, tiled=True)


def gathered(cur):
    return exchange(jnp.broadcast_to(cur[None], (lax.axis_size("tensor"),) + cur.shape))


def step_end_grad(rows, w_class, tgt, tokens_total):
    width = rows.shape[1]
    zeta = dot(rows, w_class)
    rf = rows.astype(F32)
    rstd = lax.rsqrt(jnp.sum(rf * rf, axis=1) / width + EPS)
    logits = zeta * rstd[:, None]
    expo = jnp.exp(logits)
    prob = expo / jnp.sum(expo, axis=1, keepdims=True)
    onehot = (tgt[:, None] == jnp.arange(logits.shape[1], dtype=jnp.int32)[None, :]).astype(F32)
    dlog = LOSS_SCALE / tokens_total * (prob - onehot)
    dzeta = dlog * rstd[:, None]
    dmean = jnp.sum(dlog * zeta, axis=1) * -0.5 * rstd * rstd * rstd
    drows = jnp.dot(dzeta, w_class.astype(F32).T, precision=lax.Precision.HIGHEST)
    drows = drows + dmean[:, None] * 2.0 * rf / width
    return drows.astype(BF16)


def among_replicas(x):
    return [x] + [swapped(x, "dp", k) for k in (1, 2, 3)]


def quarters_among_replicas(x, mine_rep):
    ndp = lax.axis_size("dp")
    size = x.shape[0] // ndp
    take = lambda who: lax.dynamic_slice_in_dim(x, who * size, size, axis=0)
    return [take(mine_rep)] + [swapped(take(mine_rep ^ k), "dp", k) for k in (1, 2, 3)]


def by_section(section_at, choices):
    out = choices[-1]
    for s in reversed(range(len(choices) - 1)):
        out = jnp.where(section_at == s, choices[s], out)
    return out


def after(x, *marks):
    return lax.optimization_barrier((x,) + marks)[0]


def on_device(embeds, source, lengths, bounds, targets, w_query, w_key, w_value, w_out, w_class):
    nst = lax.axis_size("section")
    peers = lax.axis_size("tensor")
    rep = lax.axis_index("dp")
    section_at = lax.axis_index("section")
    tensor_at = lax.axis_index("tensor")
    ntr, width, dsh = embeds.shape
    weights = (w_query[0], w_key[0], w_value[0], w_out[0])
    w_class = lax.all_gather(w_class, "tensor", axis=0, tiled=True)

    hi, core = rep // 2, rep % 2
    slots = source.reshape(2, 2, ntr) - rep * ntr

    def mine_for(col):
        owner = lax.dynamic_slice_in_dim(slots, col, 1, axis=1)[:, 0]
        out = jnp.zeros((2, ntr, width, dsh), BF16)
        for n in range(ntr):
            out = jnp.where((owner == n)[:, :, None, None], embeds[n][None, None], out)
        return out

    both = mine_for(core) + swapped(mine_for(1 - core), "dp", 1)
    own = lax.dynamic_slice_in_dim(both, hi, 1, axis=0)[0]
    away = lax.dynamic_slice_in_dim(both, 1 - hi, 1, axis=0)[0]
    first = [own[j] + swapped(away[j], "dp", 2) for j in range(ntr)]

    wanted = lax.dynamic_slice_in_dim(source, rep * ntr, ntr)
    lens = lengths[wanted]
    bnd = bounds[wanted]
    tgt = targets[wanted]
    tokens_total = jnp.sum(lens).astype(F32)
    picks = [
        (bnd[j][:, None] == jnp.arange(width, dtype=jnp.int32)[None, :]).astype(BF16)
        for j in range(ntr)
    ]
    nstep = bnd.shape[1]

    def ends_of(which, blocks):
        return jnp.einsum("sr,brd->bsd", picks[which], blocks, preferred_element_type=F32)

    def with_ends(blocks, ends):
        flat = ends.astype(BF16).reshape(1, peers * nstep, dsh)
        return jnp.concatenate(
            [blocks, jnp.broadcast_to(flat, (peers, peers * nstep, dsh))], axis=1
        )

    def sum_of(got):
        return jnp.sum(got[:, :width].astype(F32), axis=0)

    def end_cotangent(which, got, x):
        parts = jnp.sum(got[:, width:].astype(F32), axis=0).reshape(peers, nstep, dsh)
        rows = (ends_of(which, x) + parts).astype(BF16)
        rows = rows.transpose(1, 0, 2).reshape(nstep, peers * dsh)
        grad = step_end_grad(rows, w_class, tgt[which], tokens_total)
        grad = grad.reshape(nstep, peers, dsh)
        back = jnp.einsum("sr,sbd->brd", picks[which], grad, preferred_element_type=F32)
        return back.astype(BF16)

    kept = []
    arriving = None
    for turn in range(nst):
        cur = first[turn] if turn < ntr else jnp.zeros((width, dsh), BF16)
        if arriving is not None:
            cur = jnp.where(section_at == 0, cur, arriving)
        length = jnp.where(section_at == turn, lens[0], lens[1])
        x = gathered(cur)
        now = forward(length, x, *weights)
        kept.append(now)
        blocks = now["part"]
        if turn == nst - 1:
            blocks = with_ends(blocks, ends_of(0, blocks))
        got = exchange(blocks)
        arriving = passed_along((cur.astype(F32) + sum_of(got)).astype(BF16), "section", 1)

    taken = {}
    top = jnp.int32(0)
    g_top = end_cotangent(0, got, x)
    grad = lax.dynamic_slice_in_dim(g_top, tensor_at, 1, axis=0)[0]
    d, dx = backward(top, after(g_top, arriving), kept[-1], kept[-1], weights, True)
    taken[nst] = (d, g_top)
    x = gathered(arriving)
    now = forward(lens[1], x, *weights)
    kept.append(now)
    got = exchange(with_ends(dx, ends_of(1, now["part"])))
    g_top = end_cotangent(1, got, x)

    h_rows, o_rows, g_rows, d_rows = [], [], [], []
    for turn in range(nst + 1, 2 * nst + 1):
        grad = (grad.astype(F32) + sum_of(got)).astype(BF16)
        which = turn - nst - 1
        if which < ntr:
            h = by_section(section_at, [kept[s + which]["h"] for s in range(nst)])
            o = by_section(section_at, [kept[s + which]["o"] for s in range(nst)])
            h_rows += quarters_among_replicas(after(h, grad), rep)
            o_rows += among_replicas(after(o, grad))
        elif turn == 2 * nst:
            back = [taken[2 * nst - 1 - s] for s in range(nst)]
            d_rows += among_replicas(after(by_section(section_at, [b[0] for b in back]), grad))
            g_rows += quarters_among_replicas(
                after(by_section(section_at, [b[1] for b in back]), grad), rep
            )
        grad = passed_along(grad, "section", -1)
        g = gathered(grad)
        if turn == nst + 1:
            g = jnp.where(section_at == nst - 1, g_top, g)
            own_top = lax.dynamic_slice_in_dim(g_top, tensor_at, 1, axis=0)[0]
            grad = jnp.where(section_at == nst - 1, own_top, grad)
        late = 2 * nst + 1 - turn
        early = max(late - 2, 0)
        flag = section_at == late - 1
        if turn < 2 * nst:
            d, dx = backward(flag, g, kept[early], kept[late], weights, True)
            taken[turn] = (d, g)
            got = exchange(dx)
        else:
            (d,) = backward(flag, g, kept[early], kept[late], weights, False)
            taken[turn] = (d, g)

    back = [taken[2 * nst - s] for s in range(nst)]
    g_rows += quarters_among_replicas(by_section(section_at, [b[1] for b in back]), rep)
    d_rows += among_replicas(by_section(section_at, [b[0] for b in back]))
    grad_q, grad_k, grad_v = qkv_grad(h_rows, d_rows)
    grad_o = out_grad(o_rows, g_rows)
    return (grad_q[None], grad_k[None], grad_v[None], grad_o[None])


def solution(mesh):
    placed = (
        P("dp", None, "tensor"),
        P(),
        P(),
        P(),
        P(),
        P("section", None, "tensor"),
        P("section", None, "tensor"),
        P("section", None, "tensor"),
        P("section", "tensor", None),
        P("tensor", None),
    )
    return jax.shard_map(
        on_device,
        mesh=mesh,
        in_specs=placed,
        out_specs=(
            P("section", "dp", "tensor"),
            P("section", "dp", "tensor"),
            P("section", "dp", "tensor"),
            P("section", "tensor", "dp"),
        ),
        check_vma=False,
    )
```

```python
import functools

import jax
import jax.numpy as jnp
from jax import lax
from jax.experimental import pallas as pl
from jax.experimental.pallas import tpu as pltpu
from jax.sharding import PartitionSpec as P

HEAD_DIM = 128
EPS = 1e-06
LOSS_SCALE = 16384.0
SCORE_SCALE = 1.0 / HEAD_DIM**0.5
F32 = jnp.float32
BF16 = jnp.bfloat16
SMALL_VMEM = 16 * 1024 * 1024
LARGE_VMEM = 48 * 1024 * 1024


def dot(a, b):
    return jnp.dot(a, b, preferred_element_type=F32)


def dot_nt(a, b):
    return lax.dot_general(a, b, (((1,), (1,)), ((), ())), preferred_element_type=F32)


def dot_tn(a, b):
    return lax.dot_general(a, b, (((0,), (0,)), ((), ())), preferred_element_type=F32)


def in_vmem():
    return pl.BlockSpec(memory_space=pltpu.VMEM)


def in_smem():
    return pl.BlockSpec(memory_space=pltpu.SMEM)


def in_hbm():
    return pl.BlockSpec(memory_space=pltpu.HBM)


def kernel_params(limit):
    return pltpu.CompilerParams(vmem_limit_bytes=limit)


def weight_scratch(wq, wk, wv, wo):
    return [pltpu.VMEM(w.shape, BF16) for w in (wq, wk, wv, wo)]


def weight_copies(hbm, vmem, sems, out_first):
    wq, wk, wv, wo = zip(hbm, vmem)
    qkv, out = [], []
    step = wq[0].shape[0] // 4
    for n in range(4):
        rows = pl.ds(n * step, step)
        qkv.append(
            [
                pltpu.make_async_copy(one.at[rows, :], to.at[rows, :], sems.at[0, n, at])
                for at, (one, to) in enumerate((wq, wk, wv))
            ]
        )
        out.append(
            [pltpu.make_async_copy(wo[0].at[:, rows], wo[1].at[:, rows], sems.at[1, n, 0])]
        )
    for part in (out + qkv) if out_first else (qkv + out):
        for copy in part:
            copy.start()
    return qkv, out


def arrived(copies):
    for copy in copies:
        copy.wait()


def forward_kernel(resident, len_ref, x_ref, wq_in, wk_in, wv_in, wo_in, *rest):
    part_ref, h_ref, scale_ref, pack_ref, o_ref = rest[:5]
    nblk, rows, dsh = x_ref.shape
    qh = wq_in.shape[1] // HEAD_DIM
    if resident:
        wq_ref, wk_ref, wv_ref, wo_ref = wq_in, wk_in, wv_in, wo_in
        qkv = out = [()] * 4
    else:
        wq_ref, wk_ref, wv_ref, wo_ref, sems = rest[5:]
        qkv, out = weight_copies(
            (wq_in, wk_in, wv_in, wo_in), (wq_ref, wk_ref, wv_ref, wo_ref), sems, False
        )
    sq = jnp.zeros((rows, 1), F32)
    for j in range(nblk):
        xf = x_ref[j].astype(F32)
        sq = sq + jnp.sum(xf * xf, axis=1, keepdims=True)
    scale = lax.rsqrt(sq / (nblk * dsh) + EPS)
    scale_ref[...] = jnp.broadcast_to(scale, scale_ref.shape)
    q = jnp.zeros((rows, wq_ref.shape[1]), F32)
    k = jnp.zeros((rows, HEAD_DIM), F32)
    v = jnp.zeros((rows, HEAD_DIM), F32)
    for j in range(nblk):
        h = (x_ref[j].astype(F32) * scale).astype(BF16)
        h_ref[j] = h
        if j % (nblk // 4) == 0:
            arrived(qkv[j // (nblk // 4)])
        at = pl.ds(j * dsh, dsh)
        q = q + dot(h, wq_ref[at, :])
        k = k + dot(h, wk_ref[at, :])
        v = v + dot(h, wv_ref[at, :])
    q = q.astype(BF16)
    k = k.astype(BF16)
    v = v.astype(BF16)
    top = qh * rows
    pack_ref[pl.ds(2 * top, rows), :] = k
    pack_ref[pl.ds(2 * top + rows, rows), :] = v
    posq = lax.broadcasted_iota(jnp.int32, (rows, rows), 0)
    posk = lax.broadcasted_iota(jnp.int32, (rows, rows), 1)
    keep = ((posk <= posq) & (posk < len_ref[0])).astype(F32)
    for n in range(qh):
        qn = q[:, n * HEAD_DIM : (n + 1) * HEAD_DIM]
        pack_ref[pl.ds(n * rows, rows), :] = qn
        expo = jnp.exp(dot_nt(qn, k) * SCORE_SCALE) * keep
        weights = (expo / jnp.sum(expo, axis=1, keepdims=True)).astype(BF16)
        pack_ref[pl.ds(top + n * rows, rows), :] = weights
        o_ref[:, pl.ds(n * HEAD_DIM, HEAD_DIM)] = dot(weights, v).astype(BF16)
    o = o_ref[...]
    for j in range(nblk):
        if j % (nblk // 4) == 0:
            arrived(out[j // (nblk // 4)])
        part_ref[j] = dot(o, wo_ref[:, pl.ds(j * dsh, dsh)]).astype(BF16)


def forward(length, x, wq, wk, wv, wo, resident):
    nblk, rows, dsh = x.shape
    qcol = wq.shape[1]
    packed = 2 * qcol // HEAD_DIM * rows + 2 * rows
    outs = [(x.shape, BF16), (x.shape, BF16)]
    outs += [((rows, HEAD_DIM), F32), ((packed, HEAD_DIM), BF16), ((rows, qcol), BF16)]
    own = weight_scratch(wq, wk, wv, wo) + [pltpu.SemaphoreType.DMA((2, 4, 3))]
    out = pl.pallas_call(
        functools.partial(forward_kernel, resident),
        out_shape=tuple(jax.ShapeDtypeStruct(*one) for one in outs),
        in_specs=[in_smem(), in_vmem()] + [in_vmem() if resident else in_hbm()] * 4,
        out_specs=tuple([in_vmem()] * 5),
        scratch_shapes=[] if resident else own,
        compiler_params=kernel_params(SMALL_VMEM if resident else LARGE_VMEM),
        cost_estimate=pl.CostEstimate(
            flops=2 * rows * nblk * dsh * (2 * qcol + 2 * HEAD_DIM),
            bytes_accessed=4 * nblk * dsh * (qcol + HEAD_DIM),
            transcendentals=rows * rows * qcol // HEAD_DIM,
        ),
        name="forward_layer",
    )(length.reshape(1), x, wq, wk, wv, wo)
    return dict(zip(("part", "h", "scale", "pack", "o"), out))


def backward_kernel(
    with_input, flag_ref, g_ref, pack0_ref, pack1_ref, h0_ref, h1_ref, scale0_ref, scale1_ref,
    wq_any, wk_any, wv_any, wo_any, *rest
):
    if with_input:
        d_ref, dx_ref, wq_ref, wk_ref, wv_ref, wo_ref, pack_ref, sems, keep_sems = rest[:9]
        h_ref, scale_ref, dh_ref = rest[9:]
    else:
        d_ref, wo_ref, pack_ref, sems, keep_sems = rest
    nblk, rows, dsh = g_ref.shape
    qcol = wq_any.shape[1]
    qh = qcol // HEAD_DIM
    top = qh * rows
    if with_input:
        qkv, out = weight_copies(
            (wq_any, wk_any, wv_any, wo_any), (wq_ref, wk_ref, wv_ref, wo_ref), sems, True
        )
    else:
        step = nblk * dsh // 4
        out = []
        for n in range(4):
            cols = pl.ds(n * step, step)
            copy = pltpu.make_async_copy(wo_any.at[:, cols], wo_ref.at[:, cols], sems.at[1, n, 0])
            copy.start()
            out.append([copy])
    pairs = [(pack0_ref, pack1_ref, pack_ref)]
    if with_input:
        pairs += [(h0_ref, h1_ref, h_ref), (scale0_ref, scale1_ref, scale_ref)]
    for at, (one, two, to) in enumerate(pairs):

        @pl.when(flag_ref[0] == 0)
        def _(one=one, to=to, at=at):
            pltpu.make_async_copy(one, to, keep_sems.at[at]).start()

        @pl.when(flag_ref[0] != 0)
        def _(two=two, to=to, at=at):
            pltpu.make_async_copy(two, to, keep_sems.at[at]).start()

    do = jnp.zeros((rows, qcol), F32)
    for j in range(nblk):
        if j % (nblk // 4) == 0:
            arrived(out[j // (nblk // 4)])
        do = do + dot_nt(g_ref[j], wo_ref[:, pl.ds(j * dsh, dsh)])
    do = do.astype(BF16)
    pltpu.make_async_copy(pack0_ref, pack_ref, keep_sems.at[0]).wait()
    k = pack_ref[pl.ds(2 * top, rows), :]
    v = pack_ref[pl.ds(2 * top + rows, rows), :]
    dk = jnp.zeros((rows, HEAD_DIM), F32)
    dv = jnp.zeros((rows, HEAD_DIM), F32)
    for n in range(qh):
        cols = slice(n * HEAD_DIM, (n + 1) * HEAD_DIM)
        qn = pack_ref[pl.ds(n * rows, rows), :]
        weights = pack_ref[pl.ds(top + n * rows, rows), :]
        don = do[:, cols]
        wf = weights.astype(F32)
        dw = dot_nt(don, v)
        ds = wf * (dw - jnp.sum(dw * wf, axis=1, keepdims=True)) * SCORE_SCALE
        ds = ds.astype(BF16)
        d_ref[:, cols] = dot(ds, k).astype(BF16)
        dk = dk + dot_tn(ds, qn)
        dv = dv + dot_tn(weights, don)
    d_ref[:, qcol : qcol + HEAD_DIM] = dk.astype(BF16)
    d_ref[:, qcol + HEAD_DIM :] = dv.astype(BF16)
    if not with_input:
        return
    pltpu.make_async_copy(h0_ref, h_ref, keep_sems.at[1]).wait()
    pltpu.make_async_copy(scale0_ref, scale_ref, keep_sems.at[2]).wait()
    dq = d_ref[:, :qcol]
    dk = dk.astype(BF16)
    dv = dv.astype(BF16)
    inner = jnp.zeros((rows, 1), F32)
    for j in range(nblk):
        if j % (nblk // 4) == 0:
            arrived(qkv[j // (nblk // 4)])
        at = pl.ds(j * dsh, dsh)
        dh = dot_nt(dq, wq_ref[at, :]) + dot_nt(dk, wk_ref[at, :]) + dot_nt(dv, wv_ref[at, :])
        dh_ref[j] = dh
        inner = inner + jnp.sum(dh * h_ref[j].astype(F32), axis=1, keepdims=True)
    inner = inner / (nblk * dsh)
    scale = scale_ref[:, :1]
    for j in range(nblk):
        dx_ref[j] = (scale * (dh_ref[j] - h_ref[j].astype(F32) * inner)).astype(BF16)


def backward(flag, g, one, two, weights, with_input):
    nblk, rows, dsh = g.shape
    wq, wk, wv, wo = weights
    qcol = wq.shape[1]
    out_shape = [jax.ShapeDtypeStruct((rows, qcol + 2 * HEAD_DIM), BF16)]
    scratch = weight_scratch(*weights) if with_input else [pltpu.VMEM(wo.shape, BF16)]
    scratch += [
        pltpu.VMEM(one["pack"].shape, BF16),
        pltpu.SemaphoreType.DMA((2, 4, 3)),
        pltpu.SemaphoreType.DMA((3,)),
    ]
    if with_input:
        out_shape.append(jax.ShapeDtypeStruct(g.shape, BF16))
        scratch += [
            pltpu.VMEM(g.shape, BF16),
            pltpu.VMEM(one["scale"].shape, F32),
            pltpu.VMEM(g.shape, F32),
        ]
    return pl.pallas_call(
        functools.partial(backward_kernel, with_input),
        out_shape=tuple(out_shape),
        in_specs=[in_smem(), in_vmem()] + [in_hbm()] * 10,
        out_specs=tuple([in_vmem()] * len(out_shape)),
        scratch_shapes=scratch,
        compiler_params=kernel_params(LARGE_VMEM),
        cost_estimate=pl.CostEstimate(
            flops=2 * rows * nblk * dsh * (2 * qcol + 2 * HEAD_DIM),
            bytes_accessed=4 * nblk * dsh * (qcol + HEAD_DIM),
            transcendentals=0,
        ),
        name="backward_layer" if with_input else "backward_heads",
    )(
        flag.astype(jnp.int32).reshape(1), g, one["pack"], two["pack"], one["h"], two["h"],
        one["scale"], two["scale"], wq, wk, wv, wo,
    )


def rows_grad_kernel(n, splits, with_total, *refs):
    a_refs, b_refs, refs = refs[:n], refs[n : 2 * n], refs[2 * n :]
    totals, refs = (refs[: len(splits)], refs[len(splits) :]) if with_total else ((), refs)
    outs, (a_all, b_all) = refs[: len(splits)], refs[len(splits) :]
    rows = a_refs[0].shape[-2]

    def place(to, piece, i):
        at = pl.ds(i * rows, rows)
        if len(piece.shape) == 2:
            to[at, :] = piece[...]
        else:
            for b in range(piece.shape[0]):
                to[at, pl.ds(b * piece.shape[2], piece.shape[2])] = piece[b]

    for i in range(n):
        place(a_all, a_refs[i], i)
        place(b_all, b_refs[i], i)
    for c in range(a_all.shape[1] // 256):
        cols = pl.ds(c * 256, 256)
        got = dot_tn(a_all[:, cols], b_all[...])
        for i, (start, stop) in enumerate(splits):
            part = got[:, start:stop]
            outs[i][cols, :] = totals[i][cols, :] + part if with_total else part


def rows_grad(a, b, widths, totals=()):
    n = len(a)
    wide = lambda x: x.shape[-1] * (x.shape[0] if x.ndim == 3 else 1)
    rows = a[0].shape[-2]
    splits, at = [], 0
    for w in widths:
        splits.append((at, at + w))
        at += w
    return pl.pallas_call(
        functools.partial(rows_grad_kernel, n, splits, bool(totals)),
        out_shape=tuple(jax.ShapeDtypeStruct((wide(a[0]), w), F32) for w in widths),
        in_specs=[in_vmem()] * (2 * n + len(totals)),
        out_specs=tuple([in_vmem()] * len(widths)),
        scratch_shapes=[
            pltpu.VMEM((n * rows, wide(a[0])), BF16),
            pltpu.VMEM((n * rows, wide(b[0])), BF16),
        ],
        compiler_params=kernel_params(LARGE_VMEM),
        cost_estimate=pl.CostEstimate(
            flops=2 * n * rows * wide(a[0]) * wide(b[0]),
            bytes_accessed=4 * wide(a[0]) * wide(b[0]),
            transcendentals=0,
        ),
        name="weight_grad",
    )(*a, *b, *totals)


def passed_along(x, axis, by):
    peers = lax.axis_size(axis)
    pairs = [(i, i + by) for i in range(peers) if 0 <= i + by < peers]
    return lax.ppermute(x, axis, pairs)


def swapped(x, axis, mask):
    return lax.ppermute(x, axis, [(i, i ^ mask) for i in range(lax.axis_size(axis))])


def mirrored(x, mask):
    ndp, peers = lax.axis_size("dp"), lax.axis_size("tensor")
    to = lambda p, r: (p ^ mask) * peers + (r + peers // 2) % peers
    pairs = [(p * peers + r, to(p, r)) for p in range(ndp) for r in range(peers)]
    return lax.ppermute(x, ("dp", "tensor"), pairs)


def exchange(blocks):
    return lax.all_to_all(blocks, "tensor", split_axis=0, concat_axis=0, tiled=True)


def gathered(cur):
    return exchange(jnp.broadcast_to(cur[None], (lax.axis_size("tensor"),) + cur.shape))


def step_end_grad(rows, w_class, tgt, tokens_total):
    width = rows.shape[1]
    zeta = dot(rows, w_class)
    rf = rows.astype(F32)
    rstd = lax.rsqrt(jnp.sum(rf * rf, axis=1) / width + EPS)
    logits = zeta * rstd[:, None]
    expo = jnp.exp(logits)
    prob = expo / jnp.sum(expo, axis=1, keepdims=True)
    onehot = (tgt[:, None] == jnp.arange(logits.shape[1], dtype=jnp.int32)[None, :]).astype(F32)
    dlog = LOSS_SCALE / tokens_total * (prob - onehot)
    dzeta = dlog * rstd[:, None]
    dmean = jnp.sum(dlog * zeta, axis=1) * -0.5 * rstd * rstd * rstd
    drows = jnp.dot(dzeta, w_class.astype(F32).T, precision=lax.Precision.HIGHEST)
    drows = drows + dmean[:, None] * 2.0 * rf / width
    return drows.astype(BF16)


def by_section(section_at, choices):
    out = choices[-1]
    for s in reversed(range(len(choices) - 1)):
        out = jnp.where(section_at == s, choices[s], out)
    return out


def after(x, *marks):
    return lax.optimization_barrier((x,) + marks)[0]


def together(*xs):
    return lax.optimization_barrier(xs)


def on_device(embeds, source, lengths, bounds, targets, w_query, w_key, w_value, w_out, w_class):
    nst = lax.axis_size("section")
    peers = lax.axis_size("tensor")
    rep = lax.axis_index("dp")
    section_at = lax.axis_index("section")
    tensor_at = lax.axis_index("tensor")
    ntr, width, dsh = embeds.shape
    weights = (w_query[0], w_key[0], w_value[0], w_out[0])
    w_class = lax.all_gather(w_class, "tensor", axis=0, tiled=True)

    hi, core = rep // 2, rep % 2
    slots = source.reshape(2, 2, ntr) - rep * ntr

    def mine_for(col):
        owner = lax.dynamic_slice_in_dim(slots, col, 1, axis=1)[:, 0]
        out = jnp.zeros((2, ntr, width, dsh), BF16)
        for n in range(ntr):
            out = jnp.where((owner == n)[:, :, None, None], embeds[n][None, None], out)
        return out

    both = mine_for(core) + swapped(mine_for(1 - core), "dp", 1)
    own = lax.dynamic_slice_in_dim(both, hi, 1, axis=0)[0]
    away = lax.dynamic_slice_in_dim(both, 1 - hi, 1, axis=0)[0]
    away = [away[j] for j in range(ntr)]

    def first(j):
        return own[j] + swapped(away[j], "dp", 2)


    wanted = lax.dynamic_slice_in_dim(source, rep * ntr, ntr)
    lens = lengths[wanted]
    bnd = bounds[wanted]
    tgt = targets[wanted]
    tokens_total = jnp.sum(lens).astype(F32)
    picks = [
        (bnd[j][:, None] == jnp.arange(width, dtype=jnp.int32)[None, :]).astype(BF16)
        for j in range(ntr)
    ]
    nstep = bnd.shape[1]

    def ends_of(which, blocks):
        return jnp.einsum("sr,brd->bsd", picks[which], blocks, preferred_element_type=F32)

    def with_ends(blocks, ends):
        flat = ends.astype(BF16).reshape(1, peers * nstep, dsh)
        return jnp.concatenate(
            [blocks, jnp.broadcast_to(flat, (peers, peers * nstep, dsh))], axis=1
        )

    def sum_of(got):
        return jnp.sum(got[:, :width].astype(F32), axis=0)

    def end_cotangent(which, got, x):
        parts = jnp.sum(got[:, width:].astype(F32), axis=0).reshape(peers, nstep, dsh)
        rows = (ends_of(which, x) + parts).astype(BF16)
        rows = rows.transpose(1, 0, 2).reshape(nstep, peers * dsh)
        grad = step_end_grad(rows, w_class, tgt[which], tokens_total)
        grad = grad.reshape(nstep, peers, dsh)
        back = jnp.einsum("sr,sbd->brd", picks[which], grad, preferred_element_type=F32)
        return back.astype(BF16)

    kept = []
    arriving = None
    spans = [jnp.where(section_at == turn, lens[0], lens[1]) for turn in range(nst + 1)]
    for turn in range(nst):
        cur = first(turn) if turn < ntr else jnp.zeros((width, dsh), BF16)
        if turn == 1:
            spans, picks, bnd, tgt, tokens_total, w_class, cur, arriving = together(
                spans, picks, bnd, tgt, tokens_total, w_class, cur, arriving
            )
        if arriving is not None:
            cur = jnp.where(section_at == 0, cur, arriving)
        x = gathered(cur)
        now = forward(spans[turn], x, *weights, True)
        kept.append(now)
        blocks = now["part"]
        if turn == nst - 1:
            blocks = with_ends(blocks, ends_of(0, blocks))
        got = exchange(blocks)
        arriving = (cur.astype(F32) + sum_of(got)).astype(BF16)
        if turn == 0:
            away = [away[0], after(away[1], arriving)]
        arriving = passed_along(arriving, "section", 1)

    taken = {}
    top = jnp.int32(0)
    g_top = end_cotangent(0, got, x)
    grad = lax.dynamic_slice_in_dim(g_top, tensor_at, 1, axis=0)[0]
    d, dx = backward(top, after(g_top, arriving), kept[-1], kept[-1], weights, True)
    taken[nst] = (d, g_top)
    x = gathered(arriving)
    now = forward(spans[nst], x, *weights, False)
    kept.append(now)
    got = exchange(with_ends(dx, ends_of(1, now["part"])))
    g_top = end_cotangent(1, got, x)

    def chosen(choices, n=None):
        if n is None:
            return by_section(section_at, choices)
        size = peers // lax.axis_size("dp")
        cut = lambda x: lax.dynamic_slice_in_dim(x, n * size, size, axis=0)
        return by_section(section_at, [cut(x) for x in choices])

    def not_before(choices, mark):
        return [after(x, mark) for x in choices]

    seen = lambda name, which: [kept[s + which][name] for s in range(nst)]
    back = lambda n, which: [taken[2 * nst - 1 - s + which][n] for s in range(nst)]

    pieces = {}

    def send_quarters(name, choices, masks):
        for k in masks:
            mine = chosen(choices, rep ^ k)
            if k:
                mine = swapped(mine, "dp", k) if k == 1 else mirrored(mine, k)
            pieces[name, k] = mine

    def send_whole(name, choices):
        mine = chosen(choices)
        far = swapped(mine, "dp", 2)
        pieces[name, 0], pieces[name, 2] = mine, far
        pieces[name, 1], pieces[name, 3] = swapped(mine, "dp", 1), swapped(far, "dp", 1)

    def until(x):
        return after(x, *pieces.values())

    qcol = weights[0].shape[1]
    widths = (qcol, HEAD_DIM, HEAD_DIM)
    wide_o = (peers // lax.axis_size("dp") * dsh,)
    of = lambda name: [pieces[name, k] for k in range(4)]
    for turn in range(nst + 1, 2 * nst + 1):
        grad = (grad.astype(F32) + sum_of(got)).astype(BF16)
        which = turn - nst - 1
        if which < ntr:
            send_quarters(("h", which), not_before(seen("h", which), grad), (0, 2))
        elif turn < 2 * nst:
            send_whole(("o", 0), not_before(seen("o", 0), grad))
            send_whole(("o", 1), not_before(seen("o", 1), grad))
        else:
            send_quarters(("g", 0), not_before(back(1, 0), grad), (1, 3))
            send_whole(("d", 0), not_before(back(0, 0), grad))
        grad = passed_along(grad, "section", -1)
        g = until(gathered(grad))
        if turn == nst + 1:
            g = jnp.where(section_at == nst - 1, g_top, g)
            own_top = lax.dynamic_slice_in_dim(g_top, tensor_at, 1, axis=0)[0]
            grad = jnp.where(section_at == nst - 1, own_top, grad)
        late = 2 * nst + 1 - turn
        early = max(late - 2, 0)
        flag = section_at == late - 1
        if turn < 2 * nst:
            d, dx = backward(flag, g, kept[early], kept[late], weights, True)
            taken[turn] = (d, g)
            if which < ntr:
                send_quarters(("h", which), not_before(seen("h", which), dx), (1, 3))
            else:
                send_quarters(("g", 0), not_before(back(1, 0), dx), (0, 2))
            got = until(exchange(dx))
        else:
            taken[turn] = (d, g)
            send_quarters(("g", 1), back(1, 1), range(4))
            (d,) = backward(flag, g, kept[early], kept[late], weights, False)
            taken[turn] = (d, g)
            send_whole(("d", 1), back(0, 1))

    total_qkv = rows_grad(of(("h", 0)), of(("d", 0)), widths)
    total_o = rows_grad(of(("o", 0)), of(("g", 0)), wide_o)
    (grad_o,) = rows_grad(of(("o", 1)), of(("g", 1)), wide_o, total_o)
    grad_q, grad_k, grad_v = rows_grad(of(("h", 1)), of(("d", 1)), widths, total_qkv)
    return (grad_q[None], grad_k[None], grad_v[None], grad_o[None])


def solution(mesh):
    placed = (
        P("dp", None, "tensor"),
        P(),
        P(),
        P(),
        P(),
        P("section", None, "tensor"),
        P("section", None, "tensor"),
        P("section", None, "tensor"),
        P("section", "tensor", None),
        P("tensor", None),
    )
    return jax.shard_map(
        on_device,
        mesh=mesh,
        in_specs=placed,
        out_specs=(
            P("section", "dp", "tensor"),
            P("section", "dp", "tensor"),
            P("section", "dp", "tensor"),
            P("section", "tensor", "dp"),
        ),
        check_vma=False,
    )
```

```python
import functools

import jax
import jax.numpy as jnp
from jax import lax
from jax.experimental import pallas as pl
from jax.experimental.pallas import tpu as pltpu
from jax.sharding import PartitionSpec as P

HEAD_DIM = 128
EPS = 1e-06
LOSS_SCALE = 16384.0
SCORE_SCALE = 1.0 / HEAD_DIM**0.5
F32 = jnp.float32
BF16 = jnp.bfloat16
VMEM_LIMIT = 16 * 1024 * 1024


def dot(a, b):
    return jnp.dot(a, b, preferred_element_type=F32)


def dot_nt(a, b):
    return lax.dot_general(a, b, (((1,), (1,)), ((), ())), preferred_element_type=F32)


def dot_tn(a, b):
    return lax.dot_general(a, b, (((0,), (0,)), ((), ())), preferred_element_type=F32)


def in_vmem():
    return pl.BlockSpec(memory_space=pltpu.VMEM)


def in_smem():
    return pl.BlockSpec(memory_space=pltpu.SMEM)


def anywhere():
    return pl.BlockSpec(memory_space=pl.ANY)


def kernel_params(limit):
    return pltpu.CompilerParams(vmem_limit_bytes=limit)


def place_ends(ends_ref, block, rows, nstep):
    ends_ref[pl.ds(block * nstep, nstep), :] = rows[:nstep]


def forward_kernel(mode, nstep, len_ref, x_ref, wq_ref, wk_ref, wv_ref, wo_ref, *rest):
    if mode == "all":
        part_ref, h_ref, scale_ref, pack_ref, o_ref = rest
    else:
        pick_ref, part_ref, h_ref, scale_ref, pack_ref, o_ref, ends_ref = rest
    nblk, rows, dsh = x_ref.shape
    qh = wq_ref.shape[1] // HEAD_DIM
    sq = jnp.zeros((rows, 1), F32)
    for j in range(nblk):
        xf = x_ref[j].astype(F32)
        sq = sq + jnp.sum(xf * xf, axis=1, keepdims=True)
    scale = lax.rsqrt(sq / (nblk * dsh) + EPS)
    scale_ref[...] = jnp.broadcast_to(scale, scale_ref.shape)
    q = jnp.zeros((rows, wq_ref.shape[1]), F32)
    k = jnp.zeros((rows, HEAD_DIM), F32)
    v = jnp.zeros((rows, HEAD_DIM), F32)
    for j in range(nblk):
        h = (x_ref[j].astype(F32) * scale).astype(BF16)
        h_ref[j] = h
        at = pl.ds(j * dsh, dsh)
        q = q + dot(h, wq_ref[at, :])
        k = k + dot(h, wk_ref[at, :])
        v = v + dot(h, wv_ref[at, :])
    q = q.astype(BF16)
    k = k.astype(BF16)
    v = v.astype(BF16)
    top = qh * rows
    pack_ref[pl.ds(2 * top, rows), :] = k
    pack_ref[pl.ds(2 * top + rows, rows), :] = v
    posq = lax.broadcasted_iota(jnp.int32, (rows, rows), 0)
    posk = lax.broadcasted_iota(jnp.int32, (rows, rows), 1)
    keep = ((posk <= posq) & (posk < len_ref[0])).astype(F32)
    for n in range(qh):
        qn = q[:, n * HEAD_DIM : (n + 1) * HEAD_DIM]
        pack_ref[pl.ds(n * rows, rows), :] = qn
        expo = jnp.exp(dot_nt(qn, k) * SCORE_SCALE) * keep
        weights = (expo / jnp.sum(expo, axis=1, keepdims=True)).astype(BF16)
        pack_ref[pl.ds(top + n * rows, rows), :] = weights
        o_ref[:, pl.ds(n * HEAD_DIM, HEAD_DIM)] = dot(weights, v).astype(BF16)
    o = o_ref[...]
    if mode == "ends":
        o = dot(pick_ref[...], o).astype(BF16)
    for j in range(nblk):
        part = dot(o, wo_ref[:, pl.ds(j * dsh, dsh)])
        if mode == "ends":
            place_ends(ends_ref, j, part, nstep)
            continue
        part_ref[j, :rows] = part.astype(BF16)
        if mode == "both":
            place_ends(ends_ref, j, dot(pick_ref[...], part.astype(BF16)), nstep)
    if mode == "ends":
        part_ref[...] = ends_ref[...].astype(BF16)
    elif mode == "both":
        for j in range(nblk):
            part_ref[j, rows:] = ends_ref[...].astype(BF16)


def forward(length, x, weights, mode="all", pick=None, nstep=0):
    nblk, rows, dsh = x.shape
    qcol = weights[0].shape[1]
    packed = 2 * qcol // HEAD_DIM * rows + 2 * rows
    nend = nblk * nstep
    part = {"all": x.shape, "both": (nblk, rows + nend, dsh), "ends": (nend, dsh)}[mode]
    outs = [(part, BF16), (x.shape, BF16)]
    outs += [((rows, HEAD_DIM), F32), ((packed, HEAD_DIM), BF16), ((rows, qcol), BF16)]
    more = [] if mode == "all" else [pick]
    out = pl.pallas_call(
        functools.partial(forward_kernel, mode, nstep),
        out_shape=tuple(jax.ShapeDtypeStruct(*one) for one in outs),
        in_specs=[in_smem()] + [in_vmem()] * (5 + len(more)),
        out_specs=tuple([in_vmem()] * 5),
        scratch_shapes=[pltpu.VMEM((nend, dsh), F32)] if more else [],
        compiler_params=kernel_params(VMEM_LIMIT),
        cost_estimate=pl.CostEstimate(
            flops=2 * rows * nblk * dsh * (2 * qcol + 2 * HEAD_DIM),
            bytes_accessed=4 * nblk * dsh * (qcol + HEAD_DIM),
            transcendentals=rows * rows * qcol // HEAD_DIM,
        ),
        name="forward_layer",
    )(length, x, *weights, *more)
    return dict(zip(("part", "h", "scale", "pack", "o"), out))


def step_end_kernel(nstep, factor_ref, got_ref, x_ref, pick_ref, class_ref, hot_ref, out_ref, sum_ref, row_ref):
    nblk, rows, dsh = x_ref.shape
    width = nblk * dsh
    nend = nblk * nstep
    parts = jnp.zeros((nend, dsh), F32)
    for j in range(nblk):
        parts = parts + got_ref[j, rows:].astype(F32)
    sum_ref[...] = parts
    npad = pick_ref.shape[0]
    row_ref[...] = jnp.zeros(row_ref.shape, F32)
    zeta = jnp.zeros((npad, class_ref.shape[1]), F32)
    sumsq = jnp.zeros((npad, 1), F32)
    for j in range(nblk):
        row_ref[j, :nstep] = sum_ref[pl.ds(j * nstep, nstep), :]
        full = (dot(pick_ref[...], x_ref[j]) + row_ref[j]).astype(BF16)
        ff = full.astype(F32)
        row_ref[j] = ff
        zeta = zeta + dot(full, class_ref[pl.ds(j * dsh, dsh), :])
        sumsq = sumsq + jnp.sum(ff * ff, axis=1, keepdims=True)
    rstd = lax.rsqrt(sumsq / width + EPS)
    expo = jnp.exp(zeta * rstd)
    prob = expo / jnp.sum(expo, axis=1, keepdims=True)
    dlog = factor_ref[0] * (prob - hot_ref[...])
    dzeta = dlog * rstd
    dmean = jnp.sum(dlog * zeta, axis=1, keepdims=True) * -0.5 * rstd * rstd * rstd
    high = dzeta.astype(BF16)
    mid = (dzeta - high.astype(F32)).astype(BF16)
    low = (dzeta - high.astype(F32) - mid.astype(F32)).astype(BF16)
    for j in range(nblk):
        head = class_ref[pl.ds(j * dsh, dsh), :]
        back = dot_nt(high, head) + (dot_nt(mid, head) + dot_nt(low, head))
        back = (back + dmean * 2.0 * row_ref[j] / width).astype(BF16)
        out_ref[j] = dot_tn(pick_ref[...], back).astype(BF16)


def step_end_grad(factor, got, x, pick, w_class, hot, nstep):
    nblk, rows, dsh = x.shape
    return pl.pallas_call(
        functools.partial(step_end_kernel, nstep),
        out_shape=jax.ShapeDtypeStruct(x.shape, BF16),
        in_specs=[in_smem()] + [in_vmem()] * 5,
        out_specs=in_vmem(),
        scratch_shapes=[
            pltpu.VMEM((nblk * nstep, dsh), F32),
            pltpu.VMEM((nblk, pick.shape[0], dsh), F32),
        ],
        compiler_params=kernel_params(VMEM_LIMIT),
        cost_estimate=pl.CostEstimate(
            flops=16 * rows * nblk * dsh * pick.shape[0], bytes_accessed=4 * rows * nblk * dsh,
            transcendentals=0,
        ),
        name="step_end_grad",
    )(factor, got, x, pick, w_class, hot)


def backward_kernel(
    with_input, with_ends, flag_ref, g_ref, pack0_ref, pack1_ref, h0_ref, h1_ref, scale0_ref, scale1_ref,
    wq_ref, wk_ref, wv_ref, wo_ref, *rest
):
    if with_ends:
        ends_ref, rest = rest[0], rest[1:]
    if with_input:
        d_ref, dx_ref, pack_ref, keep_sems, h_ref, scale_ref, dh_ref = rest
    else:
        d_ref, pack_ref, keep_sems = rest
    nblk, rows, dsh = g_ref.shape
    qcol = wq_ref.shape[1]
    qh = qcol // HEAD_DIM
    top = qh * rows
    pairs = [(pack0_ref, pack1_ref, pack_ref)]
    if with_input:
        pairs += [(h0_ref, h1_ref, h_ref), (scale0_ref, scale1_ref, scale_ref)]
    for at, (one, two, to) in enumerate(pairs):

        @pl.when(flag_ref[0] == 0)
        def _(one=one, to=to, at=at):
            pltpu.make_async_copy(one, to, keep_sems.at[at]).start()

        @pl.when(flag_ref[0] != 0)
        def _(two=two, to=to, at=at):
            pltpu.make_async_copy(two, to, keep_sems.at[at]).start()

    do = jnp.zeros((rows, qcol), F32)
    for j in range(nblk):
        do = do + dot_nt(g_ref[j], wo_ref[:, pl.ds(j * dsh, dsh)])
    do = do.astype(BF16)
    pltpu.make_async_copy(pack0_ref, pack_ref, keep_sems.at[0]).wait()
    k = pack_ref[pl.ds(2 * top, rows), :]
    v = pack_ref[pl.ds(2 * top + rows, rows), :]
    dk = jnp.zeros((rows, HEAD_DIM), F32)
    dv = jnp.zeros((rows, HEAD_DIM), F32)
    for n in range(qh):
        cols = slice(n * HEAD_DIM, (n + 1) * HEAD_DIM)
        qn = pack_ref[pl.ds(n * rows, rows), :]
        weights = pack_ref[pl.ds(top + n * rows, rows), :]
        don = do[:, cols]
        wf = weights.astype(F32)
        dw = dot_nt(don, v)
        ds = wf * (dw - jnp.sum(dw * wf, axis=1, keepdims=True)) * SCORE_SCALE
        ds = ds.astype(BF16)
        d_ref[:, cols] = dot(ds, k).astype(BF16)
        dk = dk + dot_tn(ds, qn)
        dv = dv + dot_tn(weights, don)
    d_ref[:, qcol : qcol + HEAD_DIM] = dk.astype(BF16)
    d_ref[:, qcol + HEAD_DIM :] = dv.astype(BF16)
    if not with_input:
        return
    pltpu.make_async_copy(h0_ref, h_ref, keep_sems.at[1]).wait()
    pltpu.make_async_copy(scale0_ref, scale_ref, keep_sems.at[2]).wait()
    dq = d_ref[:, :qcol]
    dk = dk.astype(BF16)
    dv = dv.astype(BF16)
    inner = jnp.zeros((rows, 1), F32)
    for j in range(nblk):
        at = pl.ds(j * dsh, dsh)
        dh = dot_nt(dq, wq_ref[at, :]) + dot_nt(dk, wk_ref[at, :]) + dot_nt(dv, wv_ref[at, :])
        dh_ref[j] = dh
        inner = inner + jnp.sum(dh * h_ref[j].astype(F32), axis=1, keepdims=True)
    inner = inner / (nblk * dsh)
    scale = scale_ref[:, :1]
    for j in range(nblk):
        dx_ref[j, :rows] = (scale * (dh_ref[j] - h_ref[j].astype(F32) * inner)).astype(BF16)
        if with_ends:
            dx_ref[j, rows:] = ends_ref[...]


def backward(flag, g, one, two, weights, with_input, ends=()):
    nblk, rows, dsh = g.shape
    wq, wk, wv, wo = weights
    qcol = wq.shape[1]
    out_shape = [jax.ShapeDtypeStruct((rows, qcol + 2 * HEAD_DIM), BF16)]
    scratch = [pltpu.VMEM(one["pack"].shape, BF16), pltpu.SemaphoreType.DMA((3,))]
    if with_input:
        below = sum(x.shape[0] for x in ends)
        out_shape.append(jax.ShapeDtypeStruct((nblk, rows + below, dsh), BF16))
        scratch += [
            pltpu.VMEM(g.shape, BF16),
            pltpu.VMEM(one["scale"].shape, F32),
            pltpu.VMEM(g.shape, F32),
        ]
    return pl.pallas_call(
        functools.partial(backward_kernel, with_input, bool(ends)),
        out_shape=tuple(out_shape),
        in_specs=[in_smem(), in_vmem()] + [anywhere()] * 6 + [in_vmem()] * (4 + len(ends)),
        out_specs=tuple([in_vmem()] * len(out_shape)),
        scratch_shapes=scratch,
        compiler_params=kernel_params(VMEM_LIMIT),
        cost_estimate=pl.CostEstimate(
            flops=2 * rows * nblk * dsh * (2 * qcol + 2 * HEAD_DIM),
            bytes_accessed=4 * nblk * dsh * (qcol + HEAD_DIM),
            transcendentals=0,
        ),
        name="backward_layer" if with_input else "backward_heads",
    )(
        flag, g, one["pack"], two["pack"], one["h"], two["h"],
        one["scale"], two["scale"], wq, wk, wv, wo, *ends,
    )


def rows_grad_kernel(n, splits, with_total, *refs):
    a_refs, b_refs, refs = refs[:n], refs[n : 2 * n], refs[2 * n :]
    totals, refs = (refs[: len(splits)], refs[len(splits) :]) if with_total else ((), refs)
    outs, (a_all, b_all) = refs[: len(splits)], refs[len(splits) :]
    rows = a_refs[0].shape[-2]

    def place(to, piece, i):
        at = pl.ds(i * rows, rows)
        if len(piece.shape) == 2:
            to[at, :] = piece[...]
        else:
            for b in range(piece.shape[0]):
                to[at, pl.ds(b * piece.shape[2], piece.shape[2])] = piece[b]

    for i in range(n):
        place(a_all, a_refs[i], i)
        place(b_all, b_refs[i], i)
    for c in range(a_all.shape[1] // 256):
        cols = pl.ds(c * 256, 256)
        got = dot_tn(a_all[:, cols], b_all[...])
        for i, (start, stop) in enumerate(splits):
            part = got[:, start:stop]
            outs[i][cols, :] = totals[i][cols, :] + part if with_total else part


def rows_grad(a, b, widths, totals=()):
    n = len(a)
    wide = lambda x: x.shape[-1] * (x.shape[0] if x.ndim == 3 else 1)
    rows = a[0].shape[-2]
    splits, at = [], 0
    for w in widths:
        splits.append((at, at + w))
        at += w
    return pl.pallas_call(
        functools.partial(rows_grad_kernel, n, splits, bool(totals)),
        out_shape=tuple(jax.ShapeDtypeStruct((wide(a[0]), w), F32) for w in widths),
        in_specs=[in_vmem()] * (2 * n + len(totals)),
        out_specs=tuple([in_vmem()] * len(widths)),
        scratch_shapes=[
            pltpu.VMEM((n * rows, wide(a[0])), BF16),
            pltpu.VMEM((n * rows, wide(b[0])), BF16),
        ],
        compiler_params=kernel_params(VMEM_LIMIT),
        cost_estimate=pl.CostEstimate(
            flops=2 * n * rows * wide(a[0]) * wide(b[0]),
            bytes_accessed=4 * wide(a[0]) * wide(b[0]),
            transcendentals=0,
        ),
        name="weight_grad",
    )(*a, *b, *totals)


def passed_along(x, axis, by):
    peers = lax.axis_size(axis)
    pairs = [(i, i + by) for i in range(peers) if 0 <= i + by < peers]
    return lax.ppermute(x, axis, pairs)


def swapped(x, axis, mask):
    return lax.ppermute(x, axis, [(i, i ^ mask) for i in range(lax.axis_size(axis))])


def mirrored(x, mask):
    ndp, peers = lax.axis_size("dp"), lax.axis_size("tensor")
    to = lambda p, r: (p ^ mask) * peers + (r + peers // 2) % peers
    pairs = [(p * peers + r, to(p, r)) for p in range(ndp) for r in range(peers)]
    return lax.ppermute(x, ("dp", "tensor"), pairs)


def exchange(blocks):
    return lax.all_to_all(blocks, "tensor", split_axis=0, concat_axis=0, tiled=True)


def gathered(cur):
    return exchange(jnp.broadcast_to(cur[None], (lax.axis_size("tensor"),) + cur.shape))


def by_section(masks, choices):
    out = choices[-1]
    for mask, choice in zip(masks, choices[:-1]):
        out = jnp.where(mask, choice, out)
    return out


def after(x, *marks):
    return lax.optimization_barrier((x,) + marks)[0]


def together(*xs):
    return lax.optimization_barrier(xs)


def on_device(embeds, source, lengths, bounds, targets, w_query, w_key, w_value, w_out, w_class):
    nst = lax.axis_size("section")
    peers = lax.axis_size("tensor")
    rep = lax.axis_index("dp")
    section_at = lax.axis_index("section")
    tensor_at = lax.axis_index("tensor")
    ntr, width, dsh = embeds.shape
    weights = (w_query[0], w_key[0], w_value[0], w_out[0])
    w_class = lax.all_gather(w_class, "tensor", axis=0, tiled=True)

    hi, core = rep // 2, rep % 2
    slots = source.reshape(2, 2, ntr) - rep * ntr

    def mine_for(col):
        owner = lax.dynamic_slice_in_dim(slots, col, 1, axis=1)[:, 0]
        out = jnp.zeros((2, ntr, width, dsh), BF16)
        for n in range(ntr):
            out = jnp.where((owner == n)[:, :, None, None], embeds[n][None, None], out)
        return out

    both = mine_for(core) + swapped(mine_for(1 - core), "dp", 1)
    own = lax.dynamic_slice_in_dim(both, hi, 1, axis=0)[0]
    away = lax.dynamic_slice_in_dim(both, 1 - hi, 1, axis=0)[0]
    away = [away[j] for j in range(ntr)]

    def first(j):
        return own[j] + swapped(away[j], "dp", 2)


    wanted = lax.dynamic_slice_in_dim(source, rep * ntr, ntr)
    lens = lengths[wanted]
    bnd = bounds[wanted]
    tgt = targets[wanted]
    nstep = bnd.shape[1]
    factor = (LOSS_SCALE / jnp.sum(lens).astype(F32)).reshape(1)

    def one_hot(ids, size):
        hot = ids[:, None] == jnp.arange(size, dtype=jnp.int32)[None, :]
        return jnp.concatenate([hot, jnp.zeros((16 - nstep, size), bool)], axis=0)

    picks = [one_hot(bnd[j], width).astype(BF16) for j in range(ntr)]
    hots = [one_hot(tgt[j], w_class.shape[1]).astype(F32) for j in range(ntr)]
    spans = [jnp.where(section_at == n, lens[0], lens[1]).reshape(1) for n in range(nst + 1)]
    flags = [(section_at == s).astype(jnp.int32).reshape(1) for s in range(nst)]
    masks = [section_at == s for s in range(nst)]
    quarter = peers // lax.axis_size("dp")
    starts = [((rep ^ k) * quarter).astype(jnp.uint32) for k in range(4)]
    block_at = tensor_at.astype(jnp.uint32)

    def sum_of(got):
        return jnp.sum(got[:, :width].astype(F32), axis=0)

    kept = []
    arriving = None
    for turn in range(nst):
        cur = first(turn) if turn < ntr else jnp.zeros((width, dsh), BF16)
        if turn == 0:
            cur, factor, picks, hots, spans, flags, masks, starts, block_at = together(
                cur, factor, picks, hots, spans, flags, masks, starts, block_at
            )
        if arriving is not None:
            cur, arriving = together(cur, arriving)
            cur = jnp.where(masks[0], cur, arriving)
        x = gathered(cur)
        if turn == nst - 1:
            now = forward(spans[turn], x, weights, "both", picks[0], nstep)
        else:
            now = forward(spans[turn], x, weights)
        kept.append(now)
        blocks = now["part"]
        if turn == 0:
            blocks, w_class = together(blocks, w_class)
        got = exchange(blocks)
        arriving = (cur.astype(F32) + sum_of(got)).astype(BF16)
        if turn == 0:
            away = [away[0], after(away[1], arriving)]
        arriving = passed_along(arriving, "section", 1)

    def end_cotangent(which, got, x):
        return step_end_grad(factor, got, x, picks[which], w_class, hots[which], nstep)

    def own_block(blocks):
        return lax.dynamic_slice_in_dim(blocks, block_at, 1, axis=0)[0]

    taken = {}
    g_top = end_cotangent(0, got, x)
    grad = own_block(g_top)
    arriving, g_top, grad = together(arriving, g_top, grad)
    x = gathered(arriving)
    now = forward(spans[nst], x, weights, "ends", picks[1], nstep)
    d, dx = backward(
        jnp.zeros((1,), jnp.int32), g_top, kept[-1], kept[-1], weights, True, (now["part"],)
    )
    taken[nst] = (d, g_top)
    kept.append(now)
    got = exchange(dx)

    def chosen(choices, k=None):
        if k is None:
            return by_section(masks, choices)
        cut = lambda x: lax.dynamic_slice_in_dim(x, starts[k], quarter, axis=0)
        return by_section(masks, [cut(x) for x in choices])

    def not_before(choices, mark):
        return [after(x, mark) for x in choices]

    seen = lambda name, which: [kept[s + which][name] for s in range(nst)]
    back = lambda n, which: [taken[2 * nst - 1 - s + which][n] for s in range(nst)]

    pieces = {}

    def send_quarter(name, choices, k):
        mine = chosen(choices, k)
        if k:
            mine = swapped(mine, "dp", k) if k == 1 else mirrored(mine, k)
        pieces[name, k] = mine

    def send_whole(name, choices):
        mine = chosen(choices)
        far = swapped(mine, "dp", 2)
        pieces[name, 0], pieces[name, 2] = mine, far
        pieces[name, 1], pieces[name, 3] = swapped(mine, "dp", 1), swapped(far, "dp", 1)

    widths = (weights[0].shape[1], HEAD_DIM, HEAD_DIM)
    wide_o = (quarter * dsh,)
    of = lambda name: [pieces[name, k] for k in range(4)]
    for turn in range(nst + 1, 2 * nst + 1):
        grad = (grad.astype(F32) + sum_of(got)).astype(BF16)
        hs = [not_before(seen("h", w), grad) for w in range(ntr)]
        if turn == nst + 1:
            g_top = end_cotangent(1, got, x)
            send_quarter("h0", hs[0], 2)
        elif turn == nst + 2:
            for name, which, k in (("h0", 0, 3), ("h0", 0, 1), ("h0", 0, 0), ("h1", 1, 2)):
                send_quarter(name, hs[which], k)
        elif turn == nst + 3:
            for k in (3, 1, 0):
                send_quarter("h1", hs[1], k)
            for w in range(ntr):
                send_whole(f"o{w}", not_before(seen("o", w), grad))
        else:
            for k in range(4):
                send_quarter("g0", not_before(back(1, 0), grad), k)
            send_whole("d0", not_before(back(0, 0), grad))
        grad = after(passed_along(grad, "section", -1), *pieces.values())
        if turn == nst + 1:
            grad = jnp.where(masks[nst - 1], own_block(g_top), grad)
        g = gathered(grad)
        late = 2 * nst + 1 - turn
        early = max(late - 2, 0)
        flag = flags[late - 1]
        if turn < 2 * nst:
            d, dx = backward(flag, g, kept[early], kept[late], weights, True)
            taken[turn] = (d, g)
            got = exchange(dx)
        else:
            taken[turn] = (d, g)
            for k in (2, 3, 1, 0):
                send_quarter("g1", back(1, 1), k)
            (d,) = backward(flag, g, kept[early], kept[late], weights, False)
            taken[turn] = (d, g)
            send_whole("d1", back(0, 1))

    total_qkv = rows_grad(of("h0"), of("d0"), widths)
    total_o = rows_grad(of("o0"), of("g0"), wide_o)
    (grad_o,) = rows_grad(of("o1"), of("g1"), wide_o, total_o)
    grad_q, grad_k, grad_v = rows_grad(of("h1"), of("d1"), widths, total_qkv)
    return (grad_q[None], grad_k[None], grad_v[None], grad_o[None])


def solution(mesh):
    placed = (
        P("dp", None, "tensor"),
        P(),
        P(),
        P(),
        P(),
        P("section", None, "tensor"),
        P("section", None, "tensor"),
        P("section", None, "tensor"),
        P("section", "tensor", None),
        P("tensor", None),
    )
    return jax.shard_map(
        on_device,
        mesh=mesh,
        in_specs=placed,
        out_specs=(
            P("section", "dp", "tensor"),
            P("section", "dp", "tensor"),
            P("section", "dp", "tensor"),
            P("section", "tensor", "dp"),
        ),
        check_vma=False,
    )
```

```python
import functools

import jax
import jax.numpy as jnp
from jax import lax
from jax.experimental import pallas as pl
from jax.experimental.pallas import tpu as pltpu
from jax.sharding import PartitionSpec as P

HEAD_DIM = 128
EPS = 1e-06
LOSS_SCALE = 16384.0
SCORE_SCALE = 1.0 / HEAD_DIM**0.5
F32 = jnp.float32
BF16 = jnp.bfloat16
VMEM_LIMIT = 16 * 1024 * 1024


def dot(a, b):
    return jnp.dot(a, b, preferred_element_type=F32)


def dot_nt(a, b):
    return lax.dot_general(a, b, (((1,), (1,)), ((), ())), preferred_element_type=F32)


def dot_tn(a, b):
    return lax.dot_general(a, b, (((0,), (0,)), ((), ())), preferred_element_type=F32)


def in_vmem():
    return pl.BlockSpec(memory_space=pltpu.VMEM)


def in_smem():
    return pl.BlockSpec(memory_space=pltpu.SMEM)


def anywhere():
    return pl.BlockSpec(memory_space=pl.ANY)


def kernel_params(limit):
    return pltpu.CompilerParams(vmem_limit_bytes=limit)


def place_ends(ends_ref, block, rows, nstep):
    ends_ref[pl.ds(block * nstep, nstep), :] = rows[:nstep]


def forward_kernel(mode, nstep, len_ref, x_ref, wq_ref, wk_ref, wv_ref, wo_ref, *rest):
    if mode == "all":
        part_ref, h_ref, scale_ref, pack_ref, o_ref = rest
    else:
        pick_ref, part_ref, h_ref, scale_ref, pack_ref, o_ref, ends_ref = rest
    nblk, rows, dsh = x_ref.shape
    qh = wq_ref.shape[1] // HEAD_DIM
    sq = jnp.zeros((rows, 1), F32)
    for j in range(nblk):
        xf = x_ref[j].astype(F32)
        sq = sq + jnp.sum(xf * xf, axis=1, keepdims=True)
    scale = lax.rsqrt(sq / (nblk * dsh) + EPS)
    scale_ref[...] = jnp.broadcast_to(scale, scale_ref.shape)
    q = jnp.zeros((rows, wq_ref.shape[1]), F32)
    k = jnp.zeros((rows, HEAD_DIM), F32)
    v = jnp.zeros((rows, HEAD_DIM), F32)
    for j in range(nblk):
        h = (x_ref[j].astype(F32) * scale).astype(BF16)
        h_ref[j] = h
        at = pl.ds(j * dsh, dsh)
        q = q + dot(h, wq_ref[at, :])
        k = k + dot(h, wk_ref[at, :])
        v = v + dot(h, wv_ref[at, :])
    q = q.astype(BF16)
    k = k.astype(BF16)
    v = v.astype(BF16)
    top = qh * rows
    pack_ref[pl.ds(2 * top, rows), :] = k
    pack_ref[pl.ds(2 * top + rows, rows), :] = v
    posq = lax.broadcasted_iota(jnp.int32, (rows, rows), 0)
    posk = lax.broadcasted_iota(jnp.int32, (rows, rows), 1)
    keep = ((posk <= posq) & (posk < len_ref[0])).astype(F32)
    for n in range(qh):
        qn = q[:, n * HEAD_DIM : (n + 1) * HEAD_DIM]
        pack_ref[pl.ds(n * rows, rows), :] = qn
        expo = jnp.exp(dot_nt(qn, k) * SCORE_SCALE) * keep
        weights = (expo / jnp.sum(expo, axis=1, keepdims=True)).astype(BF16)
        pack_ref[pl.ds(top + n * rows, rows), :] = weights
        o_ref[:, pl.ds(n * HEAD_DIM, HEAD_DIM)] = dot(weights, v).astype(BF16)
    o = o_ref[...]
    if mode == "ends":
        o = dot(pick_ref[...], o).astype(BF16)
    for j in range(nblk):
        part = dot(o, wo_ref[:, pl.ds(j * dsh, dsh)])
        if mode == "ends":
            place_ends(ends_ref, j, part, nstep)
            continue
        part_ref[j, :rows] = part.astype(BF16)
        if mode == "both":
            place_ends(ends_ref, j, dot(pick_ref[...], part.astype(BF16)), nstep)
    if mode == "ends":
        part_ref[...] = ends_ref[...].astype(BF16)
    elif mode == "both":
        for j in range(nblk):
            part_ref[j, rows:] = ends_ref[...].astype(BF16)


def forward(length, x, weights, mode="all", pick=None, nstep=0):
    nblk, rows, dsh = x.shape
    qcol = weights[0].shape[1]
    packed = 2 * qcol // HEAD_DIM * rows + 2 * rows
    nend = nblk * nstep
    part = {"all": x.shape, "both": (nblk, rows + nend, dsh), "ends": (nend, dsh)}[mode]
    outs = [(part, BF16), (x.shape, BF16)]
    outs += [((rows, HEAD_DIM), F32), ((packed, HEAD_DIM), BF16), ((rows, qcol), BF16)]
    more = [] if mode == "all" else [pick]
    out = pl.pallas_call(
        functools.partial(forward_kernel, mode, nstep),
        out_shape=tuple(jax.ShapeDtypeStruct(*one) for one in outs),
        in_specs=[in_smem()] + [in_vmem()] * (5 + len(more)),
        out_specs=tuple([in_vmem()] * 5),
        scratch_shapes=[pltpu.VMEM((nend, dsh), F32)] if more else [],
        compiler_params=kernel_params(VMEM_LIMIT),
        cost_estimate=pl.CostEstimate(
            flops=2 * rows * nblk * dsh * (2 * qcol + 2 * HEAD_DIM),
            bytes_accessed=4 * nblk * dsh * (qcol + HEAD_DIM),
            transcendentals=rows * rows * qcol // HEAD_DIM,
        ),
        name="forward_layer",
    )(length, x, *weights, *more)
    return dict(zip(("part", "h", "scale", "pack", "o"), out))


def step_end_kernel(nstep, factor_ref, got_ref, x_ref, pick_ref, class_ref, hot_ref, out_ref, sum_ref, row_ref):
    nblk, rows, dsh = x_ref.shape
    width = nblk * dsh
    nend = nblk * nstep
    parts = jnp.zeros((nend, dsh), F32)
    for j in range(nblk):
        parts = parts + got_ref[j, rows:].astype(F32)
    sum_ref[...] = parts
    npad = pick_ref.shape[0]
    row_ref[...] = jnp.zeros(row_ref.shape, F32)
    zeta = jnp.zeros((npad, class_ref.shape[1]), F32)
    sumsq = jnp.zeros((npad, 1), F32)
    for j in range(nblk):
        row_ref[j, :nstep] = sum_ref[pl.ds(j * nstep, nstep), :]
        full = (dot(pick_ref[...], x_ref[j]) + row_ref[j]).astype(BF16)
        ff = full.astype(F32)
        row_ref[j] = ff
        zeta = zeta + dot(full, class_ref[pl.ds(j * dsh, dsh), :])
        sumsq = sumsq + jnp.sum(ff * ff, axis=1, keepdims=True)
    rstd = lax.rsqrt(sumsq / width + EPS)
    expo = jnp.exp(zeta * rstd)
    prob = expo / jnp.sum(expo, axis=1, keepdims=True)
    dlog = factor_ref[0] * (prob - hot_ref[...])
    dzeta = dlog * rstd
    dmean = jnp.sum(dlog * zeta, axis=1, keepdims=True) * -0.5 * rstd * rstd * rstd
    high = dzeta.astype(BF16)
    mid = (dzeta - high.astype(F32)).astype(BF16)
    low = (dzeta - high.astype(F32) - mid.astype(F32)).astype(BF16)
    for j in range(nblk):
        head = class_ref[pl.ds(j * dsh, dsh), :]
        back = dot_nt(high, head) + (dot_nt(mid, head) + dot_nt(low, head))
        back = (back + dmean * 2.0 * row_ref[j] / width).astype(BF16)
        out_ref[j] = dot_tn(pick_ref[...], back).astype(BF16)


def step_end_grad(factor, got, x, pick, w_class, hot, nstep):
    nblk, rows, dsh = x.shape
    return pl.pallas_call(
        functools.partial(step_end_kernel, nstep),
        out_shape=jax.ShapeDtypeStruct(x.shape, BF16),
        in_specs=[in_smem()] + [in_vmem()] * 5,
        out_specs=in_vmem(),
        scratch_shapes=[
            pltpu.VMEM((nblk * nstep, dsh), F32),
            pltpu.VMEM((nblk, pick.shape[0], dsh), F32),
        ],
        compiler_params=kernel_params(VMEM_LIMIT),
        cost_estimate=pl.CostEstimate(
            flops=16 * rows * nblk * dsh * pick.shape[0], bytes_accessed=4 * rows * nblk * dsh,
            transcendentals=0,
        ),
        name="step_end_grad",
    )(factor, got, x, pick, w_class, hot)


def backward_kernel(
    with_input, with_ends, flag_ref, g_ref, pack0_ref, pack1_ref, h0_ref, h1_ref, scale0_ref, scale1_ref,
    wq_ref, wk_ref, wv_ref, wo_ref, *rest
):
    if with_ends:
        ends_ref, rest = rest[0], rest[1:]
    if with_input:
        d_ref, dx_ref, pack_ref, keep_sems, h_ref, scale_ref, dh_ref = rest
    else:
        d_ref, pack_ref, keep_sems = rest
    nblk, rows, dsh = g_ref.shape
    qcol = wq_ref.shape[1]
    qh = qcol // HEAD_DIM
    top = qh * rows
    pairs = [(pack0_ref, pack1_ref, pack_ref)]
    if with_input:
        pairs += [(h0_ref, h1_ref, h_ref), (scale0_ref, scale1_ref, scale_ref)]
    for at, (one, two, to) in enumerate(pairs):

        @pl.when(flag_ref[0] == 0)
        def _(one=one, to=to, at=at):
            pltpu.make_async_copy(one, to, keep_sems.at[at]).start()

        @pl.when(flag_ref[0] != 0)
        def _(two=two, to=to, at=at):
            pltpu.make_async_copy(two, to, keep_sems.at[at]).start()

    do = jnp.zeros((rows, qcol), F32)
    for j in range(nblk):
        do = do + dot_nt(g_ref[j], wo_ref[:, pl.ds(j * dsh, dsh)])
    do = do.astype(BF16)
    pltpu.make_async_copy(pack0_ref, pack_ref, keep_sems.at[0]).wait()
    k = pack_ref[pl.ds(2 * top, rows), :]
    v = pack_ref[pl.ds(2 * top + rows, rows), :]
    dk = jnp.zeros((rows, HEAD_DIM), F32)
    dv = jnp.zeros((rows, HEAD_DIM), F32)
    for n in range(qh):
        cols = slice(n * HEAD_DIM, (n + 1) * HEAD_DIM)
        qn = pack_ref[pl.ds(n * rows, rows), :]
        weights = pack_ref[pl.ds(top + n * rows, rows), :]
        don = do[:, cols]
        wf = weights.astype(F32)
        dw = dot_nt(don, v)
        ds = wf * (dw - jnp.sum(dw * wf, axis=1, keepdims=True)) * SCORE_SCALE
        ds = ds.astype(BF16)
        d_ref[:, cols] = dot(ds, k).astype(BF16)
        dk = dk + dot_tn(ds, qn)
        dv = dv + dot_tn(weights, don)
    d_ref[:, qcol : qcol + HEAD_DIM] = dk.astype(BF16)
    d_ref[:, qcol + HEAD_DIM :] = dv.astype(BF16)
    if not with_input:
        return
    pltpu.make_async_copy(h0_ref, h_ref, keep_sems.at[1]).wait()
    pltpu.make_async_copy(scale0_ref, scale_ref, keep_sems.at[2]).wait()
    dq = d_ref[:, :qcol]
    dk = dk.astype(BF16)
    dv = dv.astype(BF16)
    inner = jnp.zeros((rows, 1), F32)
    for j in range(nblk):
        at = pl.ds(j * dsh, dsh)
        dh = dot_nt(dq, wq_ref[at, :]) + dot_nt(dk, wk_ref[at, :]) + dot_nt(dv, wv_ref[at, :])
        dh_ref[j] = dh
        inner = inner + jnp.sum(dh * h_ref[j].astype(F32), axis=1, keepdims=True)
    inner = inner / (nblk * dsh)
    scale = scale_ref[:, :1]
    for j in range(nblk):
        dx_ref[j, :rows] = (scale * (dh_ref[j] - h_ref[j].astype(F32) * inner)).astype(BF16)
        if with_ends:
            dx_ref[j, rows:] = ends_ref[...]


def backward(flag, g, one, two, weights, with_input, ends=()):
    nblk, rows, dsh = g.shape
    wq, wk, wv, wo = weights
    qcol = wq.shape[1]
    out_shape = [jax.ShapeDtypeStruct((rows, qcol + 2 * HEAD_DIM), BF16)]
    scratch = [pltpu.VMEM(one["pack"].shape, BF16), pltpu.SemaphoreType.DMA((3,))]
    if with_input:
        below = sum(x.shape[0] for x in ends)
        out_shape.append(jax.ShapeDtypeStruct((nblk, rows + below, dsh), BF16))
        scratch += [
            pltpu.VMEM(g.shape, BF16),
            pltpu.VMEM(one["scale"].shape, F32),
            pltpu.VMEM(g.shape, F32),
        ]
    return pl.pallas_call(
        functools.partial(backward_kernel, with_input, bool(ends)),
        out_shape=tuple(out_shape),
        in_specs=[in_smem(), in_vmem()] + [anywhere()] * 6 + [in_vmem()] * (4 + len(ends)),
        out_specs=tuple([in_vmem()] * len(out_shape)),
        scratch_shapes=scratch,
        compiler_params=kernel_params(VMEM_LIMIT),
        cost_estimate=pl.CostEstimate(
            flops=2 * rows * nblk * dsh * (2 * qcol + 2 * HEAD_DIM),
            bytes_accessed=4 * nblk * dsh * (qcol + HEAD_DIM),
            transcendentals=0,
        ),
        name="backward_layer" if with_input else "backward_heads",
    )(
        flag, g, one["pack"], two["pack"], one["h"], two["h"],
        one["scale"], two["scale"], wq, wk, wv, wo, *ends,
    )


def gather_rows(to, pieces):
    per = to.shape[2] // pieces[0][0].shape[2]
    for i, run in enumerate(pieces):
        at = 0
        for piece in run:
            nblk, rows, dsh = piece.shape
            for b in range(nblk):
                cols = pl.ds((at + b) % per * dsh, dsh)
                to[(at + b) // per, pl.ds(i * rows, rows), cols] = piece[b]
            at += nblk


def weight_grad_kernel(wide_first, runs, core_ref, *refs):
    nwide = sum(runs)
    wides, narrows, (mine_ref, give_ref, wide_all, narrow_all) = refs[:nwide], refs[nwide:-4], refs[-4:]
    pieces, at = [], 0
    for n in runs:
        pieces.append(wides[at : at + n])
        at += n
    gather_rows(wide_all, pieces)
    rows = narrows[0].shape[0]
    for i, piece in enumerate(narrows):
        narrow_all[pl.ds(i * rows, rows), :] = piece[...]
    core = core_ref[0]
    for out_ref, quarter in ((give_ref, 1 - core), (mine_ref, core)):
        for c in range(out_ref.shape[0] // 256):
            cols = pl.ds(c * 256, 256)
            if wide_first:
                got = dot_tn(wide_all[quarter, :, cols], narrow_all[...])
            else:
                got = dot_tn(narrow_all[:, cols], wide_all[quarter])
            out_ref[cols, :] = got.astype(out_ref.dtype)


def weight_grad(core, wide, narrow, wide_first):
    rows, cols = narrow[0].shape
    dsh = wide[0][0].shape[2]
    width = sum(x.shape[0] for x in wide[0]) * dsh // 2
    shape = (width, cols) if wide_first else (cols, width)
    total = len(narrow) * rows
    flat = [x for run in wide for x in run]
    return pl.pallas_call(
        functools.partial(weight_grad_kernel, wide_first, tuple(len(run) for run in wide)),
        out_shape=(jax.ShapeDtypeStruct(shape, F32), jax.ShapeDtypeStruct(shape, BF16)),
        in_specs=[in_smem()] + [in_vmem()] * (len(flat) + len(narrow)),
        out_specs=(in_vmem(), in_vmem()),
        scratch_shapes=[pltpu.VMEM((2, total, width), BF16), pltpu.VMEM((total, cols), BF16)],
        compiler_params=kernel_params(VMEM_LIMIT),
        cost_estimate=pl.CostEstimate(
            flops=4 * total * width * cols, bytes_accessed=6 * width * cols, transcendentals=0
        ),
        name="weight_grad",
    )(core, *flat, *narrow)


def passed_along(x, axis, by):
    peers = lax.axis_size(axis)
    pairs = [(i, i + by) for i in range(peers) if 0 <= i + by < peers]
    return lax.ppermute(x, axis, pairs)


def swapped(x, axis, mask):
    return lax.ppermute(x, axis, [(i, i ^ mask) for i in range(lax.axis_size(axis))])


def mirrored(x, mask):
    ndp, peers = lax.axis_size("dp"), lax.axis_size("tensor")
    to = lambda p, r: (p ^ mask) * peers + (r + peers // 2) % peers
    pairs = [(p * peers + r, to(p, r)) for p in range(ndp) for r in range(peers)]
    return lax.ppermute(x, ("dp", "tensor"), pairs)


def exchange(blocks):
    return lax.all_to_all(blocks, "tensor", split_axis=0, concat_axis=0, tiled=True)


def gathered(cur):
    return exchange(jnp.broadcast_to(cur[None], (lax.axis_size("tensor"),) + cur.shape))


def by_section(masks, choices):
    out = choices[-1]
    for mask, choice in zip(masks, choices[:-1]):
        out = jnp.where(mask, choice, out)
    return out


def after(x, *marks):
    return lax.optimization_barrier((x,) + marks)[0]


def together(*xs):
    return lax.optimization_barrier(xs)


def on_device(embeds, source, lengths, bounds, targets, w_query, w_key, w_value, w_out, w_class):
    nst = lax.axis_size("section")
    peers = lax.axis_size("tensor")
    rep = lax.axis_index("dp")
    section_at = lax.axis_index("section")
    tensor_at = lax.axis_index("tensor")
    ntr, width, dsh = embeds.shape
    weights = (w_query[0], w_key[0], w_value[0], w_out[0])
    w_class = lax.all_gather(w_class, "tensor", axis=0, tiled=True)

    hi, core = rep // 2, rep % 2
    slots = source.reshape(2, 2, ntr) - rep * ntr

    def mine_for(col):
        owner = lax.dynamic_slice_in_dim(slots, col, 1, axis=1)[:, 0]
        out = jnp.zeros((2, ntr, width, dsh), BF16)
        for n in range(ntr):
            out = jnp.where((owner == n)[:, :, None, None], embeds[n][None, None], out)
        return out

    both = mine_for(core) + swapped(mine_for(1 - core), "dp", 1)
    own = lax.dynamic_slice_in_dim(both, hi, 1, axis=0)[0]
    away = lax.dynamic_slice_in_dim(both, 1 - hi, 1, axis=0)[0]
    away = [away[j] for j in range(ntr)]
    source, lengths, bounds, targets, away[0] = together(source, lengths, bounds, targets, away[0])

    def first(j):
        return own[j] + swapped(away[j], "dp", 2)


    wanted = lax.dynamic_slice_in_dim(source, rep * ntr, ntr)
    lens = lengths[wanted]
    bnd = bounds[wanted]
    tgt = targets[wanted]
    nstep = bnd.shape[1]
    factor = (LOSS_SCALE / jnp.sum(lens).astype(F32)).reshape(1)

    def one_hot(ids, size):
        hot = ids[:, None] == jnp.arange(size, dtype=jnp.int32)[None, :]
        return jnp.concatenate([hot, jnp.zeros((16 - nstep, size), bool)], axis=0)

    picks = [one_hot(bnd[j], width).astype(BF16) for j in range(ntr)]
    hots = [one_hot(tgt[j], w_class.shape[1]).astype(F32) for j in range(ntr)]
    spans = [jnp.where(section_at == n, lens[0], lens[1]).reshape(1) for n in range(nst + 1)]
    flags = [(section_at == s).astype(jnp.int32).reshape(1) for s in range(nst)]
    masks = [section_at == s for s in range(nst)]
    half = peers // 2
    mine_at = (hi * half).astype(jnp.uint32)
    away_at = [((1 - hi) * half + n * half // 2).astype(jnp.uint32) for n in range(2)]
    block_at = tensor_at.astype(jnp.uint32)
    core = core.astype(jnp.int32).reshape(1)

    def sum_of(got):
        return jnp.sum(got[:, :width].astype(F32), axis=0)

    kept = []
    arriving = None
    for turn in range(nst):
        cur = first(turn) if turn < ntr else jnp.zeros((width, dsh), BF16)
        if turn == 0:
            cur, factor, picks, hots, spans, flags, masks, mine_at, away_at, block_at, core = together(
                cur, factor, picks, hots, spans, flags, masks, mine_at, away_at, block_at, core
            )
        if arriving is not None:
            cur, arriving = together(cur, arriving)
            cur = jnp.where(masks[0], cur, arriving)
        x = gathered(cur)
        if turn == nst - 1:
            now = forward(spans[turn], x, weights, "both", picks[0], nstep)
        else:
            now = forward(spans[turn], x, weights)
        kept.append(now)
        blocks = now["part"]
        if turn == 0:
            blocks, w_class = together(blocks, w_class)
        got = exchange(blocks)
        arriving = (cur.astype(F32) + sum_of(got)).astype(BF16)
        if turn == 0:
            away = [away[0], after(away[1], arriving)]
        leaving = arriving
        arriving = passed_along(arriving, "section", 1)

    def end_cotangent(which, got, x):
        return step_end_grad(factor, got, x, picks[which], w_class, hots[which], nstep)

    def own_block(blocks):
        return lax.dynamic_slice_in_dim(blocks, block_at, 1, axis=0)[0]

    def chosen(choices, at=None, count=None):
        if at is None:
            return by_section(masks, choices)
        return by_section(
            masks, [lax.dynamic_slice_in_dim(x, at, count, axis=0) for x in choices]
        )

    def not_before(choices, mark):
        return [after(x, mark) for x in choices]

    seen = lambda name, which: [kept[s + which][name] for s in range(nst)]
    back = lambda n, which: [taken[2 * nst - 1 - s + which][n] for s in range(nst)]

    pieces = {}

    def send_blocks(name, choices, n):
        pieces[f"{name}.{n}"] = mirrored(chosen(choices, away_at[n], half // 2), 2)

    def send_whole(name, choices):
        pieces[name] = swapped(chosen(choices), "dp", 2)

    taken = {}
    g_top = end_cotangent(0, got, x)
    grad = own_block(g_top)
    send_blocks("h0", not_before(seen("h", 0), leaving), 0)
    arriving, g_top, grad, pieces = together(arriving, g_top, grad, pieces)
    x = gathered(arriving)
    now = forward(spans[nst], x, weights, "ends", picks[1], nstep)
    d, dx = backward(
        jnp.zeros((1,), jnp.int32), g_top, kept[-1], kept[-1], weights, True, (now["part"],)
    )
    taken[nst] = (d, g_top)
    kept.append(now)
    got = exchange(dx)

    for turn in range(nst + 1, 2 * nst + 1):
        grad = (grad.astype(F32) + sum_of(got)).astype(BF16)
        hs = [not_before(seen("h", w), grad) for w in range(ntr)]
        if turn == nst + 1:
            g_top = end_cotangent(1, got, x)
            send_blocks("h0", hs[0], 1)
        elif turn < 2 * nst:
            n = turn - nst - 2
            send_blocks("h1", hs[1], n)
            send_whole(f"o{n}", not_before(seen("o", n), grad))
        else:
            for n in range(2):
                send_blocks("g0", not_before(back(1, 0), grad), n)
            send_whole("d0", not_before(back(0, 0), grad))
        grad, pieces = together(passed_along(grad, "section", -1), pieces)
        if turn == nst + 1:
            grad = jnp.where(masks[nst - 1], own_block(g_top), grad)
        g = gathered(grad)
        late = 2 * nst + 1 - turn
        early = max(late - 2, 0)
        flag = flags[late - 1]
        if turn < 2 * nst:
            d, dx = backward(flag, g, kept[early], kept[late], weights, True)
            taken[turn] = (d, g)
            got = exchange(dx)
        else:
            taken[turn] = (None, g)
            for n in range(2):
                send_blocks("g1", back(1, 1), n)
            (d,) = backward(flag, g, kept[early], kept[late], weights, False)
            taken[turn] = (d, g)
            send_whole("d1", back(0, 1))

    def wide(name, choices):
        runs = []
        for w in range(ntr):
            runs.append((chosen(not_before(choices(w), g), mine_at, half),))
            runs.append((pieces[f"{name}{w}.0"], pieces[f"{name}{w}.1"]))
        return runs

    def narrow(name, choices):
        out = []
        for w in range(ntr):
            out += [chosen(not_before(choices(w), g)), pieces[f"{name}{w}"]]
        return out

    mine_o, give_o = weight_grad(
        core, wide("g", lambda w: back(1, w)), narrow("o", lambda w: seen("o", w)), False
    )
    mine_d, give_d = weight_grad(
        core, wide("h", lambda w: seen("h", w)), narrow("d", lambda w: back(0, w)), True
    )
    grad_o = mine_o + swapped(give_o, "dp", 1).astype(F32)
    grad_d = mine_d + swapped(give_d, "dp", 1).astype(F32)
    qcol = weights[0].shape[1]
    grad_q, grad_k, grad_v = jnp.split(grad_d, (qcol, qcol + HEAD_DIM), axis=1)
    return (grad_q[None], grad_k[None], grad_v[None], grad_o[None])


def solution(mesh):
    placed = (
        P("dp", None, "tensor"),
        P(),
        P(),
        P(),
        P(),
        P("section", None, "tensor"),
        P("section", None, "tensor"),
        P("section", None, "tensor"),
        P("section", "tensor", None),
        P("tensor", None),
    )
    return jax.shard_map(
        on_device,
        mesh=mesh,
        in_specs=placed,
        out_specs=(
            P("section", "dp", "tensor"),
            P("section", "dp", "tensor"),
            P("section", "dp", "tensor"),
            P("section", "tensor", "dp"),
        ),
        check_vma=False,
    )
```

```python
import functools

import jax
import jax.numpy as jnp
from jax import lax
from jax.experimental import pallas as pl
from jax.experimental.pallas import tpu as pltpu
from jax.sharding import PartitionSpec as P

HEAD_DIM = 128
EPS = 1e-06
LOSS_SCALE = 16384.0
SCORE_SCALE = 1.0 / HEAD_DIM**0.5
F32 = jnp.float32
BF16 = jnp.bfloat16
VMEM_LIMIT = 16 * 1024 * 1024


def dot(a, b):
    return jnp.dot(a, b, preferred_element_type=F32)


def dot_nt(a, b):
    return lax.dot_general(a, b, (((1,), (1,)), ((), ())), preferred_element_type=F32)


def dot_tn(a, b):
    return lax.dot_general(a, b, (((0,), (0,)), ((), ())), preferred_element_type=F32)


def in_vmem():
    return pl.BlockSpec(memory_space=pltpu.VMEM)


def in_smem():
    return pl.BlockSpec(memory_space=pltpu.SMEM)


def anywhere():
    return pl.BlockSpec(memory_space=pl.ANY)


def kernel_params(limit):
    return pltpu.CompilerParams(vmem_limit_bytes=limit)


def place_ends(ends_ref, block, rows, nstep):
    ends_ref[pl.ds(block * nstep, nstep), :] = rows[:nstep]


def forward_kernel(mode, nstep, len_ref, x_ref, wq_ref, wk_ref, wv_ref, wo_ref, *rest):
    if mode == "all":
        part_ref, h_ref, scale_ref, pack_ref, o_ref = rest
    else:
        pick_ref, part_ref, h_ref, scale_ref, pack_ref, o_ref, ends_ref = rest
    nblk, rows, dsh = x_ref.shape
    qh = wq_ref.shape[1] // HEAD_DIM
    sq = jnp.zeros((rows, 1), F32)
    for j in range(nblk):
        xf = x_ref[j].astype(F32)
        sq = sq + jnp.sum(xf * xf, axis=1, keepdims=True)
    scale = lax.rsqrt(sq / (nblk * dsh) + EPS)
    scale_ref[...] = jnp.broadcast_to(scale, scale_ref.shape)
    q = jnp.zeros((rows, wq_ref.shape[1]), F32)
    k = jnp.zeros((rows, HEAD_DIM), F32)
    v = jnp.zeros((rows, HEAD_DIM), F32)
    for j in range(nblk):
        h = (x_ref[j].astype(F32) * scale).astype(BF16)
        h_ref[j] = h
        at = pl.ds(j * dsh, dsh)
        q = q + dot(h, wq_ref[at, :])
        k = k + dot(h, wk_ref[at, :])
        v = v + dot(h, wv_ref[at, :])
    q = q.astype(BF16)
    k = k.astype(BF16)
    v = v.astype(BF16)
    top = qh * rows
    pack_ref[pl.ds(2 * top, rows), :] = k
    pack_ref[pl.ds(2 * top + rows, rows), :] = v
    posq = lax.broadcasted_iota(jnp.int32, (rows, rows), 0)
    posk = lax.broadcasted_iota(jnp.int32, (rows, rows), 1)
    keep = ((posk <= posq) & (posk < len_ref[0])).astype(F32)
    for n in range(qh):
        qn = q[:, n * HEAD_DIM : (n + 1) * HEAD_DIM]
        pack_ref[pl.ds(n * rows, rows), :] = qn
        expo = jnp.exp(dot_nt(qn, k) * SCORE_SCALE) * keep
        weights = (expo / jnp.sum(expo, axis=1, keepdims=True)).astype(BF16)
        pack_ref[pl.ds(top + n * rows, rows), :] = weights
        o_ref[:, pl.ds(n * HEAD_DIM, HEAD_DIM)] = dot(weights, v).astype(BF16)
    o = o_ref[...]
    if mode == "ends":
        o = dot(pick_ref[...], o).astype(BF16)
    for j in range(nblk):
        part = dot(o, wo_ref[:, pl.ds(j * dsh, dsh)])
        if mode == "ends":
            place_ends(ends_ref, j, part, nstep)
            continue
        part_ref[j, :rows] = part.astype(BF16)
        if mode == "both":
            place_ends(ends_ref, j, dot(pick_ref[...], part.astype(BF16)), nstep)
    if mode == "ends":
        part_ref[...] = ends_ref[...].astype(BF16)
    elif mode == "both":
        for j in range(nblk):
            part_ref[j, rows:] = ends_ref[...].astype(BF16)


def forward(length, x, weights, mode="all", pick=None, nstep=0):
    nblk, rows, dsh = x.shape
    qcol = weights[0].shape[1]
    packed = 2 * qcol // HEAD_DIM * rows + 2 * rows
    nend = nblk * nstep
    part = {"all": x.shape, "both": (nblk, rows + nend, dsh), "ends": (nend, dsh)}[mode]
    outs = [(part, BF16), (x.shape, BF16)]
    outs += [((rows, HEAD_DIM), F32), ((packed, HEAD_DIM), BF16), ((rows, qcol), BF16)]
    more = [] if mode == "all" else [pick]
    out = pl.pallas_call(
        functools.partial(forward_kernel, mode, nstep),
        out_shape=tuple(jax.ShapeDtypeStruct(*one) for one in outs),
        in_specs=[in_smem()] + [in_vmem()] * (5 + len(more)),
        out_specs=tuple([in_vmem()] * 5),
        scratch_shapes=[pltpu.VMEM((nend, dsh), F32)] if more else [],
        compiler_params=kernel_params(VMEM_LIMIT),
        cost_estimate=pl.CostEstimate(
            flops=2 * rows * nblk * dsh * (2 * qcol + 2 * HEAD_DIM),
            bytes_accessed=4 * nblk * dsh * (qcol + HEAD_DIM),
            transcendentals=rows * rows * qcol // HEAD_DIM,
        ),
        name="forward_layer",
    )(length, x, *weights, *more)
    return dict(zip(("part", "h", "scale", "pack", "o"), out))


def step_end_kernel(nstep, factor_ref, got_ref, x_ref, pick_ref, class_ref, hot_ref, out_ref, sum_ref, row_ref):
    nblk, rows, dsh = x_ref.shape
    width = nblk * dsh
    nend = nblk * nstep
    parts = jnp.zeros((nend, dsh), F32)
    for j in range(nblk):
        parts = parts + got_ref[j, rows:].astype(F32)
    sum_ref[...] = parts
    npad = pick_ref.shape[0]
    row_ref[...] = jnp.zeros(row_ref.shape, F32)
    zeta = jnp.zeros((npad, class_ref.shape[1]), F32)
    sumsq = jnp.zeros((npad, 1), F32)
    for j in range(nblk):
        row_ref[j, :nstep] = sum_ref[pl.ds(j * nstep, nstep), :]
        full = (dot(pick_ref[...], x_ref[j]) + row_ref[j]).astype(BF16)
        ff = full.astype(F32)
        row_ref[j] = ff
        zeta = zeta + dot(full, class_ref[pl.ds(j * dsh, dsh), :])
        sumsq = sumsq + jnp.sum(ff * ff, axis=1, keepdims=True)
    rstd = lax.rsqrt(sumsq / width + EPS)
    expo = jnp.exp(zeta * rstd)
    prob = expo / jnp.sum(expo, axis=1, keepdims=True)
    dlog = factor_ref[0] * (prob - hot_ref[...])
    dzeta = dlog * rstd
    dmean = jnp.sum(dlog * zeta, axis=1, keepdims=True) * -0.5 * rstd * rstd * rstd
    high = dzeta.astype(BF16)
    mid = (dzeta - high.astype(F32)).astype(BF16)
    low = (dzeta - high.astype(F32) - mid.astype(F32)).astype(BF16)
    for j in range(nblk):
        head = class_ref[pl.ds(j * dsh, dsh), :]
        back = dot_nt(high, head) + (dot_nt(mid, head) + dot_nt(low, head))
        back = (back + dmean * 2.0 * row_ref[j] / width).astype(BF16)
        out_ref[j] = dot_tn(pick_ref[...], back).astype(BF16)


def step_end_grad(factor, got, x, pick, w_class, hot, nstep):
    nblk, rows, dsh = x.shape
    return pl.pallas_call(
        functools.partial(step_end_kernel, nstep),
        out_shape=jax.ShapeDtypeStruct(x.shape, BF16),
        in_specs=[in_smem()] + [in_vmem()] * 5,
        out_specs=in_vmem(),
        scratch_shapes=[
            pltpu.VMEM((nblk * nstep, dsh), F32),
            pltpu.VMEM((nblk, pick.shape[0], dsh), F32),
        ],
        compiler_params=kernel_params(VMEM_LIMIT),
        cost_estimate=pl.CostEstimate(
            flops=16 * rows * nblk * dsh * pick.shape[0], bytes_accessed=4 * rows * nblk * dsh,
            transcendentals=0,
        ),
        name="step_end_grad",
    )(factor, got, x, pick, w_class, hot)


def backward_kernel(
    with_input, with_ends, flag_ref, g_ref, pack0_ref, pack1_ref, h0_ref, h1_ref, scale0_ref, scale1_ref,
    wq_ref, wk_ref, wv_ref, wo_ref, *rest
):
    if with_ends:
        ends_ref, rest = rest[0], rest[1:]
    if with_input:
        d_ref, dx_ref, pack_ref, keep_sems, h_ref, scale_ref, dh_ref = rest
    else:
        d_ref, pack_ref, keep_sems = rest
    nblk, rows, dsh = g_ref.shape
    qcol = wq_ref.shape[1]
    qh = qcol // HEAD_DIM
    top = qh * rows
    pairs = [(pack0_ref, pack1_ref, pack_ref)]
    if with_input:
        pairs += [(h0_ref, h1_ref, h_ref), (scale0_ref, scale1_ref, scale_ref)]
    for at, (one, two, to) in enumerate(pairs):

        @pl.when(flag_ref[0] == 0)
        def _(one=one, to=to, at=at):
            pltpu.make_async_copy(one, to, keep_sems.at[at]).start()

        @pl.when(flag_ref[0] != 0)
        def _(two=two, to=to, at=at):
            pltpu.make_async_copy(two, to, keep_sems.at[at]).start()

    do = jnp.zeros((rows, qcol), F32)
    for j in range(nblk):
        do = do + dot_nt(g_ref[j], wo_ref[:, pl.ds(j * dsh, dsh)])
    do = do.astype(BF16)
    pltpu.make_async_copy(pack0_ref, pack_ref, keep_sems.at[0]).wait()
    k = pack_ref[pl.ds(2 * top, rows), :]
    v = pack_ref[pl.ds(2 * top + rows, rows), :]
    dk = jnp.zeros((rows, HEAD_DIM), F32)
    dv = jnp.zeros((rows, HEAD_DIM), F32)
    for n in range(qh):
        cols = slice(n * HEAD_DIM, (n + 1) * HEAD_DIM)
        qn = pack_ref[pl.ds(n * rows, rows), :]
        weights = pack_ref[pl.ds(top + n * rows, rows), :]
        don = do[:, cols]
        wf = weights.astype(F32)
        dw = dot_nt(don, v)
        ds = wf * (dw - jnp.sum(dw * wf, axis=1, keepdims=True)) * SCORE_SCALE
        ds = ds.astype(BF16)
        d_ref[:, cols] = dot(ds, k).astype(BF16)
        dk = dk + dot_tn(ds, qn)
        dv = dv + dot_tn(weights, don)
    d_ref[:, qcol : qcol + HEAD_DIM] = dk.astype(BF16)
    d_ref[:, qcol + HEAD_DIM :] = dv.astype(BF16)
    if not with_input:
        return
    pltpu.make_async_copy(h0_ref, h_ref, keep_sems.at[1]).wait()
    pltpu.make_async_copy(scale0_ref, scale_ref, keep_sems.at[2]).wait()
    dq = d_ref[:, :qcol]
    dk = dk.astype(BF16)
    dv = dv.astype(BF16)
    inner = jnp.zeros((rows, 1), F32)
    for j in range(nblk):
        at = pl.ds(j * dsh, dsh)
        dh = dot_nt(dq, wq_ref[at, :]) + dot_nt(dk, wk_ref[at, :]) + dot_nt(dv, wv_ref[at, :])
        dh_ref[j] = dh
        inner = inner + jnp.sum(dh * h_ref[j].astype(F32), axis=1, keepdims=True)
    inner = inner / (nblk * dsh)
    scale = scale_ref[:, :1]
    for j in range(nblk):
        dx_ref[j, :rows] = (scale * (dh_ref[j] - h_ref[j].astype(F32) * inner)).astype(BF16)
        if with_ends:
            dx_ref[j, rows:] = ends_ref[...]


def backward(flag, g, one, two, weights, with_input, ends=()):
    nblk, rows, dsh = g.shape
    wq, wk, wv, wo = weights
    qcol = wq.shape[1]
    out_shape = [jax.ShapeDtypeStruct((rows, qcol + 2 * HEAD_DIM), BF16)]
    scratch = [pltpu.VMEM(one["pack"].shape, BF16), pltpu.SemaphoreType.DMA((3,))]
    if with_input:
        below = sum(x.shape[0] for x in ends)
        out_shape.append(jax.ShapeDtypeStruct((nblk, rows + below, dsh), BF16))
        scratch += [
            pltpu.VMEM(g.shape, BF16),
            pltpu.VMEM(one["scale"].shape, F32),
            pltpu.VMEM(g.shape, F32),
        ]
    return pl.pallas_call(
        functools.partial(backward_kernel, with_input, bool(ends)),
        out_shape=tuple(out_shape),
        in_specs=[in_smem(), in_vmem()] + [anywhere()] * 6 + [in_vmem()] * (4 + len(ends)),
        out_specs=tuple([in_vmem()] * len(out_shape)),
        scratch_shapes=scratch,
        compiler_params=kernel_params(VMEM_LIMIT),
        cost_estimate=pl.CostEstimate(
            flops=2 * rows * nblk * dsh * (2 * qcol + 2 * HEAD_DIM),
            bytes_accessed=4 * nblk * dsh * (qcol + HEAD_DIM),
            transcendentals=0,
        ),
        name="backward_layer" if with_input else "backward_heads",
    )(
        flag, g, one["pack"], two["pack"], one["h"], two["h"],
        one["scale"], two["scale"], wq, wk, wv, wo, *ends,
    )


def gather_rows(to, pieces):
    per = to.shape[2] // pieces[0][0].shape[2]
    for i, run in enumerate(pieces):
        at = 0
        for piece in run:
            nblk, rows, dsh = piece.shape
            for b in range(nblk):
                cols = pl.ds((at + b) % per * dsh, dsh)
                to[(at + b) // per, pl.ds(i * rows, rows), cols] = piece[b]
            at += nblk


def weight_grad_kernel(wide_first, runs, splits, place_ref, *refs):
    nwide = sum(runs)
    nout = len(splits) + 1
    wides, narrows, outs = refs[:nwide], refs[nwide : -nout - 2], refs[-nout - 2 : -2]
    wide_all, narrow_all = refs[-2:]
    core = place_ref[0]
    pieces, at = [], 0
    for n in runs:
        pieces.append(wides[at : at + n])
        at += n
    gather_rows(wide_all, pieces)
    rows = narrows[0].shape[0]
    for i, piece in enumerate(narrows):
        narrow_all[pl.ds(i * rows, rows), :] = piece[...]
    give_ref, mine = outs[0], outs[1:]
    for given, quarter in ((True, 1 - core), (False, core)):
        for c in range(give_ref.shape[0] // 256):
            cols = pl.ds(c * 256, 256)
            if wide_first:
                got = dot_tn(wide_all[quarter, :, cols], narrow_all[...])
            else:
                got = dot_tn(narrow_all[:, cols], wide_all[quarter])
            if given:
                give_ref[cols, :] = got.astype(BF16)
            else:
                for out_ref, (start, stop) in zip(mine, splits):
                    out_ref[cols, :] = got[:, start:stop]


def weight_grad(place, wide, narrow, wide_first, widths):
    rows, cols = narrow[0].shape
    dsh = wide[0][0].shape[-1]
    width = sum(x.shape[-3] for x in wide[0]) * dsh // 2
    shape = (width, cols) if wide_first else (cols, width)
    total = len(narrow) * rows
    flat = [x for run in wide for x in run]
    splits = [(sum(widths[:i]), sum(widths[: i + 1])) for i in range(len(widths))]
    out = pl.pallas_call(
        functools.partial(
            weight_grad_kernel, wide_first, tuple(len(run) for run in wide), tuple(splits)
        ),
        out_shape=(jax.ShapeDtypeStruct(shape, BF16),)
        + tuple(jax.ShapeDtypeStruct((shape[0], w), F32) for w in widths),
        in_specs=[in_smem()] + [in_vmem()] * (len(flat) + len(narrow)),
        out_specs=tuple([in_vmem()] * (1 + len(widths))),
        scratch_shapes=[pltpu.VMEM((2, total, width), BF16), pltpu.VMEM((total, cols), BF16)],
        compiler_params=kernel_params(VMEM_LIMIT),
        cost_estimate=pl.CostEstimate(
            flops=4 * total * width * cols, bytes_accessed=6 * width * cols, transcendentals=0
        ),
        name="weight_grad",
    )(place, *flat, *narrow)
    return out[0], out[1:]


def passed_along(x, axis, by):
    peers = lax.axis_size(axis)
    pairs = [(i, i + by) for i in range(peers) if 0 <= i + by < peers]
    return lax.ppermute(x, axis, pairs)


def swapped(x, axis, mask):
    return lax.ppermute(x, axis, [(i, i ^ mask) for i in range(lax.axis_size(axis))])


def mirrored(x, mask):
    ndp, peers = lax.axis_size("dp"), lax.axis_size("tensor")
    to = lambda p, r: (p ^ mask) * peers + (r + peers // 2) % peers
    pairs = [(p * peers + r, to(p, r)) for p in range(ndp) for r in range(peers)]
    return lax.ppermute(x, ("dp", "tensor"), pairs)


def held_back(x):
    return lax.ppermute(x[:16, :128], "dp", [(i, i + 1) for i in range(0, lax.axis_size("dp"), 2)])


def exchange(blocks):
    return lax.all_to_all(blocks, "tensor", split_axis=0, concat_axis=0, tiled=True)


def gathered(cur):
    return exchange(jnp.broadcast_to(cur[None], (lax.axis_size("tensor"),) + cur.shape))


def by_section(masks, choices):
    out = choices[-1]
    for mask, choice in zip(masks, choices[:-1]):
        out = jnp.where(mask, choice, out)
    return out


def after(x, *marks):
    return lax.optimization_barrier((x,) + marks)[0]


def together(*xs):
    return lax.optimization_barrier(xs)


def on_device(embeds, source, lengths, bounds, targets, w_query, w_key, w_value, w_out, w_class):
    nst = lax.axis_size("section")
    peers = lax.axis_size("tensor")
    rep = lax.axis_index("dp")
    section_at = lax.axis_index("section")
    tensor_at = lax.axis_index("tensor")
    ntr, width, dsh = embeds.shape
    weights = (w_query[0], w_key[0], w_value[0], w_out[0])
    w_class = gathered(w_class).reshape(peers * w_class.shape[0], w_class.shape[1])

    hi, core = rep // 2, rep % 2
    slots = source.reshape(2, 2, ntr) - rep * ntr

    def mine_for(col):
        owner = lax.dynamic_slice_in_dim(slots, col, 1, axis=1)[:, 0]
        out = jnp.zeros((2, ntr, width, dsh), BF16)
        for n in range(ntr):
            out = jnp.where((owner == n)[:, :, None, None], embeds[n][None, None], out)
        return out

    both = mine_for(core) + swapped(mine_for(1 - core), "dp", 1)
    own = lax.dynamic_slice_in_dim(both, hi, 1, axis=0)[0]
    away = lax.dynamic_slice_in_dim(both, 1 - hi, 1, axis=0)[0]
    away = [away[j] for j in range(ntr)]
    source, lengths, bounds, targets, away[0] = together(source, lengths, bounds, targets, away[0])

    def first(j):
        return own[j] + swapped(away[j], "dp", 2)


    wanted = lax.dynamic_slice_in_dim(source, rep * ntr, ntr)
    lens = lengths[wanted]
    bnd = bounds[wanted]
    tgt = targets[wanted]
    nstep = bnd.shape[1]
    factor = (LOSS_SCALE / jnp.sum(lens).astype(F32)).reshape(1)

    def one_hot(ids, size):
        hot = ids[:, None] == jnp.arange(size, dtype=jnp.int32)[None, :]
        return jnp.concatenate([hot, jnp.zeros((16 - nstep, size), bool)], axis=0)

    picks = [one_hot(bnd[j], width).astype(BF16) for j in range(ntr)]
    hots = [one_hot(tgt[j], w_class.shape[1]).astype(F32) for j in range(ntr)]
    spans = [jnp.where(section_at == n, lens[0], lens[1]).reshape(1) for n in range(nst + 1)]
    flags = [(section_at == s).astype(jnp.int32).reshape(1) for s in range(nst)]
    masks = [section_at == s for s in range(nst)]
    half = peers // 2
    mine_at = (hi * half).astype(jnp.uint32)
    away_at = [((1 - hi) * half + n * half // 2).astype(jnp.uint32) for n in range(2)]
    block_at = tensor_at.astype(jnp.uint32)
    place = core.astype(jnp.int32).reshape(1)

    def sum_of(got):
        return jnp.sum(got[:, :width].astype(F32), axis=0)

    kept = []
    arriving = None
    for turn in range(nst):
        cur = first(turn) if turn < ntr else jnp.zeros((width, dsh), BF16)
        if turn == 0:
            cur, factor, picks, hots, spans, flags, masks, mine_at, away_at, block_at, place, w_class = together(
                cur, factor, picks, hots, spans, flags, masks, mine_at, away_at, block_at, place, w_class
            )
        if arriving is not None:
            cur, arriving = together(cur, arriving)
            cur = jnp.where(masks[0], cur, arriving)
        x = gathered(cur)
        if turn == nst - 1:
            now = forward(spans[turn], x, weights, "both", picks[0], nstep)
        else:
            now = forward(spans[turn], x, weights)
        kept.append(now)
        blocks = now["part"]
        got = exchange(blocks)
        arriving = (cur.astype(F32) + sum_of(got)).astype(BF16)
        if turn == 0:
            away = [away[0], after(away[1], arriving)]
        leaving = arriving
        arriving = passed_along(arriving, "section", 1)

    def end_cotangent(which, got, x):
        return step_end_grad(factor, got, x, picks[which], w_class, hots[which], nstep)

    def own_block(blocks):
        return lax.dynamic_slice_in_dim(blocks, block_at, 1, axis=0)[0]

    def chosen(choices, at=None, count=None):
        if at is None:
            return by_section(masks, choices)
        return by_section(
            masks, [lax.dynamic_slice_in_dim(x, at, count, axis=0) for x in choices]
        )

    def not_before(choices, mark):
        return [after(x, mark) for x in choices]

    seen = lambda name, which: [kept[s + which][name] for s in range(nst)]
    back = lambda n, which: [taken[2 * nst - 1 - s + which][n] for s in range(nst)]

    pieces = {}

    def send_blocks(name, choices, n):
        pieces[f"{name}.{n}"] = mirrored(chosen(choices, away_at[n], half // 2), 2)

    def send_whole(name, choices):
        pieces[name] = swapped(chosen(choices), "dp", 2)

    taken = {}
    g_top = end_cotangent(0, got, x)
    grad = own_block(g_top)
    send_blocks("h0", not_before(seen("h", 0), leaving), 0)
    arriving, g_top, grad, pieces, _ = together(
        arriving, g_top, grad, pieces, held_back(leaving)
    )
    x = gathered(arriving)
    now = forward(spans[nst], x, weights, "ends", picks[1], nstep)
    d, dx = backward(
        jnp.zeros((1,), jnp.int32), g_top, kept[-1], kept[-1], weights, True, (now["part"],)
    )
    taken[nst] = (d, g_top)
    kept.append(now)
    got = exchange(dx)

    for turn in range(nst + 1, 2 * nst + 1):
        grad = (grad.astype(F32) + sum_of(got)).astype(BF16)
        leaving = grad
        if turn == nst + 1:
            g_top = end_cotangent(1, got, x)
            send_blocks("h0", not_before(seen("h", 0), grad), 1)
        elif turn < 2 * nst:
            n = turn - nst - 2
            send_blocks("h1", not_before(seen("h", 1), grad), n)
            send_whole(f"o{n}", not_before(seen("o", n), grad))
        else:
            for n in range(2):
                send_blocks("g0", not_before(back(1, 0), grad), n)
            send_whole("d0", not_before(back(0, 0), grad))
        grad, pieces, _ = together(
            passed_along(grad, "section", -1), pieces, held_back(leaving)
        )
        if turn == nst + 1:
            grad = jnp.where(masks[nst - 1], own_block(g_top), grad)
        g = gathered(grad)
        late = 2 * nst + 1 - turn
        early = max(late - 2, 0)
        flag = flags[late - 1]
        if turn < 2 * nst:
            d, dx = backward(flag, g, kept[early], kept[late], weights, True)
            taken[turn] = (d, g)
            got = exchange(dx)
        else:
            taken[turn] = (None, g)
            for n in range(2):
                send_blocks("g1", back(1, 1), n)
            (d,) = backward(flag, g, kept[early], kept[late], weights, False)
            taken[turn] = (d, g)
            send_whole("d1", back(0, 1))

    def wide(name, choices):
        runs = []
        for w in range(ntr):
            runs.append((chosen(not_before(choices(w), g), mine_at, half),))
            runs.append((pieces[f"{name}{w}.0"], pieces[f"{name}{w}.1"]))
        return runs

    def narrow(name, choices):
        out = []
        for w in range(ntr):
            out += [chosen(not_before(choices(w), g)), pieces[f"{name}{w}"]]
        return out

    qcol = weights[0].shape[1]
    give_o, (mine_o,) = weight_grad(
        place,
        wide("g", lambda w: back(1, w)),
        narrow("o", lambda w: seen("o", w)),
        False,
        (half // 2 * dsh,),
    )
    widths = (qcol, HEAD_DIM, HEAD_DIM)
    give_d, mine_d = weight_grad(
        place, wide("h", lambda w: seen("h", w)), narrow("d", lambda w: back(0, w)), True, widths
    )
    grad_o = mine_o + swapped(give_o, "dp", 1).astype(F32)
    add = jnp.split(swapped(give_d, "dp", 1), (qcol, qcol + HEAD_DIM), axis=1)
    grad_q, grad_k, grad_v = (mine + other.astype(F32) for mine, other in zip(mine_d, add))
    return (grad_q[None], grad_k[None], grad_v[None], grad_o[None])


def solution(mesh):
    placed = (
        P("dp", None, "tensor"),
        P(),
        P(),
        P(),
        P(),
        P("section", None, "tensor"),
        P("section", None, "tensor"),
        P("section", None, "tensor"),
        P("section", "tensor", None),
        P("tensor", None),
    )
    return jax.shard_map(
        on_device,
        mesh=mesh,
        in_specs=placed,
        out_specs=(
            P("section", "dp", "tensor"),
            P("section", "dp", "tensor"),
            P("section", "dp", "tensor"),
            P("section", "tensor", "dp"),
        ),
        check_vma=False,
    )
```

```python
import functools

import jax
import jax.numpy as jnp
from jax import lax
from jax.experimental import pallas as pl
from jax.experimental.pallas import tpu as pltpu
from jax.sharding import PartitionSpec as P

HEAD_DIM = 128
EPS = 1e-06
LOSS_SCALE = 16384.0
SCORE_SCALE = 1.0 / HEAD_DIM**0.5
F32 = jnp.float32
BF16 = jnp.bfloat16
VMEM_LIMIT = 16 * 1024 * 1024


def dot(a, b):
    return jnp.dot(a, b, preferred_element_type=F32)


def dot_nt(a, b):
    return lax.dot_general(a, b, (((1,), (1,)), ((), ())), preferred_element_type=F32)


def dot_tn(a, b):
    return lax.dot_general(a, b, (((0,), (0,)), ((), ())), preferred_element_type=F32)


def in_vmem():
    return pl.BlockSpec(memory_space=pltpu.VMEM)


def in_smem():
    return pl.BlockSpec(memory_space=pltpu.SMEM)


def anywhere():
    return pl.BlockSpec(memory_space=pl.ANY)


def kernel_params(limit):
    return pltpu.CompilerParams(vmem_limit_bytes=limit)


def place_ends(ends_ref, block, rows, nstep):
    ends_ref[pl.ds(block * nstep, nstep), :] = rows[:nstep]


def forward_kernel(mode, nstep, len_ref, x_ref, wq_ref, wk_ref, wv_ref, wo_ref, *rest):
    if mode == "all":
        part_ref, h_ref, scale_ref, pack_ref, o_ref = rest
    else:
        pick_ref, part_ref, h_ref, scale_ref, pack_ref, o_ref, ends_ref = rest
    nblk, rows, dsh = x_ref.shape
    qh = wq_ref.shape[1] // HEAD_DIM
    sq = jnp.zeros((rows, 1), F32)
    for j in range(nblk):
        xf = x_ref[j].astype(F32)
        sq = sq + jnp.sum(xf * xf, axis=1, keepdims=True)
    scale = lax.rsqrt(sq / (nblk * dsh) + EPS)
    scale_ref[...] = jnp.broadcast_to(scale, scale_ref.shape)
    q = jnp.zeros((rows, wq_ref.shape[1]), F32)
    k = jnp.zeros((rows, HEAD_DIM), F32)
    v = jnp.zeros((rows, HEAD_DIM), F32)
    for j in range(nblk):
        h = (x_ref[j].astype(F32) * scale).astype(BF16)
        h_ref[j] = h
        at = pl.ds(j * dsh, dsh)
        q = q + dot(h, wq_ref[at, :])
        k = k + dot(h, wk_ref[at, :])
        v = v + dot(h, wv_ref[at, :])
    q = q.astype(BF16)
    k = k.astype(BF16)
    v = v.astype(BF16)
    top = qh * rows
    pack_ref[pl.ds(2 * top, rows), :] = k
    pack_ref[pl.ds(2 * top + rows, rows), :] = v
    posq = lax.broadcasted_iota(jnp.int32, (rows, rows), 0)
    posk = lax.broadcasted_iota(jnp.int32, (rows, rows), 1)
    keep = ((posk <= posq) & (posk < len_ref[0])).astype(F32)
    for n in range(qh):
        qn = q[:, n * HEAD_DIM : (n + 1) * HEAD_DIM]
        pack_ref[pl.ds(n * rows, rows), :] = qn
        expo = jnp.exp(dot_nt(qn, k) * SCORE_SCALE) * keep
        weights = (expo / jnp.sum(expo, axis=1, keepdims=True)).astype(BF16)
        pack_ref[pl.ds(top + n * rows, rows), :] = weights
        o_ref[:, pl.ds(n * HEAD_DIM, HEAD_DIM)] = dot(weights, v).astype(BF16)
    o = o_ref[...]
    if mode == "ends":
        o = dot(pick_ref[...], o).astype(BF16)
    for j in range(nblk):
        part = dot(o, wo_ref[:, pl.ds(j * dsh, dsh)])
        if mode == "ends":
            place_ends(ends_ref, j, part, nstep)
            continue
        part_ref[j, :rows] = part.astype(BF16)
        if mode == "both":
            place_ends(ends_ref, j, dot(pick_ref[...], part.astype(BF16)), nstep)
    if mode == "ends":
        part_ref[...] = ends_ref[...].astype(BF16)
    elif mode == "both":
        for j in range(nblk):
            part_ref[j, rows:] = ends_ref[...].astype(BF16)


def forward(length, x, weights, mode="all", pick=None, nstep=0):
    nblk, rows, dsh = x.shape
    qcol = weights[0].shape[1]
    packed = 2 * qcol // HEAD_DIM * rows + 2 * rows
    nend = nblk * nstep
    part = {"all": x.shape, "both": (nblk, rows + nend, dsh), "ends": (nend, dsh)}[mode]
    outs = [(part, BF16), (x.shape, BF16)]
    outs += [((rows, HEAD_DIM), F32), ((packed, HEAD_DIM), BF16), ((rows, qcol), BF16)]
    more = [] if mode == "all" else [pick]
    out = pl.pallas_call(
        functools.partial(forward_kernel, mode, nstep),
        out_shape=tuple(jax.ShapeDtypeStruct(*one) for one in outs),
        in_specs=[in_smem()] + [in_vmem()] * (5 + len(more)),
        out_specs=tuple([in_vmem()] * 5),
        scratch_shapes=[pltpu.VMEM((nend, dsh), F32)] if more else [],
        compiler_params=kernel_params(VMEM_LIMIT),
        cost_estimate=pl.CostEstimate(
            flops=2 * rows * nblk * dsh * (2 * qcol + 2 * HEAD_DIM),
            bytes_accessed=4 * nblk * dsh * (qcol + HEAD_DIM),
            transcendentals=rows * rows * qcol // HEAD_DIM,
        ),
        name="forward_layer",
    )(length, x, *weights, *more)
    return dict(zip(("part", "h", "scale", "pack", "o"), out))


def step_end_kernel(nstep, factor_ref, got_ref, x_ref, pick_ref, class_ref, hot_ref, out_ref, sum_ref, row_ref):
    nblk, rows, dsh = x_ref.shape
    width = nblk * dsh
    nend = nblk * nstep
    parts = jnp.zeros((nend, dsh), F32)
    for j in range(nblk):
        parts = parts + got_ref[j, rows:].astype(F32)
    sum_ref[...] = parts
    npad = pick_ref.shape[0]
    row_ref[...] = jnp.zeros(row_ref.shape, F32)
    zeta = jnp.zeros((npad, class_ref.shape[1]), F32)
    sumsq = jnp.zeros((npad, 1), F32)
    for j in range(nblk):
        row_ref[j, :nstep] = sum_ref[pl.ds(j * nstep, nstep), :]
        full = (dot(pick_ref[...], x_ref[j]) + row_ref[j]).astype(BF16)
        ff = full.astype(F32)
        row_ref[j] = ff
        zeta = zeta + dot(full, class_ref[pl.ds(j * dsh, dsh), :])
        sumsq = sumsq + jnp.sum(ff * ff, axis=1, keepdims=True)
    rstd = lax.rsqrt(sumsq / width + EPS)
    expo = jnp.exp(zeta * rstd)
    prob = expo / jnp.sum(expo, axis=1, keepdims=True)
    dlog = factor_ref[0] * (prob - hot_ref[...])
    dzeta = dlog * rstd
    dmean = jnp.sum(dlog * zeta, axis=1, keepdims=True) * -0.5 * rstd * rstd * rstd
    high = dzeta.astype(BF16)
    mid = (dzeta - high.astype(F32)).astype(BF16)
    low = (dzeta - high.astype(F32) - mid.astype(F32)).astype(BF16)
    for j in range(nblk):
        head = class_ref[pl.ds(j * dsh, dsh), :]
        back = dot_nt(high, head) + (dot_nt(mid, head) + dot_nt(low, head))
        back = (back + dmean * 2.0 * row_ref[j] / width).astype(BF16)
        out_ref[j] = dot_tn(pick_ref[...], back).astype(BF16)


def step_end_grad(factor, got, x, pick, w_class, hot, nstep):
    nblk, rows, dsh = x.shape
    return pl.pallas_call(
        functools.partial(step_end_kernel, nstep),
        out_shape=jax.ShapeDtypeStruct(x.shape, BF16),
        in_specs=[in_smem()] + [in_vmem()] * 5,
        out_specs=in_vmem(),
        scratch_shapes=[
            pltpu.VMEM((nblk * nstep, dsh), F32),
            pltpu.VMEM((nblk, pick.shape[0], dsh), F32),
        ],
        compiler_params=kernel_params(VMEM_LIMIT),
        cost_estimate=pl.CostEstimate(
            flops=16 * rows * nblk * dsh * pick.shape[0], bytes_accessed=4 * rows * nblk * dsh,
            transcendentals=0,
        ),
        name="step_end_grad",
    )(factor, got, x, pick, w_class, hot)


def backward_kernel(
    with_input, with_ends, nheld, flag_ref, g_ref, pack0_ref, pack1_ref, h0_ref, h1_ref,
    scale0_ref, scale1_ref, wq_ref, wk_ref, wv_ref, wo_ref, *rest
):
    rest = rest[nheld:]
    if with_ends:
        ends_ref, rest = rest[0], rest[1:]
    if with_input:
        d_ref, dx_ref, pack_ref, keep_sems, h_ref, scale_ref, dh_ref = rest
    else:
        d_ref, pack_ref, keep_sems = rest
    nblk, rows, dsh = g_ref.shape
    qcol = wq_ref.shape[1]
    qh = qcol // HEAD_DIM
    top = qh * rows
    pairs = [(pack0_ref, pack1_ref, pack_ref)]
    if with_input:
        pairs += [(h0_ref, h1_ref, h_ref), (scale0_ref, scale1_ref, scale_ref)]
    for at, (one, two, to) in enumerate(pairs):

        @pl.when(flag_ref[0] == 0)
        def _(one=one, to=to, at=at):
            pltpu.make_async_copy(one, to, keep_sems.at[at]).start()

        @pl.when(flag_ref[0] != 0)
        def _(two=two, to=to, at=at):
            pltpu.make_async_copy(two, to, keep_sems.at[at]).start()

    do = jnp.zeros((rows, qcol), F32)
    for j in range(nblk):
        do = do + dot_nt(g_ref[j], wo_ref[:, pl.ds(j * dsh, dsh)])
    do = do.astype(BF16)
    pltpu.make_async_copy(pack0_ref, pack_ref, keep_sems.at[0]).wait()
    k = pack_ref[pl.ds(2 * top, rows), :]
    v = pack_ref[pl.ds(2 * top + rows, rows), :]
    dk = jnp.zeros((rows, HEAD_DIM), F32)
    dv = jnp.zeros((rows, HEAD_DIM), F32)
    for n in range(qh):
        cols = slice(n * HEAD_DIM, (n + 1) * HEAD_DIM)
        qn = pack_ref[pl.ds(n * rows, rows), :]
        weights = pack_ref[pl.ds(top + n * rows, rows), :]
        don = do[:, cols]
        wf = weights.astype(F32)
        dw = dot_nt(don, v)
        ds = wf * (dw - jnp.sum(dw * wf, axis=1, keepdims=True)) * SCORE_SCALE
        ds = ds.astype(BF16)
        d_ref[:, cols] = dot(ds, k).astype(BF16)
        dk = dk + dot_tn(ds, qn)
        dv = dv + dot_tn(weights, don)
    d_ref[:, qcol : qcol + HEAD_DIM] = dk.astype(BF16)
    d_ref[:, qcol + HEAD_DIM :] = dv.astype(BF16)
    if not with_input:
        return
    pltpu.make_async_copy(h0_ref, h_ref, keep_sems.at[1]).wait()
    pltpu.make_async_copy(scale0_ref, scale_ref, keep_sems.at[2]).wait()
    dq = d_ref[:, :qcol]
    dk = dk.astype(BF16)
    dv = dv.astype(BF16)
    inner = jnp.zeros((rows, 1), F32)
    for j in range(nblk):
        at = pl.ds(j * dsh, dsh)
        dh = dot_nt(dq, wq_ref[at, :]) + dot_nt(dk, wk_ref[at, :]) + dot_nt(dv, wv_ref[at, :])
        dh_ref[j] = dh
        inner = inner + jnp.sum(dh * h_ref[j].astype(F32), axis=1, keepdims=True)
    inner = inner / (nblk * dsh)
    scale = scale_ref[:, :1]
    for j in range(nblk):
        dx_ref[j, :rows] = (scale * (dh_ref[j] - h_ref[j].astype(F32) * inner)).astype(BF16)
        if with_ends:
            dx_ref[j, rows:] = ends_ref[...]


def backward(flag, g, one, two, weights, with_input, ends=(), held=()):
    nblk, rows, dsh = g.shape
    wq, wk, wv, wo = weights
    qcol = wq.shape[1]
    out_shape = [jax.ShapeDtypeStruct((rows, qcol + 2 * HEAD_DIM), BF16)]
    scratch = [pltpu.VMEM(one["pack"].shape, BF16), pltpu.SemaphoreType.DMA((3,))]
    if with_input:
        below = sum(x.shape[0] for x in ends)
        out_shape.append(jax.ShapeDtypeStruct((nblk, rows + below, dsh), BF16))
        scratch += [
            pltpu.VMEM(g.shape, BF16),
            pltpu.VMEM(one["scale"].shape, F32),
            pltpu.VMEM(g.shape, F32),
        ]
    return pl.pallas_call(
        functools.partial(backward_kernel, with_input, bool(ends), len(held)),
        out_shape=tuple(out_shape),
        in_specs=[in_smem(), in_vmem()]
        + [anywhere()] * 6
        + [in_vmem()] * 4
        + [anywhere()] * len(held)
        + [in_vmem()] * len(ends),
        out_specs=tuple([in_vmem()] * len(out_shape)),
        scratch_shapes=scratch,
        compiler_params=kernel_params(VMEM_LIMIT),
        cost_estimate=pl.CostEstimate(
            flops=2 * rows * nblk * dsh * (2 * qcol + 2 * HEAD_DIM),
            bytes_accessed=4 * nblk * dsh * (qcol + HEAD_DIM),
            transcendentals=0,
        ),
        name="backward_layer" if with_input else "backward_heads",
    )(
        flag, g, one["pack"], two["pack"], one["h"], two["h"],
        one["scale"], two["scale"], wq, wk, wv, wo, *held, *ends,
    )


def weight_grad_kernel(wide_first, runs, nnarrow, splits, quarter_ref, *refs):
    nwide, nout = sum(runs), len(splits)
    wides, narrows = refs[:nwide], refs[nwide : nwide + nnarrow]
    given, outs = refs[nwide + nnarrow : -nout - 2], refs[-nout - 2 : -2]
    wide_all, narrow_all = refs[-2:]
    quarter = quarter_ref[0]
    at = 0
    for i, n in enumerate(runs):
        run = wides[at : at + n]
        at += n
        rows, dsh = run[0].shape[1:]
        here = pl.ds(i * rows, rows)
        if n == 1:
            half = run[0].shape[0] // 2
            for b in range(half):
                wide_all[here, pl.ds(b * dsh, dsh)] = run[0][quarter * half + b]
        for which, piece in enumerate(run if n > 1 else ()):

            @pl.when(quarter == which)
            def _(piece=piece):
                for b in range(piece.shape[0]):
                    wide_all[here, pl.ds(b * dsh, dsh)] = piece[b]

    rows = narrows[0].shape[0]
    for i, piece in enumerate(narrows):
        narrow_all[pl.ds(i * rows, rows), :] = piece[...]
    for c in range(outs[0].shape[0] // 256):
        cols = pl.ds(c * 256, 256)
        if wide_first:
            got = dot_tn(wide_all[:, cols], narrow_all[...])
        else:
            got = dot_tn(narrow_all[:, cols], wide_all[...])
        for more in given:
            got = got + more[cols, :].astype(F32)
        for out_ref, (start, stop) in zip(outs, splits):
            out_ref[cols, :] = got[:, start:stop].astype(out_ref.dtype)


def weight_grad(quarter, wide, narrow, wide_first, widths, dtype, given=()):
    rows, cols = narrow[0].shape
    dsh = wide[0][0].shape[2]
    width = sum(x.shape[0] for x in wide[0]) * dsh // 2
    height = width if wide_first else cols
    total = len(narrow) * rows
    flat = [x for run in wide for x in run]
    splits = [(sum(widths[:i]), sum(widths[: i + 1])) for i in range(len(widths))]
    runs = tuple(len(run) for run in wide)
    return pl.pallas_call(
        functools.partial(weight_grad_kernel, wide_first, runs, len(narrow), tuple(splits)),
        out_shape=tuple(jax.ShapeDtypeStruct((height, w), dtype) for w in widths),
        in_specs=[in_smem()] + [in_vmem()] * (len(flat) + len(narrow) + len(given)),
        out_specs=tuple([in_vmem()] * len(widths)),
        scratch_shapes=[pltpu.VMEM((total, width), BF16), pltpu.VMEM((total, cols), BF16)],
        compiler_params=kernel_params(VMEM_LIMIT),
        cost_estimate=pl.CostEstimate(
            flops=2 * total * width * cols, bytes_accessed=4 * width * cols, transcendentals=0
        ),
        name="weight_grad",
    )(quarter, *flat, *narrow, *given)


def passed_along(x, axis, by):
    peers = lax.axis_size(axis)
    pairs = [(i, i + by) for i in range(peers) if 0 <= i + by < peers]
    return lax.ppermute(x, axis, pairs)


def swapped(x, axis, mask):
    return lax.ppermute(x, axis, [(i, i ^ mask) for i in range(lax.axis_size(axis))])


def mirrored(x, mask):
    ndp, peers = lax.axis_size("dp"), lax.axis_size("tensor")
    to = lambda p, r: (p ^ mask) * peers + (r + peers // 2) % peers
    pairs = [(p * peers + r, to(p, r)) for p in range(ndp) for r in range(peers)]
    return lax.ppermute(x, ("dp", "tensor"), pairs)


def held_back(x):
    return lax.ppermute(x[:16, :128], "dp", [(i, i + 1) for i in range(0, lax.axis_size("dp"), 2)])


def exchange(blocks):
    return lax.all_to_all(blocks, "tensor", split_axis=0, concat_axis=0, tiled=True)


def gathered(cur):
    return exchange(jnp.broadcast_to(cur[None], (lax.axis_size("tensor"),) + cur.shape))


def by_section(masks, choices):
    out = choices[-1]
    for mask, choice in zip(masks, choices[:-1]):
        out = jnp.where(mask, choice, out)
    return out


def after(x, *marks):
    return lax.optimization_barrier((x,) + marks)[0]


def together(*xs):
    return lax.optimization_barrier(xs)


def on_device(embeds, source, lengths, bounds, targets, w_query, w_key, w_value, w_out, w_class):
    nst = lax.axis_size("section")
    peers = lax.axis_size("tensor")
    rep = lax.axis_index("dp")
    section_at = lax.axis_index("section")
    tensor_at = lax.axis_index("tensor")
    ntr, width, dsh = embeds.shape
    weights = (w_query[0], w_key[0], w_value[0], w_out[0])
    w_class = gathered(w_class).reshape(peers * w_class.shape[0], w_class.shape[1])

    hi, core = rep // 2, rep % 2
    slots = source.reshape(2, 2, ntr) - rep * ntr

    def mine_for(col):
        owner = lax.dynamic_slice_in_dim(slots, col, 1, axis=1)[:, 0]
        out = jnp.zeros((2, ntr, width, dsh), BF16)
        for n in range(ntr):
            out = jnp.where((owner == n)[:, :, None, None], embeds[n][None, None], out)
        return out

    both = mine_for(core) + swapped(mine_for(1 - core), "dp", 1)
    own = lax.dynamic_slice_in_dim(both, hi, 1, axis=0)[0]
    away = lax.dynamic_slice_in_dim(both, 1 - hi, 1, axis=0)[0]
    away = [away[j] for j in range(ntr)]
    source, lengths, bounds, targets, away[0] = together(source, lengths, bounds, targets, away[0])

    def first(j):
        return own[j] + swapped(away[j], "dp", 2)


    wanted = lax.dynamic_slice_in_dim(source, rep * ntr, ntr)
    lens = lengths[wanted]
    bnd = bounds[wanted]
    tgt = targets[wanted]
    nstep = bnd.shape[1]
    factor = (LOSS_SCALE / jnp.sum(lens).astype(F32)).reshape(1)

    def one_hot(ids, size):
        hot = ids[:, None] == jnp.arange(size, dtype=jnp.int32)[None, :]
        return jnp.concatenate([hot, jnp.zeros((16 - nstep, size), bool)], axis=0)

    picks = [one_hot(bnd[j], width).astype(BF16) for j in range(ntr)]
    hots = [one_hot(tgt[j], w_class.shape[1]).astype(F32) for j in range(ntr)]
    spans = [jnp.where(section_at == n, lens[0], lens[1]).reshape(1) for n in range(nst + 1)]
    flags = [(section_at == s).astype(jnp.int32).reshape(1) for s in range(nst)]
    masks = [section_at == s for s in range(nst)]
    half = peers // 2
    mine_at = (hi * half).astype(jnp.uint32)
    away_at = [((1 - hi) * half + n * half // 2).astype(jnp.uint32) for n in range(2)]
    block_at = tensor_at.astype(jnp.uint32)
    ours = core.astype(jnp.int32).reshape(1)
    theirs = 1 - ours

    def sum_of(got):
        return jnp.sum(got[:, :width].astype(F32), axis=0)

    kept = []
    arriving = None
    for turn in range(nst):
        cur = first(turn) if turn < ntr else jnp.zeros((width, dsh), BF16)
        if turn == 0:
            cur, factor, picks, hots, spans, flags, masks, mine_at, away_at, block_at, ours, theirs, w_class = together(
                cur, factor, picks, hots, spans, flags, masks, mine_at, away_at, block_at, ours, theirs, w_class
            )
        if arriving is not None:
            cur, arriving = together(cur, arriving)
            cur = jnp.where(masks[0], cur, arriving)
        x = gathered(cur)
        if turn == nst - 1:
            now = forward(spans[turn], x, weights, "both", picks[0], nstep)
        else:
            now = forward(spans[turn], x, weights)
        kept.append(now)
        blocks = now["part"]
        got = exchange(blocks)
        arriving = (cur.astype(F32) + sum_of(got)).astype(BF16)
        if turn == 0:
            away = [away[0], after(away[1], arriving)]
        leaving = arriving
        arriving = passed_along(arriving, "section", 1)

    def end_cotangent(which, got, x):
        return step_end_grad(factor, got, x, picks[which], w_class, hots[which], nstep)

    def own_block(blocks):
        return lax.dynamic_slice_in_dim(blocks, block_at, 1, axis=0)[0]

    def chosen(choices, at=None, count=None):
        if at is None:
            return by_section(masks, choices)
        return by_section(
            masks, [lax.dynamic_slice_in_dim(x, at, count, axis=0) for x in choices]
        )

    def not_before(choices, mark):
        return [after(x, mark) for x in choices]

    seen = lambda name, which: [kept[s + which][name] for s in range(nst)]
    back = lambda n, which: [taken[2 * nst - 1 - s + which][n] for s in range(nst)]

    pieces = {}

    def send_blocks(name, choices, n):
        pieces[f"{name}.{n}"] = mirrored(chosen(choices, away_at[n], half // 2), 2)

    def send_half(name, choices):
        pieces[name] = mirrored(chosen(choices, away_at[0], half), 2)

    def send_whole(name, choices):
        pieces[name] = swapped(chosen(choices), "dp", 2)

    taken = {}
    g_top = end_cotangent(0, got, x)
    grad = own_block(g_top)
    send_blocks("h0", not_before(seen("h", 0), leaving), 0)
    arriving, g_top, grad, pieces = together(arriving, g_top, grad, pieces)
    x = gathered(arriving)
    now = forward(spans[nst], x, weights, "ends", picks[1], nstep)
    d, dx = backward(
        jnp.zeros((1,), jnp.int32), g_top, kept[-1], kept[-1], weights, True, (now["part"],)
    )
    taken[nst] = (d, g_top)
    kept.append(now)
    got = exchange(dx)

    for turn in range(nst + 1, 2 * nst + 1):
        grad = (grad.astype(F32) + sum_of(got)).astype(BF16)
        leaving = grad
        if turn == nst + 1:
            g_top = end_cotangent(1, got, x)
            send_blocks("h0", not_before(seen("h", 0), grad), 1)
        elif turn < 2 * nst:
            n = turn - nst - 2
            send_blocks("h1", not_before(seen("h", 1), grad), n)
            send_whole(f"o{n}", not_before(seen("o", n), grad))
        else:
            send_half("g0", not_before(back(1, 0), grad))
            send_whole("d0", not_before(back(0, 0), grad))
        held = [held_back(leaving)] if turn == nst + 1 else []
        grad, pieces, held = together(passed_along(grad, "section", -1), pieces, held)
        if turn == nst + 1:
            grad = jnp.where(masks[nst - 1], own_block(g_top), grad)
        g = gathered(grad)
        late = 2 * nst + 1 - turn
        early = max(late - 2, 0)
        flag = flags[late - 1]
        if turn < 2 * nst:
            d, dx = backward(flag, g, kept[early], kept[late], weights, True, (), held)
            taken[turn] = (d, g)
            got = exchange(dx)
        else:
            taken[turn] = (None, g)
            send_half("g1", back(1, 1))
            (d,) = backward(flag, g, kept[early], kept[late], weights, False)
            taken[turn] = (d, g)
            send_whole("d1", back(0, 1))

    def wide(name, choices):
        runs = []
        for w in range(ntr):
            runs.append((chosen(not_before(choices(w), g), mine_at, half),))
            names = (f"{name}{w}",) if name == "g" else (f"{name}{w}.0", f"{name}{w}.1")
            runs.append(tuple(pieces[n] for n in names))
        return runs

    def narrow(name, choices):
        out = []
        for w in range(ntr):
            out += [chosen(not_before(choices(w), g)), pieces[f"{name}{w}"]]
        return out

    qcol = weights[0].shape[1]
    all_o = (wide("g", lambda w: back(1, w)), narrow("o", lambda w: seen("o", w)), False)
    all_d = (wide("h", lambda w: seen("h", w)), narrow("d", lambda w: back(0, w)), True)
    cols_o, cols_d = (half // 2 * dsh,), (qcol, HEAD_DIM, HEAD_DIM)
    (give_o,) = weight_grad(theirs, *all_o, cols_o, BF16)
    given_o = swapped(give_o, "dp", 1)
    (give_d,) = weight_grad(theirs, *all_d, (sum(cols_d),), BF16)
    given_d = swapped(give_d, "dp", 1)
    (grad_o,) = weight_grad(ours, *all_o, cols_o, F32, (given_o,))
    grad_q, grad_k, grad_v = weight_grad(ours, *all_d, cols_d, F32, (given_d,))
    return (grad_q[None], grad_k[None], grad_v[None], grad_o[None])


def solution(mesh):
    placed = (
        P("dp", None, "tensor"),
        P(),
        P(),
        P(),
        P(),
        P("section", None, "tensor"),
        P("section", None, "tensor"),
        P("section", None, "tensor"),
        P("section", "tensor", None),
        P("tensor", None),
    )
    return jax.shard_map(
        on_device,
        mesh=mesh,
        in_specs=placed,
        out_specs=(
            P("section", "dp", "tensor"),
            P("section", "dp", "tensor"),
            P("section", "dp", "tensor"),
            P("section", "tensor", "dp"),
        ),
        check_vma=False,
    )
```

```python
import functools

import jax
import jax.numpy as jnp
from jax import lax
from jax.experimental import pallas as pl
from jax.experimental.pallas import tpu as pltpu
from jax.sharding import PartitionSpec as P

HEAD_DIM = 128
EPS = 1e-06
LOSS_SCALE = 16384.0
SCORE_SCALE = 1.0 / HEAD_DIM**0.5
F32 = jnp.float32
BF16 = jnp.bfloat16
VMEM_LIMIT = 16 * 1024 * 1024


def dot(a, b):
    return jnp.dot(a, b, preferred_element_type=F32)


def dot_nt(a, b):
    return lax.dot_general(a, b, (((1,), (1,)), ((), ())), preferred_element_type=F32)


def dot_tn(a, b):
    return lax.dot_general(a, b, (((0,), (0,)), ((), ())), preferred_element_type=F32)


def in_vmem():
    return pl.BlockSpec(memory_space=pltpu.VMEM)


def in_smem():
    return pl.BlockSpec(memory_space=pltpu.SMEM)


def anywhere():
    return pl.BlockSpec(memory_space=pl.ANY)


def kernel_params(limit):
    return pltpu.CompilerParams(vmem_limit_bytes=limit)


def heads_down(x, heads):
    return jnp.concatenate([x[:, n * HEAD_DIM : (n + 1) * HEAD_DIM] for n in range(heads)], axis=0)


def heads_across(x, heads):
    rows = x.shape[0] // heads
    return jnp.concatenate([x[n * rows : (n + 1) * rows] for n in range(heads)], axis=1)


def place_ends(ends_ref, block, rows, nstep):
    ends_ref[pl.ds(block * nstep, nstep), :] = rows[:nstep]


def forward_kernel(mode, nstep, len_ref, x_ref, wq_ref, wk_ref, wv_ref, wo_ref, *rest):
    if mode == "all":
        part_ref, h_ref, scale_ref, pack_ref, o_ref = rest
    else:
        pick_ref, part_ref, h_ref, scale_ref, pack_ref, o_ref, ends_ref = rest
    nblk, rows, dsh = x_ref.shape
    qh = wq_ref.shape[1] // HEAD_DIM
    sq = jnp.zeros((rows, 1), F32)
    for j in range(nblk):
        xf = x_ref[j].astype(F32)
        sq = sq + jnp.sum(xf * xf, axis=1, keepdims=True)
    scale = lax.rsqrt(sq / (nblk * dsh) + EPS)
    scale_ref[...] = jnp.broadcast_to(scale, scale_ref.shape)
    q = jnp.zeros((rows, wq_ref.shape[1]), F32)
    k = jnp.zeros((rows, HEAD_DIM), F32)
    v = jnp.zeros((rows, HEAD_DIM), F32)
    for j in range(nblk):
        h = (x_ref[j].astype(F32) * scale).astype(BF16)
        h_ref[j] = h
        at = pl.ds(j * dsh, dsh)
        q = q + dot(h, wq_ref[at, :])
        k = k + dot(h, wk_ref[at, :])
        v = v + dot(h, wv_ref[at, :])
    k = k.astype(BF16)
    v = v.astype(BF16)
    q = heads_down(q.astype(BF16), qh)
    top = qh * rows
    pack_ref[:top, :] = q
    pack_ref[pl.ds(2 * top, rows), :] = k
    pack_ref[pl.ds(2 * top + rows, rows), :] = v
    posq = lax.broadcasted_iota(jnp.int32, (rows, rows), 0)
    posk = lax.broadcasted_iota(jnp.int32, (rows, rows), 1)
    keep = ((posk <= posq) & (posk < len_ref[0])).astype(F32)
    expo = jnp.exp(dot_nt(q, k) * SCORE_SCALE) * jnp.concatenate([keep] * qh, axis=0)
    weights = (expo / jnp.sum(expo, axis=1, keepdims=True)).astype(BF16)
    pack_ref[pl.ds(top, top), :] = weights
    o_ref[...] = heads_across(dot(weights, v).astype(BF16), qh)
    o = o_ref[...]
    if mode != "all":
        picked = dot(pick_ref[...], o).astype(BF16)
        o = picked if mode == "ends" else jnp.concatenate([o, picked], axis=0)
    for j in range(nblk):
        part = dot(o, wo_ref[:, pl.ds(j * dsh, dsh)])
        if mode != "ends":
            part_ref[j, :rows] = part[:rows].astype(BF16)
        if mode != "all":
            place_ends(ends_ref, j, part[-pick_ref.shape[0] :], nstep)
    if mode == "ends":
        part_ref[...] = ends_ref[...].astype(BF16)
    elif mode == "both":
        for j in range(nblk):
            part_ref[j, rows:] = ends_ref[...].astype(BF16)


def forward(length, x, weights, mode="all", pick=None, nstep=0):
    nblk, rows, dsh = x.shape
    qcol = weights[0].shape[1]
    packed = 2 * qcol // HEAD_DIM * rows + 2 * rows
    nend = nblk * nstep
    part = {"all": x.shape, "both": (nblk, rows + nend, dsh), "ends": (nend, dsh)}[mode]
    outs = [(part, BF16), (x.shape, BF16)]
    outs += [((rows, HEAD_DIM), F32), ((packed, HEAD_DIM), BF16), ((rows, qcol), BF16)]
    more = [] if mode == "all" else [pick]
    out = pl.pallas_call(
        functools.partial(forward_kernel, mode, nstep),
        out_shape=tuple(jax.ShapeDtypeStruct(*one) for one in outs),
        in_specs=[in_smem()] + [in_vmem()] * (5 + len(more)),
        out_specs=tuple([in_vmem()] * 5),
        scratch_shapes=[pltpu.VMEM((nend, dsh), F32)] if more else [],
        compiler_params=kernel_params(VMEM_LIMIT),
        cost_estimate=pl.CostEstimate(
            flops=2 * rows * nblk * dsh * (2 * qcol + 2 * HEAD_DIM),
            bytes_accessed=4 * nblk * dsh * (qcol + HEAD_DIM),
            transcendentals=rows * rows * qcol // HEAD_DIM,
        ),
        name="forward_layer",
    )(length, x, *weights, *more)
    return dict(zip(("part", "h", "scale", "pack", "o"), out))


def step_end_kernel(nstep, factor_ref, got_ref, x_ref, pick_ref, class_ref, hot_ref, out_ref, sum_ref, row_ref):
    nblk, rows, dsh = x_ref.shape
    width = nblk * dsh
    nend = nblk * nstep
    parts = jnp.zeros((nend, dsh), F32)
    for j in range(nblk):
        parts = parts + got_ref[j, rows:].astype(F32)
    sum_ref[...] = parts
    npad = pick_ref.shape[0]
    row_ref[...] = jnp.zeros(row_ref.shape, F32)
    zeta = jnp.zeros((npad, class_ref.shape[1]), F32)
    sumsq = jnp.zeros((npad, 1), F32)
    for j in range(nblk):
        row_ref[j, :nstep] = sum_ref[pl.ds(j * nstep, nstep), :]
        full = (dot(pick_ref[...], x_ref[j]) + row_ref[j]).astype(BF16)
        ff = full.astype(F32)
        row_ref[j] = ff
        zeta = zeta + dot(full, class_ref[pl.ds(j * dsh, dsh), :])
        sumsq = sumsq + jnp.sum(ff * ff, axis=1, keepdims=True)
    rstd = lax.rsqrt(sumsq / width + EPS)
    expo = jnp.exp(zeta * rstd)
    prob = expo / jnp.sum(expo, axis=1, keepdims=True)
    dlog = factor_ref[0] * (prob - hot_ref[...])
    dzeta = dlog * rstd
    dmean = jnp.sum(dlog * zeta, axis=1, keepdims=True) * -0.5 * rstd * rstd * rstd
    high = dzeta.astype(BF16)
    mid = (dzeta - high.astype(F32)).astype(BF16)
    low = (dzeta - high.astype(F32) - mid.astype(F32)).astype(BF16)
    terms = jnp.concatenate([high, mid, low], axis=0)
    for j in range(nblk):
        head = class_ref[pl.ds(j * dsh, dsh), :]
        back = dot_nt(terms, head)
        back = back[:npad] + (back[npad : 2 * npad] + back[2 * npad :])
        back = (back + dmean * 2.0 * row_ref[j] / width).astype(BF16)
        out_ref[j] = dot_tn(pick_ref[...], back).astype(BF16)


def step_end_grad(factor, got, x, pick, w_class, hot, nstep):
    nblk, rows, dsh = x.shape
    return pl.pallas_call(
        functools.partial(step_end_kernel, nstep),
        out_shape=jax.ShapeDtypeStruct(x.shape, BF16),
        in_specs=[in_smem()] + [in_vmem()] * 5,
        out_specs=in_vmem(),
        scratch_shapes=[
            pltpu.VMEM((nblk * nstep, dsh), F32),
            pltpu.VMEM((nblk, pick.shape[0], dsh), F32),
        ],
        compiler_params=kernel_params(VMEM_LIMIT),
        cost_estimate=pl.CostEstimate(
            flops=16 * rows * nblk * dsh * pick.shape[0], bytes_accessed=4 * rows * nblk * dsh,
            transcendentals=0,
        ),
        name="step_end_grad",
    )(factor, got, x, pick, w_class, hot)


def backward_kernel(
    with_input, with_ends, nheld, flag_ref, g_ref, pack0_ref, pack1_ref, h0_ref, h1_ref,
    scale0_ref, scale1_ref, wq_ref, wk_ref, wv_ref, wo_ref, *rest
):
    rest = rest[nheld:]
    if with_ends:
        ends_ref, rest = rest[0], rest[1:]
    if with_input:
        d_ref, dx_ref, pack_ref, keep_sems, h_ref, scale_ref, dh_ref = rest
    else:
        d_ref, pack_ref, keep_sems = rest
    nblk, rows, dsh = g_ref.shape
    qcol = wq_ref.shape[1]
    qh = qcol // HEAD_DIM
    top = qh * rows
    pairs = [(pack0_ref, pack1_ref, pack_ref)]
    if with_input:
        pairs += [(h0_ref, h1_ref, h_ref), (scale0_ref, scale1_ref, scale_ref)]
    for at, (one, two, to) in enumerate(pairs):

        @pl.when(flag_ref[0] == 0)
        def _(one=one, to=to, at=at):
            pltpu.make_async_copy(one, to, keep_sems.at[at]).start()

        @pl.when(flag_ref[0] != 0)
        def _(two=two, to=to, at=at):
            pltpu.make_async_copy(two, to, keep_sems.at[at]).start()

    do = jnp.zeros((rows, qcol), F32)
    for j in range(nblk):
        do = do + dot_nt(g_ref[j], wo_ref[:, pl.ds(j * dsh, dsh)])
    do = do.astype(BF16)
    pltpu.make_async_copy(pack0_ref, pack_ref, keep_sems.at[0]).wait()
    k = pack_ref[pl.ds(2 * top, rows), :]
    v = pack_ref[pl.ds(2 * top + rows, rows), :]
    do = heads_down(do, qh)
    weights = pack_ref[pl.ds(top, top), :]
    wf = weights.astype(F32)
    dw = dot_nt(do, v)
    ds = wf * (dw - jnp.sum(dw * wf, axis=1, keepdims=True)) * SCORE_SCALE
    ds = ds.astype(BF16)
    dk = dot_tn(ds, pack_ref[:top, :])
    dv = dot_tn(weights, do)
    d_ref[:, :qcol] = heads_across(dot(ds, k).astype(BF16), qh)
    d_ref[:, qcol : qcol + HEAD_DIM] = dk.astype(BF16)
    d_ref[:, qcol + HEAD_DIM :] = dv.astype(BF16)
    if not with_input:
        return
    pltpu.make_async_copy(h0_ref, h_ref, keep_sems.at[1]).wait()
    pltpu.make_async_copy(scale0_ref, scale_ref, keep_sems.at[2]).wait()
    dq = d_ref[:, :qcol]
    dk = dk.astype(BF16)
    dv = dv.astype(BF16)
    inner = jnp.zeros((rows, 1), F32)
    for j in range(nblk):
        at = pl.ds(j * dsh, dsh)
        dh = dot_nt(dq, wq_ref[at, :]) + dot_nt(dk, wk_ref[at, :]) + dot_nt(dv, wv_ref[at, :])
        dh_ref[j] = dh
        inner = inner + jnp.sum(dh * h_ref[j].astype(F32), axis=1, keepdims=True)
    inner = inner / (nblk * dsh)
    scale = scale_ref[:, :1]
    for j in range(nblk):
        dx_ref[j, :rows] = (scale * (dh_ref[j] - h_ref[j].astype(F32) * inner)).astype(BF16)
        if with_ends:
            dx_ref[j, rows:] = ends_ref[...]


def backward(flag, g, one, two, weights, with_input, ends=(), held=()):
    nblk, rows, dsh = g.shape
    wq, wk, wv, wo = weights
    qcol = wq.shape[1]
    out_shape = [jax.ShapeDtypeStruct((rows, qcol + 2 * HEAD_DIM), BF16)]
    scratch = [pltpu.VMEM(one["pack"].shape, BF16), pltpu.SemaphoreType.DMA((3,))]
    if with_input:
        below = sum(x.shape[0] for x in ends)
        out_shape.append(jax.ShapeDtypeStruct((nblk, rows + below, dsh), BF16))
        scratch += [
            pltpu.VMEM(g.shape, BF16),
            pltpu.VMEM(one["scale"].shape, F32),
            pltpu.VMEM(g.shape, F32),
        ]
    return pl.pallas_call(
        functools.partial(backward_kernel, with_input, bool(ends), len(held)),
        out_shape=tuple(out_shape),
        in_specs=[in_smem(), in_vmem()]
        + [anywhere()] * 6
        + [in_vmem()] * 4
        + [anywhere()] * len(held)
        + [in_vmem()] * len(ends),
        out_specs=tuple([in_vmem()] * len(out_shape)),
        scratch_shapes=scratch,
        compiler_params=kernel_params(VMEM_LIMIT),
        cost_estimate=pl.CostEstimate(
            flops=2 * rows * nblk * dsh * (2 * qcol + 2 * HEAD_DIM) if with_input else 1,
            bytes_accessed=4 * nblk * dsh * (qcol + HEAD_DIM) if with_input else 1,
            transcendentals=0,
        ),
        name="backward_layer" if with_input else "backward_heads",
    )(
        flag, g, one["pack"], two["pack"], one["h"], two["h"],
        one["scale"], two["scale"], wq, wk, wv, wo, *held, *ends,
    )


def weight_grad_kernel(wide_first, runs, nnarrow, splits, quarter_ref, *refs):
    nwide, nout = sum(runs), len(splits)
    wides, narrows = refs[:nwide], refs[nwide : nwide + nnarrow]
    given, outs = refs[nwide + nnarrow : -nout - 2], refs[-nout - 2 : -2]
    wide_all, narrow_all = refs[-2:]
    quarter = quarter_ref[0]
    at = 0
    for i, n in enumerate(runs):
        run = wides[at : at + n]
        at += n
        rows, dsh = run[0].shape[1:]
        here = pl.ds(i * rows, rows)
        if n == 1:
            half = run[0].shape[0] // 2
            for b in range(half):
                wide_all[here, pl.ds(b * dsh, dsh)] = run[0][quarter * half + b]
        for which, piece in enumerate(run if n > 1 else ()):

            @pl.when(quarter == which)
            def _(piece=piece):
                for b in range(piece.shape[0]):
                    wide_all[here, pl.ds(b * dsh, dsh)] = piece[b]

    rows = narrows[0].shape[0]
    for i, piece in enumerate(narrows):
        narrow_all[pl.ds(i * rows, rows), :] = piece[...]
    for c in range(outs[0].shape[0] // 256):
        cols = pl.ds(c * 256, 256)
        if wide_first:
            got = dot_tn(wide_all[:, cols], narrow_all[...])
        else:
            got = dot_tn(narrow_all[:, cols], wide_all[...])
        for more in given:
            got = got + more[cols, :].astype(F32)
        for out_ref, (start, stop) in zip(outs, splits):
            out_ref[cols, :] = got[:, start:stop].astype(out_ref.dtype)


def weight_grad(quarter, wide, narrow, wide_first, widths, dtype, given=()):
    rows, cols = narrow[0].shape
    dsh = wide[0][0].shape[2]
    width = sum(x.shape[0] for x in wide[0]) * dsh // 2
    height = width if wide_first else cols
    total = len(narrow) * rows
    flat = [x for run in wide for x in run]
    splits = [(sum(widths[:i]), sum(widths[: i + 1])) for i in range(len(widths))]
    runs = tuple(len(run) for run in wide)
    return pl.pallas_call(
        functools.partial(weight_grad_kernel, wide_first, runs, len(narrow), tuple(splits)),
        out_shape=tuple(jax.ShapeDtypeStruct((height, w), dtype) for w in widths),
        in_specs=[in_smem()] + [in_vmem()] * (len(flat) + len(narrow) + len(given)),
        out_specs=tuple([in_vmem()] * len(widths)),
        scratch_shapes=[pltpu.VMEM((total, width), BF16), pltpu.VMEM((total, cols), BF16)],
        compiler_params=kernel_params(VMEM_LIMIT),
        cost_estimate=pl.CostEstimate(flops=1, bytes_accessed=1, transcendentals=0),
        name="weight_grad",
    )(quarter, *flat, *narrow, *given)


def passed_along(x, axis, by):
    peers = lax.axis_size(axis)
    pairs = [(i, i + by) for i in range(peers) if 0 <= i + by < peers]
    return lax.ppermute(x, axis, pairs)


def swapped(x, axis, mask):
    return lax.ppermute(x, axis, [(i, i ^ mask) for i in range(lax.axis_size(axis))])


def mirrored(x, mask):
    ndp, peers = lax.axis_size("dp"), lax.axis_size("tensor")
    to = lambda p, r: (p ^ mask) * peers + (r + peers // 2) % peers
    pairs = [(p * peers + r, to(p, r)) for p in range(ndp) for r in range(peers)]
    return lax.ppermute(x, ("dp", "tensor"), pairs)


def held_back(x):
    return lax.ppermute(x[:16, :128], "dp", [(i, i + 1) for i in range(0, lax.axis_size("dp"), 2)])


def exchange(blocks):
    return lax.all_to_all(blocks, "tensor", split_axis=0, concat_axis=0, tiled=True)


def gathered(cur):
    return exchange(jnp.broadcast_to(cur[None], (lax.axis_size("tensor"),) + cur.shape))


def by_section(masks, choices):
    out = choices[-1]
    for mask, choice in zip(masks, choices[:-1]):
        out = jnp.where(mask, choice, out)
    return out


def after(x, *marks):
    return lax.optimization_barrier((x,) + marks)[0]


def together(*xs):
    return lax.optimization_barrier(xs)


def on_device(embeds, source, lengths, bounds, targets, w_query, w_key, w_value, w_out, w_class):
    nst = lax.axis_size("section")
    peers = lax.axis_size("tensor")
    rep = lax.axis_index("dp")
    section_at = lax.axis_index("section")
    tensor_at = lax.axis_index("tensor")
    ntr, width, dsh = embeds.shape
    weights = (w_query[0], w_key[0], w_value[0], w_out[0])
    w_class = gathered(w_class).reshape(peers * w_class.shape[0], w_class.shape[1])

    hi, core = rep // 2, rep % 2
    slots = source.reshape(2, 2, ntr) - rep * ntr

    def mine_for(col):
        owner = lax.dynamic_slice_in_dim(slots, col, 1, axis=1)[:, 0]
        out = jnp.zeros((2, ntr, width, dsh), BF16)
        for n in range(ntr):
            out = jnp.where((owner == n)[:, :, None, None], embeds[n][None, None], out)
        return out

    both = mine_for(core) + swapped(mine_for(1 - core), "dp", 1)
    own = lax.dynamic_slice_in_dim(both, hi, 1, axis=0)[0]
    away = lax.dynamic_slice_in_dim(both, 1 - hi, 1, axis=0)[0]
    away = [away[j] for j in range(ntr)]

    def first(j):
        return own[j] + swapped(away[j], "dp", 2)


    begin = first(0)
    source, lengths, bounds, targets, begin = together(source, lengths, bounds, targets, begin)
    wanted = lax.dynamic_slice_in_dim(source, rep * ntr, ntr)
    lens = lengths[wanted]
    bnd = bounds[wanted]
    tgt = targets[wanted]
    nstep = bnd.shape[1]
    factor = (LOSS_SCALE / jnp.sum(lens).astype(F32)).reshape(1)

    def one_hot(ids, size):
        hot = ids[:, None] == jnp.arange(size, dtype=jnp.int32)[None, :]
        return jnp.concatenate([hot, jnp.zeros((16 - nstep, size), bool)], axis=0)

    picks = [one_hot(bnd[j], width).astype(BF16) for j in range(ntr)]
    hots = [one_hot(tgt[j], w_class.shape[1]).astype(F32) for j in range(ntr)]
    spans = [jnp.where(section_at == n, lens[0], lens[1]).reshape(1) for n in range(nst + 1)]
    flags = [(section_at == s).astype(jnp.int32).reshape(1) for s in range(nst)]
    masks = [section_at == s for s in range(nst)]
    half = peers // 2
    mine_at = (hi * half).astype(jnp.uint32)
    away_at = [((1 - hi) * half + n * half // 2).astype(jnp.uint32) for n in range(2)]
    block_at = tensor_at.astype(jnp.uint32)
    ours = core.astype(jnp.int32).reshape(1)
    theirs = 1 - ours

    def sum_of(got):
        return jnp.sum(got[:, :width].astype(F32), axis=0)

    kept = []
    arriving = None
    for turn in range(nst):
        cur = (begin if turn == 0 else first(turn)) if turn < ntr else jnp.zeros((width, dsh), BF16)
        if turn == 0:
            cur, factor, picks, hots, spans, flags, masks, mine_at, away_at, block_at, ours, theirs, w_class = together(
                cur, factor, picks, hots, spans, flags, masks, mine_at, away_at, block_at, ours, theirs, w_class
            )
        if arriving is not None:
            cur, arriving = together(cur, arriving)
            cur = jnp.where(masks[0], cur, arriving)
        x = gathered(cur)
        if turn == nst - 1:
            now = forward(spans[turn], x, weights, "both", picks[0], nstep)
        else:
            now = forward(spans[turn], x, weights)
        kept.append(now)
        blocks = now["part"]
        got = exchange(blocks)
        arriving = (cur.astype(F32) + sum_of(got)).astype(BF16)
        if turn == 0:
            away = [away[0], after(away[1], arriving)]
        leaving = arriving
        arriving = passed_along(arriving, "section", 1)

    def end_cotangent(which, got, x):
        return step_end_grad(factor, got, x, picks[which], w_class, hots[which], nstep)

    def own_block(blocks):
        return lax.dynamic_slice_in_dim(blocks, block_at, 1, axis=0)[0]

    def chosen(choices, at=None, count=None):
        if at is None:
            return by_section(masks, choices)
        return by_section(
            masks, [lax.dynamic_slice_in_dim(x, at, count, axis=0) for x in choices]
        )

    def not_before(choices, mark):
        return [after(x, mark) for x in choices]

    seen = lambda name, which: [kept[s + which][name] for s in range(nst)]
    back = lambda n, which: [taken[2 * nst - 1 - s + which][n] for s in range(nst)]

    pieces = {}

    def send_blocks(name, choices, n):
        pieces[f"{name}.{n}"] = mirrored(chosen(choices, away_at[n], half // 2), 2)

    def send_half(name, choices):
        pieces[name] = mirrored(chosen(choices, away_at[0], half), 2)

    def send_whole(name, choices):
        pieces[name] = swapped(chosen(choices), "dp", 2)

    taken = {}
    g_top = end_cotangent(0, got, x)
    grad = own_block(g_top)
    send_blocks("h0", not_before(seen("h", 0), leaving), 0)
    send_whole("o0", not_before(seen("o", 0), leaving))
    arriving, g_top, grad, pieces = together(arriving, g_top, grad, pieces)
    x = gathered(arriving)
    now = forward(spans[nst], x, weights, "ends", picks[1], nstep)
    d, dx = backward(
        jnp.zeros((1,), jnp.int32), g_top, kept[-1], kept[-1], weights, True, (now["part"],)
    )
    taken[nst] = (d, g_top)
    kept.append(now)
    got = exchange(dx)

    for turn in range(nst + 1, 2 * nst + 1):
        grad = (grad.astype(F32) + sum_of(got)).astype(BF16)
        leaving = grad
        if turn == nst + 1:
            g_top = end_cotangent(1, got, x)
            send_blocks("h0", not_before(seen("h", 0), grad), 1)
            send_whole("o1", not_before(seen("o", 1), grad))
        elif turn < 2 * nst:
            n = turn - nst - 2
            send_blocks("h1", not_before(seen("h", 1), grad), n)
        else:
            send_half("g0", not_before(back(1, 0), grad))
            send_whole("d0", not_before(back(0, 0), grad))
        held = [held_back(leaving)] if turn == nst + 1 else []
        grad, pieces, held = together(passed_along(grad, "section", -1), pieces, held)
        if turn == nst + 1:
            grad = jnp.where(masks[nst - 1], own_block(g_top), grad)
        g = gathered(grad)
        late = 2 * nst + 1 - turn
        early = max(late - 2, 0)
        flag = flags[late - 1]
        if turn < 2 * nst:
            d, dx = backward(flag, g, kept[early], kept[late], weights, True, (), held)
            taken[turn] = (d, g)
            got = exchange(dx)
        else:
            taken[turn] = (None, g)
            send_half("g1", back(1, 1))
            (d,) = backward(flag, g, kept[early], kept[late], weights, False)
            taken[turn] = (d, g)
            send_whole("d1", back(0, 1))

    def wide(name, choices):
        runs = []
        for w in range(ntr):
            runs.append((chosen(not_before(choices(w), g), mine_at, half),))
            names = (f"{name}{w}",) if name == "g" else (f"{name}{w}.0", f"{name}{w}.1")
            runs.append(tuple(pieces[n] for n in names))
        return runs

    def narrow(name, choices):
        out = []
        for w in range(ntr):
            out += [chosen(not_before(choices(w), g)), pieces[f"{name}{w}"]]
        return out

    qcol = weights[0].shape[1]
    all_o = (wide("g", lambda w: back(1, w)), narrow("o", lambda w: seen("o", w)), False)
    all_d = (wide("h", lambda w: seen("h", w)), narrow("d", lambda w: back(0, w)), True)
    cols_o, cols_d = (half // 2 * dsh,), (qcol, HEAD_DIM, HEAD_DIM)
    (give_o,) = weight_grad(theirs, *all_o, cols_o, BF16)
    given_o = swapped(give_o, "dp", 1)
    (give_d,) = weight_grad(theirs, *all_d, (sum(cols_d),), BF16)
    given_d = swapped(give_d, "dp", 1)
    (grad_o,) = weight_grad(ours, *all_o, cols_o, F32, (given_o,))
    grad_q, grad_k, grad_v = weight_grad(ours, *all_d, cols_d, F32, (given_d,))
    return (grad_q[None], grad_k[None], grad_v[None], grad_o[None])


def solution(mesh):
    placed = (
        P("dp", None, "tensor"),
        P(),
        P(),
        P(),
        P(),
        P("section", None, "tensor"),
        P("section", None, "tensor"),
        P("section", None, "tensor"),
        P("section", "tensor", None),
        P("tensor", None),
    )
    return jax.shard_map(
        on_device,
        mesh=mesh,
        in_specs=placed,
        out_specs=(
            P("section", "dp", "tensor"),
            P("section", "dp", "tensor"),
            P("section", "dp", "tensor"),
            P("section", "tensor", "dp"),
        ),
        check_vma=False,
    )
```

```python
import functools

import jax
import jax.numpy as jnp
from jax import lax
from jax.experimental import pallas as pl
from jax.experimental.pallas import tpu as pltpu
from jax.sharding import PartitionSpec as P

HEAD_DIM = 128
EPS = 1e-06
LOSS_SCALE = 16384.0
SCORE_SCALE = 1.0 / HEAD_DIM**0.5
F32 = jnp.float32
BF16 = jnp.bfloat16
VMEM_LIMIT = 16 * 1024 * 1024


def dot(a, b):
    return jnp.dot(a, b, preferred_element_type=F32)


def dot_nt(a, b):
    return lax.dot_general(a, b, (((1,), (1,)), ((), ())), preferred_element_type=F32)


def dot_tn(a, b):
    return lax.dot_general(a, b, (((0,), (0,)), ((), ())), preferred_element_type=F32)


def in_vmem():
    return pl.BlockSpec(memory_space=pltpu.VMEM)


def in_smem():
    return pl.BlockSpec(memory_space=pltpu.SMEM)


def anywhere():
    return pl.BlockSpec(memory_space=pl.ANY)


def kernel_params(limit):
    return pltpu.CompilerParams(vmem_limit_bytes=limit)


def heads_down(x, heads):
    return jnp.concatenate([x[:, n * HEAD_DIM : (n + 1) * HEAD_DIM] for n in range(heads)], axis=0)


def heads_across(x, heads):
    rows = x.shape[0] // heads
    return jnp.concatenate([x[n * rows : (n + 1) * rows] for n in range(heads)], axis=1)


def place_ends(ends_ref, block, rows, nstep):
    ends_ref[pl.ds(block * nstep, nstep), :] = rows[:nstep]


def forward_kernel(mode, nstep, len_ref, x_ref, wq_ref, wk_ref, wv_ref, wo_ref, *rest):
    if mode == "all":
        part_ref, h_ref, scale_ref, pack_ref, o_ref = rest
    else:
        pick_ref, part_ref, h_ref, scale_ref, pack_ref, o_ref, ends_ref = rest
    nblk, rows, dsh = x_ref.shape
    qh = wq_ref.shape[1] // HEAD_DIM
    sq = jnp.zeros((rows, 1), F32)
    for j in range(nblk):
        xf = x_ref[j].astype(F32)
        sq = sq + jnp.sum(xf * xf, axis=1, keepdims=True)
    scale = lax.rsqrt(sq / (nblk * dsh) + EPS)
    scale_ref[...] = jnp.broadcast_to(scale, scale_ref.shape)
    q = jnp.zeros((rows, wq_ref.shape[1]), F32)
    k = jnp.zeros((rows, HEAD_DIM), F32)
    v = jnp.zeros((rows, HEAD_DIM), F32)
    for j in range(nblk):
        h = (x_ref[j].astype(F32) * scale).astype(BF16)
        h_ref[j] = h
        at = pl.ds(j * dsh, dsh)
        q = q + dot(h, wq_ref[at, :])
        k = k + dot(h, wk_ref[at, :])
        v = v + dot(h, wv_ref[at, :])
    k = k.astype(BF16)
    v = v.astype(BF16)
    q = heads_down(q.astype(BF16), qh)
    top = qh * rows
    pack_ref[:top, :] = q
    pack_ref[pl.ds(2 * top, rows), :] = k
    pack_ref[pl.ds(2 * top + rows, rows), :] = v
    posq = lax.broadcasted_iota(jnp.int32, (rows, rows), 0)
    posk = lax.broadcasted_iota(jnp.int32, (rows, rows), 1)
    keep = ((posk <= posq) & (posk < len_ref[0])).astype(F32)
    expo = jnp.exp(dot_nt(q, k) * SCORE_SCALE) * jnp.concatenate([keep] * qh, axis=0)
    weights = (expo / jnp.sum(expo, axis=1, keepdims=True)).astype(BF16)
    pack_ref[pl.ds(top, top), :] = weights
    o_ref[...] = heads_across(dot(weights, v).astype(BF16), qh)
    o = o_ref[...]
    if mode != "all":
        picked = dot(pick_ref[...], o).astype(BF16)
        o = picked if mode == "ends" else jnp.concatenate([o, picked], axis=0)
    for j in range(nblk):
        part = dot(o, wo_ref[:, pl.ds(j * dsh, dsh)])
        if mode != "ends":
            part_ref[j, :rows] = part[:rows].astype(BF16)
        if mode != "all":
            place_ends(ends_ref, j, part[-pick_ref.shape[0] :], nstep)
    if mode == "ends":
        part_ref[...] = ends_ref[...].astype(BF16)
    elif mode == "both":
        for j in range(nblk):
            part_ref[j, rows:] = ends_ref[...].astype(BF16)


def forward(length, x, weights, mode="all", pick=None, nstep=0):
    nblk, rows, dsh = x.shape
    qcol = weights[0].shape[1]
    packed = 2 * qcol // HEAD_DIM * rows + 2 * rows
    nend = nblk * nstep
    part = {"all": x.shape, "both": (nblk, rows + nend, dsh), "ends": (nend, dsh)}[mode]
    outs = [(part, BF16), (x.shape, BF16)]
    outs += [((rows, HEAD_DIM), F32), ((packed, HEAD_DIM), BF16), ((rows, qcol), BF16)]
    more = [] if mode == "all" else [pick]
    out = pl.pallas_call(
        functools.partial(forward_kernel, mode, nstep),
        out_shape=tuple(jax.ShapeDtypeStruct(*one) for one in outs),
        in_specs=[in_smem()] + [in_vmem()] * (5 + len(more)),
        out_specs=tuple([in_vmem()] * 5),
        scratch_shapes=[pltpu.VMEM((nend, dsh), F32)] if more else [],
        compiler_params=kernel_params(VMEM_LIMIT),
        cost_estimate=pl.CostEstimate(
            flops=2 * rows * nblk * dsh * (2 * qcol + 2 * HEAD_DIM),
            bytes_accessed=4 * nblk * dsh * (qcol + HEAD_DIM),
            transcendentals=rows * rows * qcol // HEAD_DIM,
        ),
        name="forward_layer",
    )(length, x, *weights, *more)
    return dict(zip(("part", "h", "scale", "pack", "o"), out))


def step_end_kernel(nstep, factor_ref, got_ref, x_ref, pick_ref, class_ref, hot_ref, out_ref, sum_ref, row_ref):
    nblk, rows, dsh = x_ref.shape
    width = nblk * dsh
    nend = nblk * nstep
    parts = jnp.zeros((nend, dsh), F32)
    for j in range(nblk):
        parts = parts + got_ref[j, rows:].astype(F32)
    sum_ref[...] = parts
    npad = pick_ref.shape[0]
    row_ref[...] = jnp.zeros(row_ref.shape, F32)
    zeta = jnp.zeros((npad, class_ref.shape[1]), F32)
    sumsq = jnp.zeros((npad, 1), F32)
    for j in range(nblk):
        row_ref[j, :nstep] = sum_ref[pl.ds(j * nstep, nstep), :]
        full = (dot(pick_ref[...], x_ref[j]) + row_ref[j]).astype(BF16)
        ff = full.astype(F32)
        row_ref[j] = ff
        zeta = zeta + dot(full, class_ref[pl.ds(j * dsh, dsh), :])
        sumsq = sumsq + jnp.sum(ff * ff, axis=1, keepdims=True)
    rstd = lax.rsqrt(sumsq / width + EPS)
    expo = jnp.exp(zeta * rstd)
    prob = expo / jnp.sum(expo, axis=1, keepdims=True)
    dlog = factor_ref[0] * (prob - hot_ref[...])
    dzeta = dlog * rstd
    dmean = jnp.sum(dlog * zeta, axis=1, keepdims=True) * -0.5 * rstd * rstd * rstd
    high = dzeta.astype(BF16)
    mid = (dzeta - high.astype(F32)).astype(BF16)
    low = (dzeta - high.astype(F32) - mid.astype(F32)).astype(BF16)
    terms = jnp.concatenate([high, mid, low], axis=0)
    for j in range(nblk):
        head = class_ref[pl.ds(j * dsh, dsh), :]
        back = dot_nt(terms, head)
        back = back[:npad] + (back[npad : 2 * npad] + back[2 * npad :])
        back = (back + dmean * 2.0 * row_ref[j] / width).astype(BF16)
        out_ref[j] = dot_tn(pick_ref[...], back).astype(BF16)


def step_end_grad(factor, got, x, pick, w_class, hot, nstep):
    nblk, rows, dsh = x.shape
    return pl.pallas_call(
        functools.partial(step_end_kernel, nstep),
        out_shape=jax.ShapeDtypeStruct(x.shape, BF16),
        in_specs=[in_smem()] + [in_vmem()] * 5,
        out_specs=in_vmem(),
        scratch_shapes=[
            pltpu.VMEM((nblk * nstep, dsh), F32),
            pltpu.VMEM((nblk, pick.shape[0], dsh), F32),
        ],
        compiler_params=kernel_params(VMEM_LIMIT),
        cost_estimate=pl.CostEstimate(
            flops=16 * rows * nblk * dsh * pick.shape[0], bytes_accessed=4 * rows * nblk * dsh,
            transcendentals=0,
        ),
        name="step_end_grad",
    )(factor, got, x, pick, w_class, hot)


def backward_kernel(
    with_input, with_ends, nheld, flag_ref, g_ref, pack0_ref, pack1_ref, h0_ref, h1_ref,
    scale0_ref, scale1_ref, wq_ref, wk_ref, wv_ref, wo_ref, *rest
):
    rest = rest[nheld:]
    if with_ends:
        ends_ref, rest = rest[0], rest[1:]
    if with_input:
        d_ref, dx_ref, pack_ref, keep_sems, h_ref, scale_ref, dh_ref = rest
    else:
        d_ref, pack_ref, keep_sems = rest
    nblk, rows, dsh = g_ref.shape
    qcol = wq_ref.shape[1]
    qh = qcol // HEAD_DIM
    top = qh * rows
    pairs = [(pack0_ref, pack1_ref, pack_ref)]
    if with_input:
        pairs += [(h0_ref, h1_ref, h_ref), (scale0_ref, scale1_ref, scale_ref)]
    for at, (one, two, to) in enumerate(pairs):

        @pl.when(flag_ref[0] == 0)
        def _(one=one, to=to, at=at):
            pltpu.make_async_copy(one, to, keep_sems.at[at]).start()

        @pl.when(flag_ref[0] != 0)
        def _(two=two, to=to, at=at):
            pltpu.make_async_copy(two, to, keep_sems.at[at]).start()

    do = jnp.zeros((rows, qcol), F32)
    for j in range(nblk):
        do = do + dot_nt(g_ref[j], wo_ref[:, pl.ds(j * dsh, dsh)])
    do = do.astype(BF16)
    pltpu.make_async_copy(pack0_ref, pack_ref, keep_sems.at[0]).wait()
    k = pack_ref[pl.ds(2 * top, rows), :]
    v = pack_ref[pl.ds(2 * top + rows, rows), :]
    do = heads_down(do, qh)
    weights = pack_ref[pl.ds(top, top), :]
    wf = weights.astype(F32)
    dw = dot_nt(do, v)
    ds = wf * (dw - jnp.sum(dw * wf, axis=1, keepdims=True)) * SCORE_SCALE
    ds = ds.astype(BF16)
    dk = dot_tn(ds, pack_ref[:top, :])
    dv = dot_tn(weights, do)
    d_ref[:, :qcol] = heads_across(dot(ds, k).astype(BF16), qh)
    d_ref[:, qcol : qcol + HEAD_DIM] = dk.astype(BF16)
    d_ref[:, qcol + HEAD_DIM :] = dv.astype(BF16)
    if not with_input:
        return
    pltpu.make_async_copy(h0_ref, h_ref, keep_sems.at[1]).wait()
    pltpu.make_async_copy(scale0_ref, scale_ref, keep_sems.at[2]).wait()
    dq = d_ref[:, :qcol]
    dk = dk.astype(BF16)
    dv = dv.astype(BF16)
    inner = jnp.zeros((rows, 1), F32)
    for j in range(nblk):
        at = pl.ds(j * dsh, dsh)
        dh = dot_nt(dq, wq_ref[at, :]) + dot_nt(dk, wk_ref[at, :]) + dot_nt(dv, wv_ref[at, :])
        dh_ref[j] = dh
        inner = inner + jnp.sum(dh * h_ref[j].astype(F32), axis=1, keepdims=True)
    inner = inner / (nblk * dsh)
    scale = scale_ref[:, :1]
    for j in range(nblk):
        dx_ref[j, :rows] = (scale * (dh_ref[j] - h_ref[j].astype(F32) * inner)).astype(BF16)
        if with_ends:
            dx_ref[j, rows:] = ends_ref[...]


def backward(flag, g, one, two, weights, with_input, ends=(), held=()):
    nblk, rows, dsh = g.shape
    wq, wk, wv, wo = weights
    qcol = wq.shape[1]
    out_shape = [jax.ShapeDtypeStruct((rows, qcol + 2 * HEAD_DIM), BF16)]
    scratch = [pltpu.VMEM(one["pack"].shape, BF16), pltpu.SemaphoreType.DMA((3,))]
    if with_input:
        below = sum(x.shape[0] for x in ends)
        out_shape.append(jax.ShapeDtypeStruct((nblk, rows + below, dsh), BF16))
        scratch += [
            pltpu.VMEM(g.shape, BF16),
            pltpu.VMEM(one["scale"].shape, F32),
            pltpu.VMEM(g.shape, F32),
        ]
    return pl.pallas_call(
        functools.partial(backward_kernel, with_input, bool(ends), len(held)),
        out_shape=tuple(out_shape),
        in_specs=[in_smem(), in_vmem()]
        + [anywhere()] * 6
        + [in_vmem()] * 4
        + [anywhere()] * len(held)
        + [in_vmem()] * len(ends),
        out_specs=tuple([in_vmem()] * len(out_shape)),
        scratch_shapes=scratch,
        compiler_params=kernel_params(VMEM_LIMIT),
        cost_estimate=pl.CostEstimate(
            flops=2 * rows * nblk * dsh * (2 * qcol + 2 * HEAD_DIM) if with_input else 1,
            bytes_accessed=4 * nblk * dsh * (qcol + HEAD_DIM) if with_input else 1,
            transcendentals=0,
        ),
        name="backward_layer" if with_input else "backward_heads",
    )(
        flag, g, one["pack"], two["pack"], one["h"], two["h"],
        one["scale"], two["scale"], wq, wk, wv, wo, *held, *ends,
    )


def weight_grad_kernel(wide_first, runs, nnarrow, splits, quarter_ref, *refs):
    nwide, nout = sum(runs), len(splits)
    wides, narrows = refs[:nwide], refs[nwide : nwide + nnarrow]
    given, outs = refs[nwide + nnarrow : -nout - 2], refs[-nout - 2 : -2]
    wide_all, narrow_all = refs[-2:]
    quarter = quarter_ref[0]
    at = 0
    for i, n in enumerate(runs):
        run = wides[at : at + n]
        at += n
        rows, dsh = run[0].shape[1:]
        here = pl.ds(i * rows, rows)
        if n == 1:
            half = run[0].shape[0] // 2
            for b in range(half):
                wide_all[here, pl.ds(b * dsh, dsh)] = run[0][quarter * half + b]
        for which, piece in enumerate(run if n > 1 else ()):

            @pl.when(quarter == which)
            def _(piece=piece):
                for b in range(piece.shape[0]):
                    wide_all[here, pl.ds(b * dsh, dsh)] = piece[b]

    rows = narrows[0].shape[0]
    for i, piece in enumerate(narrows):
        narrow_all[pl.ds(i * rows, rows), :] = piece[...]
    for c in range(outs[0].shape[0] // 256):
        cols = pl.ds(c * 256, 256)
        if wide_first:
            got = dot_tn(wide_all[:, cols], narrow_all[...])
        else:
            got = dot_tn(narrow_all[:, cols], wide_all[...])
        for more in given:
            got = got + more[cols, :].astype(F32)
        for out_ref, (start, stop) in zip(outs, splits):
            out_ref[cols, :] = got[:, start:stop].astype(out_ref.dtype)


def weight_grad(quarter, wide, narrow, wide_first, widths, dtype, given=()):
    rows, cols = narrow[0].shape
    dsh = wide[0][0].shape[2]
    width = sum(x.shape[0] for x in wide[0]) * dsh // 2
    height = width if wide_first else cols
    total = len(narrow) * rows
    flat = [x for run in wide for x in run]
    splits = [(sum(widths[:i]), sum(widths[: i + 1])) for i in range(len(widths))]
    runs = tuple(len(run) for run in wide)
    return pl.pallas_call(
        functools.partial(weight_grad_kernel, wide_first, runs, len(narrow), tuple(splits)),
        out_shape=tuple(jax.ShapeDtypeStruct((height, w), dtype) for w in widths),
        in_specs=[in_smem()] + [in_vmem()] * (len(flat) + len(narrow) + len(given)),
        out_specs=tuple([in_vmem()] * len(widths)),
        scratch_shapes=[pltpu.VMEM((total, width), BF16), pltpu.VMEM((total, cols), BF16)],
        compiler_params=kernel_params(VMEM_LIMIT),
        cost_estimate=pl.CostEstimate(flops=1, bytes_accessed=1, transcendentals=0),
        name="weight_grad",
    )(quarter, *flat, *narrow, *given)


def passed_along(x, axis, by):
    peers = lax.axis_size(axis)
    pairs = [(i, i + by) for i in range(peers) if 0 <= i + by < peers]
    return lax.ppermute(x, axis, pairs)


def swapped(x, axis, mask):
    return lax.ppermute(x, axis, [(i, i ^ mask) for i in range(lax.axis_size(axis))])


def mirrored(x, mask):
    ndp, peers = lax.axis_size("dp"), lax.axis_size("tensor")
    to = lambda p, r: (p ^ mask) * peers + (r + peers // 2) % peers
    pairs = [(p * peers + r, to(p, r)) for p in range(ndp) for r in range(peers)]
    return lax.ppermute(x, ("dp", "tensor"), pairs)


def held_back(x):
    return lax.ppermute(x[:16, :128], "dp", [(i, i + 1) for i in range(0, lax.axis_size("dp"), 2)])


def exchange(blocks):
    return lax.all_to_all(blocks, "tensor", split_axis=0, concat_axis=0, tiled=True)


def gathered(cur):
    return exchange(jnp.broadcast_to(cur[None], (lax.axis_size("tensor"),) + cur.shape))


def by_section(masks, choices):
    out = choices[-1]
    for mask, choice in zip(masks, choices[:-1]):
        out = jnp.where(mask, choice, out)
    return out


def after(x, *marks):
    return lax.optimization_barrier((x,) + marks)[0]


def together(*xs):
    return lax.optimization_barrier(xs)


def on_device(embeds, source, lengths, bounds, targets, w_query, w_key, w_value, w_out, w_class):
    nst = lax.axis_size("section")
    peers = lax.axis_size("tensor")
    rep = lax.axis_index("dp")
    section_at = lax.axis_index("section")
    tensor_at = lax.axis_index("tensor")
    ntr, width, dsh = embeds.shape
    weights = (w_query[0], w_key[0], w_value[0], w_out[0])
    w_class = gathered(w_class).reshape(peers * w_class.shape[0], w_class.shape[1])

    hi, core = rep // 2, rep % 2
    slots = source.reshape(2, 2, ntr) - rep * ntr

    def mine_for(col):
        owner = lax.dynamic_slice_in_dim(slots, col, 1, axis=1)[:, 0]
        out = jnp.zeros((2, ntr, width, dsh), BF16)
        for n in range(ntr):
            out = jnp.where((owner == n)[:, :, None, None], embeds[n][None, None], out)
        return out

    both = mine_for(core) + swapped(mine_for(1 - core), "dp", 1)
    own = lax.dynamic_slice_in_dim(both, hi, 1, axis=0)[0]
    away = lax.dynamic_slice_in_dim(both, 1 - hi, 1, axis=0)[0]
    taken_here = own + swapped(away, "dp", 2)
    source, lengths, bounds, targets, taken_here = together(
        source, lengths, bounds, targets, taken_here
    )
    wanted = lax.dynamic_slice_in_dim(source, rep * ntr, ntr)
    lens = lengths[wanted]
    bnd = bounds[wanted]
    tgt = targets[wanted]
    nstep = bnd.shape[1]
    factor = (LOSS_SCALE / jnp.sum(lens).astype(F32)).reshape(1)

    def one_hot(ids, size):
        hot = ids[:, None] == jnp.arange(size, dtype=jnp.int32)[None, :]
        return jnp.concatenate([hot, jnp.zeros((16 - nstep, size), bool)], axis=0)

    picks = [one_hot(bnd[j], width).astype(BF16) for j in range(ntr)]
    hots = [one_hot(tgt[j], w_class.shape[1]).astype(F32) for j in range(ntr)]
    spans = [jnp.where(section_at == n, lens[0], lens[1]).reshape(1) for n in range(nst + 1)]
    flags = [(section_at == s).astype(jnp.int32).reshape(1) for s in range(nst)]
    masks = [section_at == s for s in range(nst)]
    half = peers // 2
    mine_at = (hi * half).astype(jnp.uint32)
    away_at = [((1 - hi) * half + n * half // 2).astype(jnp.uint32) for n in range(2)]
    block_at = tensor_at.astype(jnp.uint32)
    ours = core.astype(jnp.int32).reshape(1)
    theirs = 1 - ours

    def sum_of(got):
        return jnp.sum(got[:, :width].astype(F32), axis=0)

    kept = []
    arriving = None
    for turn in range(nst):
        cur = taken_here[turn] if turn < ntr else jnp.zeros((width, dsh), BF16)
        if turn == 0:
            cur, factor, picks, hots, spans, flags, masks, mine_at, away_at, block_at, ours, theirs, w_class = together(
                cur, factor, picks, hots, spans, flags, masks, mine_at, away_at, block_at, ours, theirs, w_class
            )
        if arriving is not None:
            cur, arriving = together(cur, arriving)
            cur = jnp.where(masks[0], cur, arriving)
        x = gathered(cur)
        if turn == nst - 1:
            now = forward(spans[turn], x, weights, "both", picks[0], nstep)
        else:
            now = forward(spans[turn], x, weights)
        kept.append(now)
        blocks = now["part"]
        got = exchange(blocks)
        arriving = (cur.astype(F32) + sum_of(got)).astype(BF16)
        leaving = arriving
        arriving = passed_along(arriving, "section", 1)

    def end_cotangent(which, got, x):
        return step_end_grad(factor, got, x, picks[which], w_class, hots[which], nstep)

    def own_block(blocks):
        return lax.dynamic_slice_in_dim(blocks, block_at, 1, axis=0)[0]

    def chosen(choices, at=None, count=None):
        if at is None:
            return by_section(masks, choices)
        return by_section(
            masks, [lax.dynamic_slice_in_dim(x, at, count, axis=0) for x in choices]
        )

    def not_before(choices, mark):
        return [after(x, mark) for x in choices]

    seen = lambda name, which: [kept[s + which][name] for s in range(nst)]
    back = lambda n, which: [taken[2 * nst - 1 - s + which][n] for s in range(nst)]

    pieces = {}

    def send_blocks(name, choices, n):
        pieces[f"{name}.{n}"] = mirrored(chosen(choices, away_at[n], half // 2), 2)

    def send_half(name, choices):
        pieces[name] = mirrored(chosen(choices, away_at[0], half), 2)

    def send_whole(name, choices):
        pieces[name] = swapped(chosen(choices), "dp", 2)

    taken = {}
    g_top = end_cotangent(0, got, x)
    grad = own_block(g_top)
    send_blocks("h0", not_before(seen("h", 0), leaving), 0)
    send_whole("o0", not_before(seen("o", 0), leaving))
    arriving, g_top, grad, pieces = together(arriving, g_top, grad, pieces)
    x = gathered(arriving)
    now = forward(spans[nst], x, weights, "ends", picks[1], nstep)
    d, dx = backward(
        jnp.zeros((1,), jnp.int32), g_top, kept[-1], kept[-1], weights, True, (now["part"],)
    )
    taken[nst] = (d, g_top)
    kept.append(now)
    got = exchange(dx)

    for turn in range(nst + 1, 2 * nst + 1):
        grad = (grad.astype(F32) + sum_of(got)).astype(BF16)
        leaving = grad
        if turn == nst + 1:
            g_top = end_cotangent(1, got, x)
            send_blocks("h0", not_before(seen("h", 0), grad), 1)
            send_whole("o1", not_before(seen("o", 1), grad))
        elif turn < 2 * nst:
            n = turn - nst - 2
            send_blocks("h1", not_before(seen("h", 1), grad), n)
        else:
            send_half("g0", not_before(back(1, 0), grad))
            send_whole("d0", not_before(back(0, 0), grad))
        held = [held_back(leaving)] if turn == nst + 1 else []
        grad, pieces, held = together(passed_along(grad, "section", -1), pieces, held)
        if turn == nst + 1:
            grad = jnp.where(masks[nst - 1], own_block(g_top), grad)
        g = gathered(grad)
        late = 2 * nst + 1 - turn
        early = max(late - 2, 0)
        flag = flags[late - 1]
        if turn < 2 * nst:
            d, dx = backward(flag, g, kept[early], kept[late], weights, True, (), held)
            taken[turn] = (d, g)
            got = exchange(dx)
        else:
            taken[turn] = (None, g)
            send_half("g1", back(1, 1))
            (d,) = backward(flag, g, kept[early], kept[late], weights, False)
            taken[turn] = (d, g)
            send_whole("d1", back(0, 1))

    def wide(name, choices):
        runs = []
        for w in range(ntr):
            runs.append((chosen(not_before(choices(w), g), mine_at, half),))
            names = (f"{name}{w}",) if name == "g" else (f"{name}{w}.0", f"{name}{w}.1")
            runs.append(tuple(pieces[n] for n in names))
        return runs

    def narrow(name, choices):
        out = []
        for w in range(ntr):
            out += [chosen(not_before(choices(w), g)), pieces[f"{name}{w}"]]
        return out

    qcol = weights[0].shape[1]
    all_o = (wide("g", lambda w: back(1, w)), narrow("o", lambda w: seen("o", w)), False)
    all_d = (wide("h", lambda w: seen("h", w)), narrow("d", lambda w: back(0, w)), True)
    cols_o, cols_d = (half // 2 * dsh,), (qcol, HEAD_DIM, HEAD_DIM)
    (give_o,) = weight_grad(theirs, *all_o, cols_o, BF16)
    given_o = swapped(give_o, "dp", 1)
    (give_d,) = weight_grad(theirs, *all_d, (sum(cols_d),), BF16)
    given_d = swapped(give_d, "dp", 1)
    (grad_o,) = weight_grad(ours, *all_o, cols_o, F32, (given_o,))
    grad_q, grad_k, grad_v = weight_grad(ours, *all_d, cols_d, F32, (given_d,))
    return (grad_q[None], grad_k[None], grad_v[None], grad_o[None])


def solution(mesh):
    placed = (
        P("dp", None, "tensor"),
        P(),
        P(),
        P(),
        P(),
        P("section", None, "tensor"),
        P("section", None, "tensor"),
        P("section", None, "tensor"),
        P("section", "tensor", None),
        P("tensor", None),
    )
    return jax.shard_map(
        on_device,
        mesh=mesh,
        in_specs=placed,
        out_specs=(
            P("section", "dp", "tensor"),
            P("section", "dp", "tensor"),
            P("section", "dp", "tensor"),
            P("section", "tensor", "dp"),
        ),
        check_vma=False,
    )
```

```python
import functools

import jax
import jax.numpy as jnp
from jax import lax
from jax.experimental import pallas as pl
from jax.experimental.pallas import tpu as pltpu
from jax.sharding import PartitionSpec as P

HEAD_DIM = 128
EPS = 1e-06
LOSS_SCALE = 16384.0
SCORE_SCALE = 1.0 / HEAD_DIM**0.5
F32 = jnp.float32
BF16 = jnp.bfloat16
VMEM_LIMIT = 16 * 1024 * 1024


def dot(a, b):
    return jnp.dot(a, b, preferred_element_type=F32)


def dot_nt(a, b):
    return lax.dot_general(a, b, (((1,), (1,)), ((), ())), preferred_element_type=F32)


def dot_tn(a, b):
    return lax.dot_general(a, b, (((0,), (0,)), ((), ())), preferred_element_type=F32)


def in_vmem():
    return pl.BlockSpec(memory_space=pltpu.VMEM)


def in_smem():
    return pl.BlockSpec(memory_space=pltpu.SMEM)


def anywhere():
    return pl.BlockSpec(memory_space=pl.ANY)


def kernel_params(limit):
    return pltpu.CompilerParams(vmem_limit_bytes=limit)


def heads_down(x, heads):
    return jnp.concatenate([x[:, n * HEAD_DIM : (n + 1) * HEAD_DIM] for n in range(heads)], axis=0)


def heads_across(x, heads):
    rows = x.shape[0] // heads
    return jnp.concatenate([x[n * rows : (n + 1) * rows] for n in range(heads)], axis=1)


def place_ends(ends_ref, block, rows, nstep):
    ends_ref[pl.ds(block * nstep, nstep), :] = rows[:nstep]


def forward_kernel(mode, nstep, len_ref, x_ref, wq_ref, wk_ref, wv_ref, wo_ref, *rest):
    if mode == "all":
        part_ref, h_ref, scale_ref, pack_ref, o_ref = rest
    else:
        pick_ref, part_ref, h_ref, scale_ref, pack_ref, o_ref, ends_ref = rest
    nblk, rows, dsh = x_ref.shape
    qh = wq_ref.shape[1] // HEAD_DIM
    sq = jnp.zeros((rows, 1), F32)
    for j in range(nblk):
        xf = x_ref[j].astype(F32)
        sq = sq + jnp.sum(xf * xf, axis=1, keepdims=True)
    scale = lax.rsqrt(sq / (nblk * dsh) + EPS)
    scale_ref[...] = jnp.broadcast_to(scale, scale_ref.shape)
    q = jnp.zeros((rows, wq_ref.shape[1]), F32)
    k = jnp.zeros((rows, HEAD_DIM), F32)
    v = jnp.zeros((rows, HEAD_DIM), F32)
    for j in range(nblk):
        h = (x_ref[j].astype(F32) * scale).astype(BF16)
        h_ref[j] = h
        at = pl.ds(j * dsh, dsh)
        q = q + dot(h, wq_ref[at, :])
        k = k + dot(h, wk_ref[at, :])
        v = v + dot(h, wv_ref[at, :])
    k = k.astype(BF16)
    v = v.astype(BF16)
    q = heads_down(q.astype(BF16), qh)
    top = qh * rows
    pack_ref[:top, :] = q
    pack_ref[pl.ds(2 * top, rows), :] = k
    pack_ref[pl.ds(2 * top + rows, rows), :] = v
    posq = lax.broadcasted_iota(jnp.int32, (rows, rows), 0)
    posk = lax.broadcasted_iota(jnp.int32, (rows, rows), 1)
    keep = ((posk <= posq) & (posk < len_ref[0])).astype(F32)
    expo = jnp.exp(dot_nt(q, k) * SCORE_SCALE) * jnp.concatenate([keep] * qh, axis=0)
    weights = (expo / jnp.sum(expo, axis=1, keepdims=True)).astype(BF16)
    pack_ref[pl.ds(top, top), :] = weights
    o_ref[...] = heads_across(dot(weights, v).astype(BF16), qh)
    o = o_ref[...]
    if mode != "all":
        picked = dot(pick_ref[...], o).astype(BF16)
        o = picked if mode == "ends" else jnp.concatenate([o, picked], axis=0)
    for j in range(nblk):
        part = dot(o, wo_ref[:, pl.ds(j * dsh, dsh)])
        if mode != "ends":
            part_ref[j, :rows] = part[:rows].astype(BF16)
        if mode != "all":
            place_ends(ends_ref, j, part[-pick_ref.shape[0] :], nstep)
    if mode == "ends":
        part_ref[...] = ends_ref[...].astype(BF16)
    elif mode == "both":
        for j in range(nblk):
            part_ref[j, rows:] = ends_ref[...].astype(BF16)


def forward(length, x, weights, mode="all", pick=None, nstep=0):
    nblk, rows, dsh = x.shape
    qcol = weights[0].shape[1]
    packed = 2 * qcol // HEAD_DIM * rows + 2 * rows
    nend = nblk * nstep
    part = {"all": x.shape, "both": (nblk, rows + nend, dsh), "ends": (nend, dsh)}[mode]
    outs = [(part, BF16), (x.shape, BF16)]
    outs += [((rows, HEAD_DIM), F32), ((packed, HEAD_DIM), BF16), ((rows, qcol), BF16)]
    more = [] if mode == "all" else [pick]
    out = pl.pallas_call(
        functools.partial(forward_kernel, mode, nstep),
        out_shape=tuple(jax.ShapeDtypeStruct(*one) for one in outs),
        in_specs=[in_smem()] + [in_vmem()] * (5 + len(more)),
        out_specs=tuple([in_vmem()] * 5),
        scratch_shapes=[pltpu.VMEM((nend, dsh), F32)] if more else [],
        compiler_params=kernel_params(VMEM_LIMIT),
        cost_estimate=pl.CostEstimate(
            flops=2 * rows * nblk * dsh * (2 * qcol + 2 * HEAD_DIM),
            bytes_accessed=4 * nblk * dsh * (qcol + HEAD_DIM),
            transcendentals=rows * rows * qcol // HEAD_DIM,
        ),
        name="forward_layer",
    )(length, x, *weights, *more)
    return dict(zip(("part", "h", "scale", "pack", "o"), out))


def step_end_kernel(nstep, factor_ref, got_ref, x_ref, pick_ref, class_ref, hot_ref, out_ref, sum_ref, row_ref):
    nblk, rows, dsh = x_ref.shape
    width = nblk * dsh
    nend = nblk * nstep
    parts = jnp.zeros((nend, dsh), F32)
    for j in range(nblk):
        parts = parts + got_ref[j, rows:].astype(F32)
    sum_ref[...] = parts
    npad = pick_ref.shape[0]
    row_ref[...] = jnp.zeros(row_ref.shape, F32)
    zeta = jnp.zeros((npad, class_ref.shape[1]), F32)
    sumsq = jnp.zeros((npad, 1), F32)
    for j in range(nblk):
        row_ref[j, :nstep] = sum_ref[pl.ds(j * nstep, nstep), :]
        full = (dot(pick_ref[...], x_ref[j]) + row_ref[j]).astype(BF16)
        ff = full.astype(F32)
        row_ref[j] = ff
        zeta = zeta + dot(full, class_ref[pl.ds(j * dsh, dsh), :])
        sumsq = sumsq + jnp.sum(ff * ff, axis=1, keepdims=True)
    rstd = lax.rsqrt(sumsq / width + EPS)
    expo = jnp.exp(zeta * rstd)
    prob = expo / jnp.sum(expo, axis=1, keepdims=True)
    dlog = factor_ref[0] * (prob - hot_ref[...])
    dzeta = dlog * rstd
    dmean = jnp.sum(dlog * zeta, axis=1, keepdims=True) * -0.5 * rstd * rstd * rstd
    high = dzeta.astype(BF16)
    mid = (dzeta - high.astype(F32)).astype(BF16)
    low = (dzeta - high.astype(F32) - mid.astype(F32)).astype(BF16)
    terms = jnp.concatenate([high, mid, low], axis=0)
    for j in range(nblk):
        head = class_ref[pl.ds(j * dsh, dsh), :]
        back = dot_nt(terms, head)
        back = back[:npad] + (back[npad : 2 * npad] + back[2 * npad :])
        back = (back + dmean * 2.0 * row_ref[j] / width).astype(BF16)
        out_ref[j] = dot_tn(pick_ref[...], back).astype(BF16)


def step_end_grad(factor, got, x, pick, w_class, hot, nstep):
    nblk, rows, dsh = x.shape
    return pl.pallas_call(
        functools.partial(step_end_kernel, nstep),
        out_shape=jax.ShapeDtypeStruct(x.shape, BF16),
        in_specs=[in_smem()] + [in_vmem()] * 5,
        out_specs=in_vmem(),
        scratch_shapes=[
            pltpu.VMEM((nblk * nstep, dsh), F32),
            pltpu.VMEM((nblk, pick.shape[0], dsh), F32),
        ],
        compiler_params=kernel_params(VMEM_LIMIT),
        cost_estimate=pl.CostEstimate(
            flops=16 * rows * nblk * dsh * pick.shape[0], bytes_accessed=4 * rows * nblk * dsh,
            transcendentals=0,
        ),
        name="step_end_grad",
    )(factor, got, x, pick, w_class, hot)


def backward_kernel(
    with_input, with_ends, nheld, flag_ref, g_ref, pack0_ref, pack1_ref, h0_ref, h1_ref,
    scale0_ref, scale1_ref, wq_ref, wk_ref, wv_ref, wo_ref, *rest
):
    rest = rest[nheld:]
    if with_ends:
        ends_ref, rest = rest[0], rest[1:]
    if with_input:
        d_ref, dx_ref, pack_ref, keep_sems, h_ref, scale_ref, dh_ref = rest
    else:
        d_ref, pack_ref, keep_sems = rest
    nblk, rows, dsh = g_ref.shape
    qcol = wq_ref.shape[1]
    qh = qcol // HEAD_DIM
    top = qh * rows
    pairs = [(pack0_ref, pack1_ref, pack_ref)]
    if with_input:
        pairs += [(h0_ref, h1_ref, h_ref), (scale0_ref, scale1_ref, scale_ref)]
    for at, (one, two, to) in enumerate(pairs):

        @pl.when(flag_ref[0] == 0)
        def _(one=one, to=to, at=at):
            pltpu.make_async_copy(one, to, keep_sems.at[at]).start()

        @pl.when(flag_ref[0] != 0)
        def _(two=two, to=to, at=at):
            pltpu.make_async_copy(two, to, keep_sems.at[at]).start()

    do = jnp.zeros((rows, qcol), F32)
    for j in range(nblk):
        do = do + dot_nt(g_ref[j], wo_ref[:, pl.ds(j * dsh, dsh)])
    do = do.astype(BF16)
    pltpu.make_async_copy(pack0_ref, pack_ref, keep_sems.at[0]).wait()
    k = pack_ref[pl.ds(2 * top, rows), :]
    v = pack_ref[pl.ds(2 * top + rows, rows), :]
    do = heads_down(do, qh)
    weights = pack_ref[pl.ds(top, top), :]
    wf = weights.astype(F32)
    dw = dot_nt(do, v)
    ds = wf * (dw - jnp.sum(dw * wf, axis=1, keepdims=True)) * SCORE_SCALE
    ds = ds.astype(BF16)
    dk = dot_tn(ds, pack_ref[:top, :])
    dv = dot_tn(weights, do)
    d_ref[:, :qcol] = heads_across(dot(ds, k).astype(BF16), qh)
    d_ref[:, qcol : qcol + HEAD_DIM] = dk.astype(BF16)
    d_ref[:, qcol + HEAD_DIM :] = dv.astype(BF16)
    if not with_input:
        return
    pltpu.make_async_copy(h0_ref, h_ref, keep_sems.at[1]).wait()
    pltpu.make_async_copy(scale0_ref, scale_ref, keep_sems.at[2]).wait()
    dq = d_ref[:, :qcol]
    dk = dk.astype(BF16)
    dv = dv.astype(BF16)
    inner = jnp.zeros((rows, 1), F32)
    for j in range(nblk):
        at = pl.ds(j * dsh, dsh)
        dh = dot_nt(dq, wq_ref[at, :]) + dot_nt(dk, wk_ref[at, :]) + dot_nt(dv, wv_ref[at, :])
        dh_ref[j] = dh
        inner = inner + jnp.sum(dh * h_ref[j].astype(F32), axis=1, keepdims=True)
    inner = inner / (nblk * dsh)
    scale = scale_ref[:, :1]
    for j in range(nblk):
        dx_ref[j, :rows] = (scale * (dh_ref[j] - h_ref[j].astype(F32) * inner)).astype(BF16)
        if with_ends:
            dx_ref[j, rows:] = ends_ref[...]


def backward(flag, g, one, two, weights, with_input, ends=(), held=()):
    nblk, rows, dsh = g.shape
    wq, wk, wv, wo = weights
    qcol = wq.shape[1]
    out_shape = [jax.ShapeDtypeStruct((rows, qcol + 2 * HEAD_DIM), BF16)]
    scratch = [pltpu.VMEM(one["pack"].shape, BF16), pltpu.SemaphoreType.DMA((3,))]
    if with_input:
        below = sum(x.shape[0] for x in ends)
        out_shape.append(jax.ShapeDtypeStruct((nblk, rows + below, dsh), BF16))
        scratch += [
            pltpu.VMEM(g.shape, BF16),
            pltpu.VMEM(one["scale"].shape, F32),
            pltpu.VMEM(g.shape, F32),
        ]
    return pl.pallas_call(
        functools.partial(backward_kernel, with_input, bool(ends), len(held)),
        out_shape=tuple(out_shape),
        in_specs=[in_smem(), in_vmem()]
        + [anywhere()] * 6
        + [in_vmem()] * 4
        + [anywhere()] * len(held)
        + [in_vmem()] * len(ends),
        out_specs=tuple([in_vmem()] * len(out_shape)),
        scratch_shapes=scratch,
        compiler_params=kernel_params(VMEM_LIMIT),
        cost_estimate=pl.CostEstimate(
            flops=2 * rows * nblk * dsh * (2 * qcol + 2 * HEAD_DIM) if with_input else 1,
            bytes_accessed=4 * nblk * dsh * (qcol + HEAD_DIM) if with_input else 1,
            transcendentals=0,
        ),
        name="backward_layer" if with_input else "backward_heads",
    )(
        flag, g, one["pack"], two["pack"], one["h"], two["h"],
        one["scale"], two["scale"], wq, wk, wv, wo, *held, *ends,
    )


def weight_grad_kernel(wide_first, runs, nnarrow, splits, outs_dtype, quarter_ref, *refs):
    nwide, nout = sum(runs), len(splits)
    wides, narrows = refs[:nwide], refs[nwide : nwide + nnarrow]
    chunked = outs_dtype == F32
    if chunked:
        held, outs = refs[-nout - 3 : -3], refs[-2 * nout - 3 : -nout - 3]
        wide_all, narrow_all, sems = refs[-3:]
        given = refs[nwide + nnarrow : -2 * nout - 3]
    else:
        given, outs = refs[nwide + nnarrow : -nout - 2], refs[-nout - 2 : -2]
        wide_all, narrow_all = refs[-2:]
    saves = []
    quarter = quarter_ref[0]
    at = 0
    for i, n in enumerate(runs):
        run = wides[at : at + n]
        at += n
        rows, dsh = run[0].shape[1:]
        here = pl.ds(i * rows, rows)
        if n == 1:
            half = run[0].shape[0] // 2
            for b in range(half):
                wide_all[here, pl.ds(b * dsh, dsh)] = run[0][quarter * half + b]
        for which, piece in enumerate(run if n > 1 else ()):

            @pl.when(quarter == which)
            def _(piece=piece):
                for b in range(piece.shape[0]):
                    wide_all[here, pl.ds(b * dsh, dsh)] = piece[b]

    rows = narrows[0].shape[0]
    for i, piece in enumerate(narrows):
        narrow_all[pl.ds(i * rows, rows), :] = piece[...]
    for c in range(outs[0].shape[0] // 256):
        cols = pl.ds(c * 256, 256)
        if wide_first:
            got = dot_tn(wide_all[:, cols], narrow_all[...])
        else:
            got = dot_tn(narrow_all[:, cols], wide_all[...])
        for more in given:
            got = got + more[cols, :].astype(F32)
        for i, (start, stop) in enumerate(splits):
            to = held[i] if chunked else outs[i]
            to[cols, :] = got[:, start:stop].astype(outs_dtype)
            if chunked:
                saves.append(
                    pltpu.make_async_copy(to.at[cols, :], outs[i].at[cols, :], sems.at[c, i])
                )
                saves[-1].start()
    for save in saves:
        save.wait()


def weight_grad(quarter, wide, narrow, wide_first, widths, dtype, given=()):
    rows, cols = narrow[0].shape
    dsh = wide[0][0].shape[2]
    width = sum(x.shape[0] for x in wide[0]) * dsh // 2
    height = width if wide_first else cols
    total = len(narrow) * rows
    flat = [x for run in wide for x in run]
    splits = [(sum(widths[:i]), sum(widths[: i + 1])) for i in range(len(widths))]
    runs = tuple(len(run) for run in wide)
    return pl.pallas_call(
        functools.partial(weight_grad_kernel, wide_first, runs, len(narrow), tuple(splits), dtype),
        out_shape=tuple(jax.ShapeDtypeStruct((height, w), dtype) for w in widths),
        in_specs=[in_smem()] + [in_vmem()] * (len(flat) + len(narrow) + len(given)),
        out_specs=tuple([anywhere() if dtype == F32 else in_vmem()] * len(widths)),
        scratch_shapes=(
            [pltpu.VMEM((height, w), F32) for w in widths] if dtype == F32 else []
        )
        + [pltpu.VMEM((total, width), BF16), pltpu.VMEM((total, cols), BF16)]
        + ([pltpu.SemaphoreType.DMA((height // 256, len(widths)))] if dtype == F32 else []),
        compiler_params=kernel_params(VMEM_LIMIT),
        cost_estimate=pl.CostEstimate(flops=1, bytes_accessed=1, transcendentals=0),
        name="weight_grad",
    )(quarter, *flat, *narrow, *given)


def passed_along(x, axis, by):
    peers = lax.axis_size(axis)
    pairs = [(i, i + by) for i in range(peers) if 0 <= i + by < peers]
    return lax.ppermute(x, axis, pairs)


def swapped(x, axis, mask):
    return lax.ppermute(x, axis, [(i, i ^ mask) for i in range(lax.axis_size(axis))])


def mirrored(x, mask):
    ndp, peers = lax.axis_size("dp"), lax.axis_size("tensor")
    to = lambda p, r: (p ^ mask) * peers + (r + peers // 2) % peers
    pairs = [(p * peers + r, to(p, r)) for p in range(ndp) for r in range(peers)]
    return lax.ppermute(x, ("dp", "tensor"), pairs)


def held_back(x):
    return lax.ppermute(x[:16, :128], "dp", [(i, i + 1) for i in range(0, lax.axis_size("dp"), 2)])


def exchange(blocks):
    return lax.all_to_all(blocks, "tensor", split_axis=0, concat_axis=0, tiled=True)


def gathered(cur):
    return exchange(jnp.broadcast_to(cur[None], (lax.axis_size("tensor"),) + cur.shape))


def by_section(masks, choices):
    out = choices[-1]
    for mask, choice in zip(masks, choices[:-1]):
        out = jnp.where(mask, choice, out)
    return out


def after(x, *marks):
    return lax.optimization_barrier((x,) + marks)[0]


def together(*xs):
    return lax.optimization_barrier(xs)


def on_device(embeds, source, lengths, bounds, targets, w_query, w_key, w_value, w_out, w_class):
    nst = lax.axis_size("section")
    peers = lax.axis_size("tensor")
    rep = lax.axis_index("dp")
    section_at = lax.axis_index("section")
    tensor_at = lax.axis_index("tensor")
    ntr, width, dsh = embeds.shape
    weights = (w_query[0], w_key[0], w_value[0], w_out[0])
    w_class = gathered(w_class).reshape(peers * w_class.shape[0], w_class.shape[1])

    hi, core = rep // 2, rep % 2
    slots = source.reshape(2, 2, ntr) - rep * ntr

    def mine_for(col):
        owner = lax.dynamic_slice_in_dim(slots, col, 1, axis=1)[:, 0]
        out = jnp.zeros((2, ntr, width, dsh), BF16)
        for n in range(ntr):
            out = jnp.where((owner == n)[:, :, None, None], embeds[n][None, None], out)
        return out

    both = mine_for(core) + swapped(mine_for(1 - core), "dp", 1)
    own = lax.dynamic_slice_in_dim(both, hi, 1, axis=0)[0]
    away = lax.dynamic_slice_in_dim(both, 1 - hi, 1, axis=0)[0]
    taken_here = own + swapped(away, "dp", 2)
    source, lengths, bounds, targets, taken_here = together(
        source, lengths, bounds, targets, taken_here
    )
    wanted = lax.dynamic_slice_in_dim(source, rep * ntr, ntr)
    lens = lengths[wanted]
    bnd = bounds[wanted]
    tgt = targets[wanted]
    nstep = bnd.shape[1]
    factor = (LOSS_SCALE / jnp.sum(lens).astype(F32)).reshape(1)

    def one_hot(ids, size):
        hot = ids[:, None] == jnp.arange(size, dtype=jnp.int32)[None, :]
        return jnp.concatenate([hot, jnp.zeros((16 - nstep, size), bool)], axis=0)

    picks = [one_hot(bnd[j], width).astype(BF16) for j in range(ntr)]
    hots = [one_hot(tgt[j], w_class.shape[1]).astype(F32) for j in range(ntr)]
    spans = [jnp.where(section_at == n, lens[0], lens[1]).reshape(1) for n in range(nst + 1)]
    flags = [(section_at == s).astype(jnp.int32).reshape(1) for s in range(nst)]
    masks = [section_at == s for s in range(nst)]
    half = peers // 2
    mine_at = (hi * half).astype(jnp.uint32)
    away_at = [((1 - hi) * half + n * half // 2).astype(jnp.uint32) for n in range(2)]
    block_at = tensor_at.astype(jnp.uint32)
    ours = core.astype(jnp.int32).reshape(1)
    theirs = 1 - ours

    def sum_of(got):
        return jnp.sum(got[:, :width].astype(F32), axis=0)

    kept = []
    arriving = None
    for turn in range(nst):
        cur = taken_here[turn] if turn < ntr else jnp.zeros((width, dsh), BF16)
        if turn == 0:
            cur, factor, picks, hots, spans, flags, masks, mine_at, away_at, block_at, ours, theirs, w_class = together(
                cur, factor, picks, hots, spans, flags, masks, mine_at, away_at, block_at, ours, theirs, w_class
            )
        if arriving is not None:
            cur, arriving = together(cur, arriving)
            cur = jnp.where(masks[0], cur, arriving)
        x = gathered(cur)
        if turn == nst - 1:
            now = forward(spans[turn], x, weights, "both", picks[0], nstep)
        else:
            now = forward(spans[turn], x, weights)
        kept.append(now)
        blocks = now["part"]
        got = exchange(blocks)
        arriving = (cur.astype(F32) + sum_of(got)).astype(BF16)
        leaving = arriving
        arriving = passed_along(arriving, "section", 1)

    def end_cotangent(which, got, x):
        return step_end_grad(factor, got, x, picks[which], w_class, hots[which], nstep)

    def own_block(blocks):
        return lax.dynamic_slice_in_dim(blocks, block_at, 1, axis=0)[0]

    def chosen(choices, at=None, count=None):
        if at is None:
            return by_section(masks, choices)
        return by_section(
            masks, [lax.dynamic_slice_in_dim(x, at, count, axis=0) for x in choices]
        )

    def not_before(choices, mark):
        return [after(x, mark) for x in choices]

    seen = lambda name, which: [kept[s + which][name] for s in range(nst)]
    back = lambda n, which: [taken[2 * nst - 1 - s + which][n] for s in range(nst)]

    pieces = {}

    def send_blocks(name, choices, n):
        pieces[f"{name}.{n}"] = mirrored(chosen(choices, away_at[n], half // 2), 2)

    def send_half(name, choices):
        pieces[name] = mirrored(chosen(choices, away_at[0], half), 2)

    def send_whole(name, choices):
        pieces[name] = swapped(chosen(choices), "dp", 2)

    taken = {}
    g_top = end_cotangent(0, got, x)
    grad = own_block(g_top)
    send_blocks("h0", not_before(seen("h", 0), leaving), 0)
    send_whole("o0", not_before(seen("o", 0), leaving))
    arriving, g_top, grad, pieces = together(arriving, g_top, grad, pieces)
    x = gathered(arriving)
    now = forward(spans[nst], x, weights, "ends", picks[1], nstep)
    d, dx = backward(
        jnp.zeros((1,), jnp.int32), g_top, kept[-1], kept[-1], weights, True, (now["part"],)
    )
    taken[nst] = (d, g_top)
    kept.append(now)
    got = exchange(dx)

    for turn in range(nst + 1, 2 * nst + 1):
        grad = (grad.astype(F32) + sum_of(got)).astype(BF16)
        leaving = grad
        if turn == nst + 1:
            g_top = end_cotangent(1, got, x)
            send_blocks("h0", not_before(seen("h", 0), grad), 1)
            send_whole("o1", not_before(seen("o", 1), grad))
        elif turn < 2 * nst:
            n = turn - nst - 2
            send_blocks("h1", not_before(seen("h", 1), grad), n)
        else:
            send_half("g0", not_before(back(1, 0), grad))
            send_whole("d0", not_before(back(0, 0), grad))
        held = [held_back(leaving)] if turn == nst + 1 else []
        grad, pieces, held = together(passed_along(grad, "section", -1), pieces, held)
        if turn == nst + 1:
            grad = jnp.where(masks[nst - 1], own_block(g_top), grad)
        g = gathered(grad)
        late = 2 * nst + 1 - turn
        early = max(late - 2, 0)
        flag = flags[late - 1]
        if turn < 2 * nst:
            d, dx = backward(flag, g, kept[early], kept[late], weights, True, (), held)
            taken[turn] = (d, g)
            got = exchange(dx)
        else:
            taken[turn] = (None, g)
            send_half("g1", back(1, 1))
            (d,) = backward(flag, g, kept[early], kept[late], weights, False)
            taken[turn] = (d, g)
            send_whole("d1", back(0, 1))

    def wide(name, choices):
        runs = []
        for w in range(ntr):
            runs.append((chosen(not_before(choices(w), g), mine_at, half),))
            names = (f"{name}{w}",) if name == "g" else (f"{name}{w}.0", f"{name}{w}.1")
            runs.append(tuple(pieces[n] for n in names))
        return runs

    def narrow(name, choices):
        out = []
        for w in range(ntr):
            out += [chosen(not_before(choices(w), g)), pieces[f"{name}{w}"]]
        return out

    qcol = weights[0].shape[1]
    all_o = (wide("g", lambda w: back(1, w)), narrow("o", lambda w: seen("o", w)), False)
    all_d = (wide("h", lambda w: seen("h", w)), narrow("d", lambda w: back(0, w)), True)
    cols_o, cols_d = (half // 2 * dsh,), (qcol, HEAD_DIM, HEAD_DIM)
    (give_o,) = weight_grad(theirs, *all_o, cols_o, BF16)
    given_o = swapped(give_o, "dp", 1)
    (give_d,) = weight_grad(theirs, *all_d, (sum(cols_d),), BF16)
    given_d = swapped(give_d, "dp", 1)
    (grad_o,) = weight_grad(ours, *all_o, cols_o, F32, (given_o,))
    grad_q, grad_k, grad_v = weight_grad(ours, *all_d, cols_d, F32, (given_d,))
    return (grad_q[None], grad_k[None], grad_v[None], grad_o[None])


def solution(mesh):
    placed = (
        P("dp", None, "tensor"),
        P(),
        P(),
        P(),
        P(),
        P("section", None, "tensor"),
        P("section", None, "tensor"),
        P("section", None, "tensor"),
        P("section", "tensor", None),
        P("tensor", None),
    )
    return jax.shard_map(
        on_device,
        mesh=mesh,
        in_specs=placed,
        out_specs=(
            P("section", "dp", "tensor"),
            P("section", "dp", "tensor"),
            P("section", "dp", "tensor"),
            P("section", "tensor", "dp"),
        ),
        check_vma=False,
    )
```
